32 devices in a mesh: head: 4 (over x, core), blk: 8 (over z, y).
Axes of the slice: x: 2, y: 2, z: 4, core: 2. Of those that a mesh axis runs over, the one named last changes fastest.
Arguments:
- inputs: bfloat16 [2, 8, 256, 2048], P(None, 'blk', 'head'), may hold values from -6 to 6
- norm_gain: bfloat16 [2048], P(('head', 'blk')), may hold values from 0.099609375 to 1.8984375
- norm_bias: bfloat16 [2048], P(('head', 'blk')), may hold values from -4 to 4
- triple_weight: bfloat16 [2048, 6144], P(('head', 'blk')), may hold values from -0.125 to 0.125
- triple_bias: bfloat16 [6144], P(('head', 'blk')), may hold values from -6 to 6
- dense_weight: bfloat16 [2048, 2048], P(('head', 'blk')), may hold values from -1 to 1
- dense_bias: bfloat16 [2048], P(('head', 'blk')), may hold values from -4 to 4
- expand_weight: bfloat16 [2048, 8192], P(('head', 'blk')), may hold values from -0.125 to 0.125
- expand_bias: bfloat16 [8192], P(('head', 'blk')), may hold values from -6 to 6
- shrink_weight: bfloat16 [2048, 8192], P(('head', 'blk')), may hold values from -0.09375 to 0.09375
- shrink_bias: bfloat16 [2048], P(('head', 'blk')), may hold values from -4 to 4
- lengths: int32 [2], replicated, may hold values from 256 to 2048, as said below
- block_order: int32 [8], replicated, may hold values from 0 to 7, each once
- cotangent: bfloat16 [2, 8, 256, 2048], P(None, 'blk', 'head'), may hold values from -6 to 6
Outputs:
- output: bfloat16 [2, 8, 256, 2048], P(None, 'blk', 'head')
- grad_inputs: bfloat16 [2, 8, 256, 2048], P(None, 'blk', 'head')
- grad_norm_gain: float32 [2048], P(('head', 'blk'))
- grad_norm_bias: float32 [2048], P(('head', 'blk'))
- grad_triple_weight: float32 [2048, 6144], P(('head', 'blk'))
- grad_triple_bias: float32 [6144], P(('head', 'blk'))
- grad_dense_weight: float32 [2048, 2048], P(('head', 'blk'))
- grad_dense_bias: float32 [2048], P(('head', 'blk'))
- grad_expand_weight: float32 [2048, 8192], P(('head', 'blk'))
- grad_expand_bias: float32 [8192], P(('head', 'blk'))
- grad_shrink_weight: float32 [2048, 8192], P(('head', 'blk'))
- grad_shrink_bias: float32 [2048], P(('head', 'blk'))
The draws below stay inside these ranges and needn't reach their ends.
Inputs may be any that keep to these rules, and one draw needn't show every extreme that they name: `lengths`: some micro-batch has all 2048 slots valid. `block_order`: each block index appears once.
All inputs are finite; a program needn't handle non-finite values.
Results may differ from the reference program's by a relative error of at most 0.013.
Values may be sent and summed in bfloat16 or wider, within the bound.
No kernel may reach another device: no remote copies, remote signals or barrier semaphores. Data moves between devices by JAX's collectives and lax.ppermute only.
A program may use at most 704 MiB of HBM per device.

```python
import jax
import jax.numpy as jnp
from jax import lax

D = 2048
FF = 8192
HEADS = 32
HEAD_DIM = 64
ROT = 32
MB = 2
LOC = 256
SEQ = 2048
N_BLK = 8


def draw_lengths(key, part):
    key = jax.random.fold_in(key, 11)
    full_key, rest_key = jax.random.split(key)
    chosen = jax.random.randint(full_key, (), 0, MB)
    drawn = jax.random.randint(rest_key, (MB,), LOC, SEQ + 1)
    return jnp.where(jnp.arange(MB) == chosen, SEQ, drawn).astype(jnp.int32)


def shard_levels(rng, dims, shards, smallest, top_value):
    def one(dim, shards_of):
        draws = jax.random.uniform(jax.random.fold_in(jax.random.fold_in(rng, 6), dim), (shards_of,), jnp.float32, smallest / len(shards), top_value / len(shards))
        return jnp.repeat(jnp.exp(draws), dims[dim] // shards_of).reshape((-1,) + (1,) * (len(dims) - dim - 1))

    loudness = one(*shards[0])
    for cut in shards[1:]:
        loudness = loudness * one(*cut)
    return loudness


def noise(key, shape, scale, reach, cuts=(), held_as=jnp.bfloat16):
    values = scale * jax.random.normal(key, shape, jnp.float32)
    if cuts:
        values = values * shard_levels(key, shape, cuts, -0.22, 0.18)
    return jnp.clip(values, -reach, reach).astype(held_as)


def setup_inputs(seed: int = 0) -> dict:
    keys = jax.random.split(jax.random.key(seed), 15)
    return {
        "inputs": noise(keys[0], (MB, N_BLK, LOC, D), 1.0, 6.0, ((1, 8), (2, 4))),
        "norm_gain": jnp.clip(1.0 + 0.18 * jax.random.normal(keys[1], (D,), jnp.float32), 0.099609375, 1.8984375).astype(jnp.bfloat16),
        "norm_bias": noise(keys[2], (D,), 0.3, 4.0, ((0, 32),)),
        "triple_weight": noise(keys[3], (D, 3 * D), D ** -0.5, 0.125, ((0, 32),)),
        "triple_bias": noise(keys[4], (3 * D,), 0.5, 6.0, ((0, 32),)),
        "dense_weight": noise(keys[5], (D, D), (D // 64) ** -0.5, 1.0, ((0, 32),)),
        "dense_bias": noise(keys[6], (D,), 0.3, 4.0, ((0, 32),)),
        "expand_weight": noise(keys[7], (D, FF), D ** -0.5, 0.125, ((0, 32),)),
        "expand_bias": noise(keys[8], (FF,), 0.5, 6.0, ((0, 32),)),
        "shrink_weight": noise(keys[9], (D, FF), (FF // 2) ** -0.5, 0.09375, ((0, 32),)),
        "shrink_bias": noise(keys[10], (D,), 0.3, 4.0, ((0, 32),)),
        "lengths": draw_lengths(jax.random.fold_in(keys[14], 71), 0),
        "block_order": jax.random.permutation(keys[12], N_BLK).astype(jnp.int32),
        "cotangent": noise(keys[13], (MB, N_BLK, LOC, D), 1.0, 6.0, ((1, 8), (2, 4))),
    }


@jax.custom_vjp
def low(v):
    return lax.optimization_barrier(v.astype(jnp.bfloat16)).astype(jnp.float32)

@jax.custom_vjp
def low_back(v):
    return v

def low_keep(v):
    return (low(v), None)

def low_pass(kept, grad):
    return (grad,)

def back_keep(v):
    return (v, None)

def back_low(kept, grad):
    return (low(grad),)
low.defvjp(low_keep, low_pass)
low_back.defvjp(back_keep, back_low)

def matmul(left, right):
    return jnp.dot(left, right, precision=lax.Precision.HIGHEST)

def layer_norm(values, gain, shift):
    centred = values - lax.optimization_barrier(jnp.mean(values, -1, keepdims=True))
    variance = lax.optimization_barrier(jnp.mean(centred * centred, -1, keepdims=True))
    return centred * lax.rsqrt(variance + 1e-05) * gain + shift

def rotary_tables(positions):
    half = ROT // 2
    inverse = 10000.0 ** (-(jnp.arange(half, dtype=jnp.float32) * 2.0) / ROT)
    angles = positions.astype(jnp.float32)[:, None] * inverse[None, :]
    return (jnp.cos(angles), jnp.sin(angles))

def rotate(pair, cosine, sine):
    half = ROT // 2
    first = pair[..., :half]
    second = pair[..., half:ROT]
    return jnp.concatenate([first * cosine - second * sine, second * cosine + first * sine, pair[..., ROT:]], -1)

def attend_block(queries, query_pos, key_rows, value_rows, key_pos, length):
    scores = low_back(jnp.einsum('qhd,khd->hqk', queries, key_rows, precision=lax.Precision.HIGHEST) * HEAD_DIM ** (-0.5))
    allowed = ((key_pos[None, :] <= query_pos[:, None]) & (key_pos[None, :] < length))[None]
    masked = jnp.where(allowed, scores, -1e+30)
    largest = lax.optimization_barrier(jnp.max(masked, -1, keepdims=True))
    weights = jnp.where(allowed, jnp.exp(masked - largest), 0.0)
    summed = lax.optimization_barrier(jnp.sum(weights, -1))
    mixed = jnp.einsum('hqk,khd->qhd', low(weights), value_rows, precision=lax.Precision.HIGHEST)
    return mixed / jnp.transpose(summed)[:, :, None]

def layer(source, gain, shift, triple_w, triple_b, dense_w, dense_b, expand_w, expand_b, shrink_w, shrink_b, lengths, block_order):
    positions = (block_order[:, None] * LOC + jnp.arange(LOC, dtype=jnp.int32)[None, :]).reshape(SEQ)
    valid = (positions[None, :] < lengths[:, None]).astype(source.dtype).reshape(MB * SEQ, 1)
    flat = source.reshape(MB * SEQ, D)
    normed = low(layer_norm(flat, gain, shift))
    linear = low_back(matmul(normed, triple_w) + triple_b).reshape(MB * SEQ, 3, HEADS, HEAD_DIM)
    cosine, sine = rotary_tables(positions)
    cosine = jnp.tile(cosine, (MB, 1))[:, None, None, :]
    sine = jnp.tile(sine, (MB, 1))[:, None, None, :]
    turned = jnp.concatenate([rotate(linear[:, :2], cosine, sine), linear[:, 2:]], 1)
    rotated = low_back(low(turned)).reshape(MB, SEQ, 3, HEADS, HEAD_DIM)
    query_block = 512 if SEQ % 512 == 0 else SEQ
    pieces = []
    for batch in range(MB):

        def one_block(pair, key_rows=rotated[batch, :, 1], value_rows=rotated[batch, :, 2], length=lengths[batch]):
            return attend_block(pair[0], pair[1], key_rows, value_rows, positions, length)
        attended = lax.map(jax.checkpoint(one_block), (rotated[batch, :, 0].reshape(SEQ // query_block, query_block, HEADS, HEAD_DIM), positions.reshape(SEQ // query_block, query_block)))
        pieces.append(attended.reshape(SEQ, D))
    attention = low_back(low(jnp.concatenate(pieces, 0)))
    dense_out = matmul(attention, dense_w) + dense_b
    expand_pre = low_back(matmul(normed, expand_w) + expand_b)
    expand_out = low(jax.nn.gelu(expand_pre, approximate=True))
    shrink_out = matmul(expand_out, jnp.transpose(shrink_w)) + shrink_b
    return (valid * (flat + dense_out + shrink_out)).reshape(MB, N_BLK, LOC, D)

def reference(inputs, norm_gain, norm_bias, triple_weight, triple_bias, dense_weight, dense_bias, expand_weight, expand_bias, shrink_weight, shrink_bias, lengths, block_order, cotangent):
    floats = (inputs.astype(jnp.float32), norm_gain.astype(jnp.float32), norm_bias.astype(jnp.float32), triple_weight.astype(jnp.float32), triple_bias.astype(jnp.float32), dense_weight.astype(jnp.float32), dense_bias.astype(jnp.float32), expand_weight.astype(jnp.float32), expand_bias.astype(jnp.float32), shrink_weight.astype(jnp.float32), shrink_bias.astype(jnp.float32))

    def forward(source, gain, shift, triple_w, triple_b, dense_w, dense_b, expand_w, expand_b, shrink_w, shrink_b):
        return layer(source, gain, shift, triple_w, triple_b, dense_w, dense_b, expand_w, expand_b, shrink_w, shrink_b, lengths, block_order)
    result, pullback = jax.vjp(forward, floats[0], floats[1], floats[2], floats[3], floats[4], floats[5], floats[6], floats[7], floats[8], floats[9], floats[10])
    grads = pullback(cotangent.astype(jnp.float32))
    return (result.astype(jnp.bfloat16), grads[0].astype(jnp.bfloat16), grads[1], grads[2], grads[3], grads[4], grads[5], grads[6], grads[7], grads[8], grads[9], grads[10])
```

```python
import functools

import jax
import jax.numpy as jnp
from jax import lax
from jax.experimental import pallas as pl
from jax.experimental.pallas import tpu as pltpu
from jax.sharding import Mesh
from jax.sharding import PartitionSpec as P

HEADS = 32
HEAD_DIM = 64
ROT = 32
EPS = 1e-05
NEG = -1e30
BF = jnp.bfloat16
F32 = jnp.float32

RANK = ("hx", "bz", "by")
ALL = ("hx", "core", "bs", "bz", "by")
Z_LEN = 4
SWAP = [(0, 1), (1, 0)]
UP = [(i, (i + 1) % Z_LEN) for i in range(Z_LEN)]
DOWN = [((i + 1) % Z_LEN, i) for i in range(Z_LEN)]
VMEM_LIMIT = 50 * 1024 * 1024


def swap(value, axis):
    return lax.ppermute(value, axis, SWAP)


def dot_rows(left, right):
    return lax.dot_general(left, right, (((1,), (1,)), ((), ())), preferred_element_type=F32)


def dot_cols(left, right):
    return lax.dot_general(left, right, (((0,), (0,)), ((), ())), preferred_element_type=F32)


def dot(left, right):
    return jnp.dot(left, right, preferred_element_type=F32)


def gather_pieces(own, other):
    first, second = [own], [other]
    both = jnp.stack([own, other])
    for _ in range(Z_LEN - 1):
        both = lax.ppermute(both, "bz", UP)
        first.append(both[0])
        second.append(both[1])
    rows = []
    for a, b in zip(first, second):
        a_y = swap(a, "by")
        b_x = swap(b, "hx")
        a_pair = jnp.stack([a, a_y])
        b_pair = jnp.stack([b, b_x])
        a_far = swap(a_pair, "hx")
        b_far = swap(b_pair, "by")
        rows += [a, b, a_far[0], b_x, a_y, b_far[0], a_far[1], b_far[1]]
    return jnp.concatenate(rows, 0)


def add_low(left, right):
    return (left.astype(F32) + right.astype(F32)).astype(BF)


def scatter_sum(parts, share, width):
    parts = parts.reshape(Z_LEN, 2, 2, 2, share, width)
    carried = None
    for kz in range(Z_LEN - 1, -1, -1):
        a = parts[kz, :, :, 0]
        b = parts[kz, :, :, 1]
        a_half = add_low(a[:, 0], swap(a[:, 1], "hx"))
        b_half = add_low(b[0], swap(b[1], "by"))
        a_sum = a_half[0].astype(F32) + swap(a_half[1], "by").astype(F32)
        b_sum = b_half[0].astype(F32) + swap(b_half[1], "hx").astype(F32)
        total = jnp.stack([a_sum, b_sum])
        if carried is not None:
            total = total + lax.ppermute(carried, "bz", DOWN).astype(F32)
        carried = total.astype(BF)
    return total


def turn(value, cosine, sine, lane):
    near = jnp.where(
        (lane % HEAD_DIM) < ROT // 2,
        pltpu.roll(value, 128 - ROT // 2, 1),
        pltpu.roll(value, ROT // 2, 1),
    )
    return value * cosine + near * sine


def front_kernel(x_ref, gain_ref, shift_ref, w_ref, bias_ref, cos_ref, sin_ref, h_ref, q_ref, kv_ref, pre_ref, out_ref):
    x = x_ref[...].astype(F32)
    centred = x - jnp.mean(x, -1, keepdims=True)
    variance = jnp.mean(centred * centred, -1, keepdims=True)
    h = (centred * lax.rsqrt(variance + EPS) * gain_ref[...] + shift_ref[...]).astype(BF)
    h_ref[...] = h
    linear = dot(h, w_ref[...]) + bias_ref[...]
    lane = lax.broadcasted_iota(jnp.int32, (x.shape[0], 128), 1)
    cosine, sine = cos_ref[...], sin_ref[...]
    q_ref[...] = turn(linear[:, :128], cosine, sine, lane).astype(BF) * BF(HEAD_DIM**-0.5)
    kv_ref[:, :128] = turn(linear[:, 128:256], cosine, sine, lane).astype(BF)
    kv_ref[:, 128:] = linear[:, 256:384].astype(BF)
    pre = linear[:, 384:]
    pre_ref[...] = pre
    out_ref[...] = (0.5 * pre * (1.0 + jnp.tanh(0.7978845608 * (pre + 0.044715 * pre * pre * pre)))).astype(BF)


def front(x, gain, shift, weight, bias, cosine, sine, block):
    rows, width = x.shape
    cols = weight.shape[1]
    wide = cols - 384
    by_row = lambda n: pl.BlockSpec((block, n), lambda i: (i, 0))
    whole = lambda r, n: pl.BlockSpec((r, n), lambda i: (0, 0))
    return pl.pallas_call(
        front_kernel,
        grid=(rows // block,),
        in_specs=[by_row(width), whole(1, width), whole(1, width), whole(width, cols), whole(1, cols), by_row(128), by_row(128)],
        out_specs=[by_row(width), by_row(128), by_row(256), by_row(wide), by_row(wide)],
        out_shape=[
            jax.ShapeDtypeStruct((rows, width), BF),
            jax.ShapeDtypeStruct((rows, 128), BF),
            jax.ShapeDtypeStruct((rows, 256), BF),
            jax.ShapeDtypeStruct((rows, wide), F32),
            jax.ShapeDtypeStruct((rows, wide), BF),
        ],
        compiler_params=pltpu.CompilerParams(vmem_limit_bytes=VMEM_LIMIT),
        cost_estimate=pl.CostEstimate(
            flops=2 * rows * width * cols + 12 * rows * width, bytes_accessed=rows * width * 6, transcendentals=rows * wide
        ),
    )(x, gain, shift, weight, bias, cosine, sine)


def two_heads(value):
    lane = lax.broadcasted_iota(jnp.int32, value.shape, 1)
    zero = jnp.zeros_like(value)
    return jnp.concatenate([jnp.where(lane < HEAD_DIM, value, zero), jnp.where(lane < HEAD_DIM, zero, value)], 0)


def one_row(value):
    half = value.shape[0] // 2
    lane = lax.broadcasted_iota(jnp.int32, (half, 128), 1)
    return jnp.where(lane < HEAD_DIM, value[:half], value[half:])


def allowed_pairs(table_ref, block, query_at, key_at):
    turned, length = table_ref[0], table_ref[1]
    shape = (2 * block, block)
    query = query_at * block + ((lax.broadcasted_iota(jnp.int32, shape, 0) & (block - 1)) ^ turned)
    key = key_at * block + (lax.broadcasted_iota(jnp.int32, shape, 1) ^ turned)
    return (key <= query) & (key < length)


def key_ranges(table_ref, block, query_at):
    length = table_ref[1]
    plain = jnp.minimum(query_at, length // block)
    last = jnp.minimum(query_at + 1, (length + block - 1) // block)
    return plain, last


def attend_kernel(blocks, block, table_ref, q_ref, kv_ref, full_ref, low_ref, lse_ref):
    query_at = table_ref[2 + pl.program_id(0)]
    queries = two_heads(q_ref[...])

    def step(masked, at, state):
        top, total, mixed = state
        begin = pl.multiple_of(table_ref[2 + blocks + at] * block, block)
        keys = kv_ref[pl.ds(begin, block), :128]
        values = kv_ref[pl.ds(begin, block), 128:]
        scores = dot_rows(queries, keys)
        if masked:
            allowed = allowed_pairs(table_ref, block, query_at, at)
            scores = jnp.where(allowed, scores, NEG)
        fresh = jnp.maximum(top, jnp.max(scores, -1, keepdims=True))
        factor = jnp.exp(top - fresh)
        weights = jnp.exp(scores - fresh)
        if masked:
            weights = jnp.where(allowed, weights, 0.0)
        total = total * factor + jnp.sum(weights, -1, keepdims=True)
        return fresh, total, mixed * factor + dot(weights.astype(BF), values)

    state = (
        jnp.full((2 * block, 1), NEG, F32),
        jnp.zeros((2 * block, 1), F32),
        jnp.zeros((2 * block, 128), F32),
    )
    plain, last = key_ranges(table_ref, block, query_at)
    state = lax.fori_loop(0, plain, functools.partial(step, False), state)
    top, total, mixed = lax.fori_loop(plain, last, functools.partial(step, True), state)
    full = one_row(mixed / total)
    full_ref[...] = full
    low_ref[...] = full.astype(BF)
    lse_ref[...] = jnp.broadcast_to(top + jnp.log(total), lse_ref.shape)


def attend(table, q, kv, block):
    rows = q.shape[0]
    keys = kv.shape[0]
    blocks = rows // block
    by_row = lambda r, n: pl.BlockSpec((r, n), lambda i, t: (i, 0))
    whole = lambda r, n: pl.BlockSpec((r, n), lambda i, t: (0, 0))
    return pl.pallas_call(
        functools.partial(attend_kernel, blocks, block),
        grid_spec=pltpu.PrefetchScalarGridSpec(
            num_scalar_prefetch=1,
            grid=(blocks,),
            in_specs=[by_row(block, 128), whole(keys, 256)],
            out_specs=[by_row(block, 128), by_row(block, 128), by_row(2 * block, 128)],
        ),
        out_shape=[
            jax.ShapeDtypeStruct((rows, 128), F32),
            jax.ShapeDtypeStruct((rows, 128), BF),
            jax.ShapeDtypeStruct((2 * rows, 128), F32),
        ],
        compiler_params=pltpu.CompilerParams(vmem_limit_bytes=VMEM_LIMIT),
        cost_estimate=pl.CostEstimate(
            flops=16 * rows * keys * 128, bytes_accessed=rows * 128 * 16, transcendentals=rows * keys
        ),
    )(table, q, kv)


def attend_back_kernel(blocks, block, table_ref, q_ref, kv_ref, full_ref, lse_ref, grad_ref, dq_ref, dkv_ref, dk_acc, dv_acc):
    at_block = pl.program_id(0)
    query_at = table_ref[2 + at_block]
    queries = two_heads(q_ref[...])
    grads = two_heads(grad_ref[...])
    full = full_ref[...]
    delta = jnp.sum(grads.astype(F32) * jnp.concatenate([full, full], 0), -1, keepdims=True)
    lse = lse_ref[:, :1]

    @pl.when(at_block == 0)
    def _():
        dk_acc[...] = jnp.zeros_like(dk_acc)
        dv_acc[...] = jnp.zeros_like(dv_acc)

    def step(masked, at, grad_query):
        begin = pl.multiple_of(table_ref[2 + blocks + at] * block, block)
        rows = pl.ds(begin, block)
        keys = kv_ref[rows, :128]
        values = kv_ref[rows, 128:]
        scores = dot_rows(queries, keys)
        if masked:
            allowed = allowed_pairs(table_ref, block, query_at, at)
            scores = jnp.where(allowed, scores, NEG)
        weights = jnp.exp(scores - lse)
        if masked:
            weights = jnp.where(allowed, weights, 0.0)
        grad_scores = (weights * (dot_rows(grads, values) - delta)).astype(BF)
        dk_acc[rows, :] += dot_cols(grad_scores, queries)
        dv_acc[rows, :] += dot_cols(weights.astype(BF), grads)
        return grad_query + dot(grad_scores, keys)

    plain, last = key_ranges(table_ref, block, query_at)
    grad_query = jnp.zeros((2 * block, 128), F32)
    grad_query = lax.fori_loop(0, plain, functools.partial(step, False), grad_query)
    grad_query = lax.fori_loop(plain, last, functools.partial(step, True), grad_query)
    dq_ref[...] = (one_row(grad_query) * HEAD_DIM**-0.5).astype(BF)

    @pl.when(at_block == blocks - 1)
    def _():
        dkv_ref[:, :128] = dk_acc[...].astype(BF)
        dkv_ref[:, 128:] = dv_acc[...].astype(BF)


def attend_back(table, q, kv, full, lse, grad, block):
    rows = q.shape[0]
    keys = kv.shape[0]
    blocks = rows // block
    by_row = lambda r, n: pl.BlockSpec((r, n), lambda i, t: (i, 0))
    whole = lambda r, n: pl.BlockSpec((r, n), lambda i, t: (0, 0))
    return pl.pallas_call(
        functools.partial(attend_back_kernel, blocks, block),
        grid_spec=pltpu.PrefetchScalarGridSpec(
            num_scalar_prefetch=1,
            grid=(blocks,),
            in_specs=[by_row(block, 128), whole(keys, 256), by_row(block, 128), by_row(2 * block, 128), by_row(block, 128)],
            out_specs=[by_row(block, 128), whole(keys, 256)],
            scratch_shapes=[pltpu.VMEM((keys, 128), F32), pltpu.VMEM((keys, 128), F32)],
        ),
        out_shape=[jax.ShapeDtypeStruct((rows, 128), BF), jax.ShapeDtypeStruct((keys, 256), BF)],
        compiler_params=pltpu.CompilerParams(vmem_limit_bytes=VMEM_LIMIT),
        cost_estimate=pl.CostEstimate(
            flops=40 * rows * keys * 128, bytes_accessed=rows * 128 * 24, transcendentals=rows * keys
        ),
    )(table, q, kv, full, lse, grad)


def turn_tables(positions):
    half = ROT // 2
    inverse = 10000.0 ** (-(jnp.arange(half, dtype=F32) * 2.0) / ROT)
    angles = positions.astype(F32)[:, None] * inverse[None, :]
    cosine, sine = jnp.cos(angles), jnp.sin(angles)
    rest = (positions.shape[0], HEAD_DIM - ROT)
    cosine = jnp.concatenate([cosine, cosine, jnp.ones(rest, F32)], 1)
    sine = jnp.concatenate([-sine, sine, jnp.zeros(rest, F32)], 1)
    return jnp.tile(cosine, (1, 2)), jnp.tile(sine, (1, 2))


def near_columns():
    lane = jnp.arange(256, dtype=jnp.int32)
    within = lane % HEAD_DIM
    source = jnp.where(within < ROT // 2, lane + ROT // 2, jnp.where(within < ROT, lane - ROT // 2, lane))
    return (lane[:, None] == source[None, :]).astype(BF)


def core_pair(own, other, core):
    return jnp.where(core == 0, jnp.stack([own, other], 1), jnp.stack([other, own], 1))


def body(
    inputs,
    norm_gain,
    norm_bias,
    triple_weight,
    triple_bias,
    dense_weight,
    dense_bias,
    expand_weight,
    expand_bias,
    shrink_weight,
    shrink_bias,
    lengths,
    block_order,
    cotangent,
):
    share, width = inputs.shape[2], inputs.shape[3]
    hx, core, bs, bz, by = (lax.axis_index(name) for name in ALL)
    spread = lax.axis_size("bs")
    ranks = 2 * Z_LEN * 2
    devices = 2 * ranks * spread
    block = 4 * share
    rows = ranks * 2 * share
    near_blocks = Z_LEN * 2
    blocks = block_order.shape[0]
    held = width // devices
    ff = expand_weight.shape[1]
    ff_here = ff // ranks
    length = lengths[core]

    def block_at(index):
        return jnp.sum(jnp.where(jnp.arange(blocks, dtype=jnp.int32) == index, block_order, 0))

    token_pos = (
        block_at(bs * near_blocks + bz * 2 + by) * block
        + (hx * 2 + core) * share
        + jnp.arange(share, dtype=jnp.int32)
    )
    valid = (token_pos[None, :] < lengths[:, None]).astype(F32)[:, :, None]

    def near_at(group):
        return jnp.stack(
            [
                block_at(group * near_blocks + ((bz + Z_LEN - kz) % Z_LEN) * 2 + (by + ky) % 2)
                for kz in range(Z_LEN)
                for ky in range(2)
            ]
        )

    query_at = near_at(bs)
    turned = hx * 2 * share + core * share
    row_pos = (query_at[:, None] * block + (jnp.arange(block, dtype=jnp.int32) ^ turned)[None, :]).reshape(rows)
    key_at = jnp.concatenate([near_at(group) for group in range(spread)])
    spots = jnp.arange(blocks, dtype=jnp.int32)
    order = jnp.sum(jnp.where(key_at[None, :] == spots[:, None], spots[None, :], 0), 1)
    table = jnp.concatenate([jnp.stack([turned, length]), query_at, order]).astype(jnp.int32)
    cosine, sine = turn_tables(row_pos)

    x_mine = jnp.where(core == 0, inputs[0, 0], inputs[1, 0])
    x_away = jnp.where(core == 0, inputs[1, 0], inputs[0, 0])
    x_all = gather_pieces(x_mine, swap(x_away, "core"))

    small = jnp.concatenate([norm_gain, norm_bias, triple_bias, expand_bias, dense_bias, shrink_bias])
    cuts = [0]
    for leaf in (norm_gain, norm_bias, triple_bias, expand_bias, dense_bias, shrink_bias):
        cuts.append(cuts[-1] + leaf.shape[0])
    small = lax.all_gather(small, ALL, axis=0, tiled=False).reshape(devices, cuts[-1])
    gain, shift, triple_b, expand_b, dense_b, shrink_b = (
        small[:, low:high].reshape(-1).astype(F32) for low, high in zip(cuts[:-1], cuts[1:])
    )
    rank = hx * near_blocks + bz * 2 + by
    bias_triple = lax.dynamic_index_in_dim(
        triple_b.reshape(3, 2, 2, near_blocks, HEAD_DIM).transpose(1, 3, 0, 2, 4).reshape(ranks, 384), rank, 0
    )
    bias_expand = lax.dynamic_index_in_dim(expand_b.reshape(ranks, ff_here), rank, 0)
    bias_in = jnp.concatenate([bias_triple, bias_expand], 1)
    sent = jnp.concatenate(
        [
            triple_weight.reshape(held, 3, 2, 2, near_blocks, HEAD_DIM).transpose(2, 4, 0, 1, 3, 5).reshape(ranks, held, 384),
            expand_weight.reshape(held, ranks, ff_here).transpose(1, 0, 2),
            shrink_weight.reshape(held, ranks, ff_here).transpose(1, 0, 2),
        ],
        2,
    )
    got = lax.all_to_all(sent, RANK, split_axis=0, concat_axis=0, tiled=True)
    cols = got.shape[2]
    got = got.reshape(2, 1, near_blocks, held, cols)
    if spread > 1:
        got = lax.all_gather(got, "bs", axis=1, tiled=True)
    got = core_pair(got, swap(got, "core"), core).reshape(width, cols)
    edge = 384 + ff_here
    weight_in = got[:, :edge]
    if spread == 1:
        dense_pair = core_pair(dense_weight[None], swap(dense_weight, "core")[None], core).reshape(128, width)
    else:
        dense_all = lax.all_gather(dense_weight, ALL, axis=0, tiled=True).reshape(2, 2, near_blocks, HEAD_DIM, width)
        dense_pair = lax.dynamic_index_in_dim(
            lax.dynamic_index_in_dim(dense_all, hx, 0, keepdims=False), bz * 2 + by, 1, keepdims=False
        ).reshape(128, width)
    weight_out = jnp.concatenate([dense_pair.T, got[:, edge:]], 1)

    h, q, kv, pre, expand_out = front(x_all, gain[None], shift[None], weight_in, bias_in, cosine, sine, block)
    kv_all = kv if spread == 1 else lax.all_gather(kv, "bs", axis=0, tiled=True)
    attn_full, attn_low, lse = attend(table, q, kv_all, block)
    branches = jnp.concatenate([attn_low, expand_out], 1)
    out_parts = dot_rows(branches, weight_out).astype(BF)
    out_sum = scatter_sum(out_parts, share, width)

    grad_y = (cotangent[:, 0].astype(F32) * valid).astype(BF)
    g_mine = jnp.where(core == 0, grad_y[0], grad_y[1])
    g_away = jnp.where(core == 0, grad_y[1], grad_y[0])
    g_all = gather_pieces(g_mine, swap(g_away, "core"))

    out_away = swap(out_sum[1].astype(BF), "core").astype(F32)
    mixed = jnp.where(core == 0, jnp.stack([out_sum[0], out_away]), jnp.stack([out_away, out_sum[0]]))
    source = inputs[:, 0].astype(F32)
    output = (valid * (source + mixed + dense_b + shrink_b)).astype(BF).reshape(inputs.shape)

    grad_branches = dot(g_all, weight_out)
    grad_attention = grad_branches[:, :128].astype(BF)
    _, gelu_back = jax.vjp(lambda u: jax.nn.gelu(u, approximate=True), pre)
    grad_pre = gelu_back(grad_branches[:, 128:])[0].astype(BF)
    dq, dkv = attend_back(table, q, kv_all, attn_full, lse, grad_attention, block)
    if spread > 1:
        dkv = lax.psum_scatter(dkv, "bs", scatter_dimension=0, tiled=True)
    turned_grads = jnp.concatenate([dq, dkv[:, :128]], 1)
    plain_grads = turned_grads.astype(F32) * jnp.tile(cosine, (1, 2)) - dot(turned_grads, near_columns()) * jnp.tile(
        sine, (1, 2)
    )
    grad_in = jnp.concatenate([plain_grads.astype(BF), dkv[:, 128:], grad_pre], 1)
    h_parts = dot_rows(grad_in, weight_in).astype(BF)
    h_sum = scatter_sum(h_parts, share, width)
    grad_weight_out = dot_cols(g_all, branches)
    grad_weight_in = dot_cols(h, grad_in)

    both = jnp.concatenate([grad_weight_in, grad_weight_out[:, 128:]], 1).reshape(2, 2, spread, near_blocks, held, cols)
    mine = lax.dynamic_index_in_dim(both, core, 1, keepdims=False)
    away = lax.dynamic_index_in_dim(both, 1 - core, 1, keepdims=False).astype(BF)
    mine = mine + swap(away, "core").astype(F32)
    if spread > 1:
        mine = lax.psum_scatter(mine.astype(BF), "bs", scatter_dimension=1, tiled=True)
    mine = mine.astype(BF).reshape(ranks, held, cols)
    back = lax.all_to_all(mine, RANK, split_axis=0, concat_axis=0, tiled=True).astype(F32)
    grad_triple = (
        back[:, :, :384]
        .reshape(2, near_blocks, held, 3, 2, HEAD_DIM)
        .transpose(2, 3, 0, 4, 1, 5)
        .reshape(held, 3 * width)
    )
    grad_expand = back[:, :, 384:edge].transpose(1, 0, 2).reshape(held, ff)
    grad_shrink = back[:, :, edge:].transpose(1, 0, 2).reshape(held, ff)
    dense_grads = grad_weight_out[:, :128].T.reshape(2, HEAD_DIM, width)
    if spread == 1:
        dense_mine = lax.dynamic_index_in_dim(dense_grads, core, 0, keepdims=False)
        dense_away = lax.dynamic_index_in_dim(dense_grads, 1 - core, 0, keepdims=False)
        grad_dense = dense_mine + swap(dense_away.astype(BF), "core").astype(F32)
    else:
        spot = jnp.arange(ranks, dtype=jnp.int32).reshape(2, 1, near_blocks, 1, 1) == rank
        dense_whole = jnp.where(spot, dense_grads[None, :, None], 0.0).reshape(width, width)
        grad_dense = lax.psum_scatter(dense_whole, ALL, scatter_dimension=0, tiled=True)

    x_f = x_all.astype(F32)
    x_c = x_f - jnp.mean(x_f, -1, keepdims=True)
    normed_all = x_c * lax.rsqrt(jnp.mean(x_c * x_c, -1, keepdims=True) + EPS)
    parts_f = h_parts.astype(F32)
    sum_gain = jnp.sum(parts_f * normed_all, 0)
    sum_shift = jnp.sum(parts_f, 0)
    sum_in = jnp.sum(grad_in.astype(F32), 0)
    here = jnp.arange(ranks, dtype=jnp.int32)[:, None] == rank
    sum_triple = (
        jnp.where(here, sum_in[None, :384], 0.0)
        .reshape(2, near_blocks, 3, 2, HEAD_DIM)
        .transpose(2, 0, 3, 1, 4)
        .reshape(3 * width)
    )
    sum_expand = jnp.where(here, sum_in[None, 384:], 0.0).reshape(ff)
    sum_y = jnp.sum(grad_y.astype(F32), (0, 1))
    pieces = [leaf.reshape(devices, -1) for leaf in (sum_gain, sum_shift, sum_triple, sum_expand, sum_y)]
    small_sum = lax.psum_scatter(
        jnp.concatenate(pieces, 1).reshape(-1), ALL, scatter_dimension=0, tiled=True
    )
    small_grads = []
    begin = 0
    for piece in pieces:
        small_grads.append(small_sum[begin : begin + piece.shape[1]])
        begin += piece.shape[1]
    small_gain, small_shift, small_triple, small_expand, small_out = small_grads

    h_away = swap(h_sum[1].astype(BF), "core").astype(F32)
    grad_h = jnp.where(core == 0, jnp.stack([h_sum[0], h_away]), jnp.stack([h_away, h_sum[0]]))
    centred = source - jnp.mean(source, -1, keepdims=True)
    scale = lax.rsqrt(jnp.mean(centred * centred, -1, keepdims=True) + EPS)
    normed = centred * scale
    g = grad_h * gain
    grad_source = scale * (
        g - jnp.mean(g, -1, keepdims=True) - normed * jnp.mean(g * normed, -1, keepdims=True)
    )
    grad_inputs = (grad_y.astype(F32) + grad_source).astype(BF).reshape(inputs.shape)
    return (
        output,
        grad_inputs,
        small_gain,
        small_shift,
        grad_triple,
        small_triple,
        grad_dense,
        small_out,
        grad_expand,
        small_expand,
        grad_shrink,
        small_out,
    )


def solution(mesh):
    head, blk = mesh.devices.shape
    split = Mesh(mesh.devices.reshape(head // 2, 2, blk // (2 * Z_LEN), Z_LEN, 2), ALL)
    tokens = P(None, ("bs", "bz", "by"), ("hx", "core"), None)
    vector = P(ALL)
    matrix = P(ALL, None)
    return jax.shard_map(
        body,
        mesh=split,
        in_specs=(
            tokens,
            vector,
            vector,
            matrix,
            vector,
            matrix,
            vector,
            matrix,
            vector,
            matrix,
            vector,
            P(),
            P(),
            tokens,
        ),
        out_specs=(
            tokens,
            tokens,
            vector,
            vector,
            matrix,
            vector,
            matrix,
            vector,
            matrix,
            vector,
            matrix,
            vector,
        ),
        check_vma=False,
    )
```

```python
import functools

import jax
import jax.numpy as jnp
from jax import lax
from jax.experimental import pallas as pl
from jax.experimental.pallas import tpu as pltpu
from jax.sharding import Mesh
from jax.sharding import PartitionSpec as P

HEADS = 32
HEAD_DIM = 64
ROT = 32
EPS = 1e-05
NEG = -1e30
BF = jnp.bfloat16
F32 = jnp.float32

RANK = ("hx", "bz", "by")
ALL = ("hx", "core", "bs", "bz", "by")
Z_LEN = 4
SWAP = [(0, 1), (1, 0)]
UP = [(i, (i + 1) % Z_LEN) for i in range(Z_LEN)]
DOWN = [((i + 1) % Z_LEN, i) for i in range(Z_LEN)]
VMEM_LIMIT = 60 * 1024 * 1024


def around(far):
    return [(i, (i + far) % Z_LEN) for i in range(Z_LEN)]


def swap(value, axis):
    return lax.ppermute(value, axis, SWAP)


def dot_rows(left, right):
    return lax.dot_general(left, right, (((1,), (1,)), ((), ())), preferred_element_type=F32)


def dot_cols(left, right):
    return lax.dot_general(left, right, (((0,), (0,)), ((), ())), preferred_element_type=F32)


def dot(left, right):
    return jnp.dot(left, right, preferred_element_type=F32)


def fence(now, *then):
    return lax.optimization_barrier((tuple(now),) + then)[0]


def ring(value):
    return lax.ppermute(value, "bz", UP)


def both_ways(value):
    return swap(value, "hx"), swap(value, "by")


def far_ways(x_rows, y_rows):
    half = x_rows.shape[0] // 2
    return swap(y_rows[:half], "hx"), swap(x_rows[half:], "by")


def pair(low, high):
    return jnp.concatenate([low[0], high[0], low[1], high[1]], 0)


def add_low(left, right):
    return (left.astype(F32) + right.astype(F32)).astype(BF)


def far_terms(rest, got):
    half = got[0].shape[0] // 2
    return add_low(rest[2 * half : 3 * half], got[0][:half]), add_low(rest[3 * half :], got[1][:half])


def far_back(terms):
    return swap(terms[0], "by"), swap(terms[1], "hx")


def square_sums(rest, got, far, share):
    half = 2 * share
    a = rest[:half].astype(F32) + got[0][half:].astype(F32) + far[0].astype(F32)
    b = rest[half : 2 * half].astype(F32) + got[1][half:].astype(F32) + far[1].astype(F32)
    return [jnp.stack([a[row : row + share], b[row : row + share]]) for row in (0, share)]


def ring_back(total):
    return lax.ppermute(total.astype(BF), "bz", DOWN).astype(F32)


def other_first(index, pair):
    return jnp.where(index == 0, pair, pair[::-1])


def gather_small(value, devices):
    hx, core, bs, bz, by = (lax.axis_index(name) for name in ALL)
    value = value[None]
    for name, index in (("by", by), ("core", core), ("hx", hx)):
        value = other_first(index, jnp.stack([value, swap(value, name)]))
        value = value.reshape((-1,) + value.shape[2:])
    whole = jnp.stack([value] + [lax.ppermute(value, "bz", around(kz)) for kz in range(1, Z_LEN)])
    places = (bz + Z_LEN - jnp.arange(Z_LEN)) % Z_LEN
    whole = sum(
        jnp.where((places == z)[:, None, None], whole, jnp.zeros_like(whole)).sum(0)[None] * (jnp.arange(Z_LEN) == z)[:, None, None]
        for z in range(Z_LEN)
    )
    whole = whole.astype(value.dtype).reshape(1, Z_LEN, 2, 2, 2, -1)
    if devices > 8 * Z_LEN:
        whole = lax.all_gather(whole, "bs", axis=0, tiled=True)
    return whole.transpose(2, 3, 0, 1, 4, 5).reshape(devices, -1)


def scatter_small(value, devices):
    hx, core, bs, bz, by = (lax.axis_index(name) for name in ALL)
    value = value.reshape(2, 2, devices // (8 * Z_LEN), Z_LEN, 2, -1)
    for axis, name, index in ((0, "hx", hx), (0, "core", core), (2, "by", by)):
        mine = lax.dynamic_index_in_dim(value, index, axis, keepdims=False)
        away = lax.dynamic_index_in_dim(value, 1 - index, axis, keepdims=False)
        value = mine + swap(away, name)
    terms = [lax.dynamic_index_in_dim(value, (bz + kz) % Z_LEN, 1, keepdims=False) for kz in range(Z_LEN)]
    return terms[:1] + [lax.ppermute(terms[kz], "bz", around(kz)) for kz in range(1, Z_LEN)]


def small_sum(terms, devices):
    total = sum(terms)
    if devices > 8 * Z_LEN:
        total = lax.psum_scatter(total, "bs", scatter_dimension=0, tiled=True)
    return total.reshape(-1)


def turn(value, cosine, sine, lane):
    near = jnp.where(
        (lane % HEAD_DIM) < ROT // 2,
        pltpu.roll(value, 128 - ROT // 2, 1),
        pltpu.roll(value, ROT // 2, 1),
    )
    return value * cosine + near * sine


def by_row(block, lanes):
    return pl.BlockSpec((block, lanes), lambda i: (i, 0))


def whole(rows, lanes):
    return pl.BlockSpec((rows, lanes), lambda i: (0, 0))


def take_rows(rows_ref, pieces, begin):
    half = pieces[-1].shape[0]
    step = pl.program_id(0)
    for at in range(3):

        @pl.when(step == begin + at)
        def _(at=at):
            rows_ref[...] = pieces[at][...]

    @pl.when(step == begin + 3)
    def _():
        rows_ref[:half] = pieces[3][...]
        rows_ref[half:] = pieces[4][...]


def piece_specs(pieces):
    return [whole(*piece.shape) for piece in pieces]


def front_kernel(*refs):
    pieces, refs = refs[:5], refs[5:]
    gain_ref, shift_ref, w_ref, bias_ref, cos_ref, sin_ref = refs[:6]
    h_ref, q_ref, kv_ref, pre_ref, out_ref, mean_ref, scale_ref, x_ref = refs[-8:]
    take_rows(x_ref, pieces, 0)
    x = x_ref[...].astype(F32)
    mean = jnp.mean(x, -1, keepdims=True)
    centred = x - mean
    scale = lax.rsqrt(jnp.mean(centred * centred, -1, keepdims=True) + EPS)
    mean_ref[...] = mean
    scale_ref[...] = scale
    h = (centred * scale * gain_ref[...] + shift_ref[...]).astype(BF)
    h_ref[...] = h
    linear = dot(h, w_ref[...]) + bias_ref[...]
    lane = lax.broadcasted_iota(jnp.int32, (x.shape[0], 128), 1)
    cosine, sine = cos_ref[...], sin_ref[...]
    q_ref[...] = turn(linear[:, :128], cosine, sine, lane).astype(BF) * BF(HEAD_DIM**-0.5)
    kv_ref[:, :128] = turn(linear[:, 128:256], cosine, sine, lane).astype(BF)
    kv_ref[:, 128:] = linear[:, 256:384].astype(BF)
    pre = linear[:, 384:]
    pre_ref[...] = pre
    out_ref[...] = (0.5 * pre * (1.0 + jnp.tanh(0.7978845608 * (pre + 0.044715 * pre * pre * pre)))).astype(BF)


def half_rows(begin, block, lanes):
    return pl.BlockSpec((block, lanes), lambda i: (i + begin, 0))


def front(pieces, held, gain, shift, weight, bias, cosine, sine):
    block, width = pieces[0].shape
    rows = 8 * block
    cols = weight.shape[1]
    wide = cols - 384
    here = functools.partial(half_rows, 4 if held else 0, block)
    lanes = (width, 128, 256, wide, wide, 1, 1)
    types = (BF, BF, BF, F32, BF, F32, F32)
    return pl.pallas_call(
        front_kernel,
        grid=(4,),
        in_specs=piece_specs(pieces)
        + [whole(1, width), whole(1, width), whole(width, cols), whole(1, cols), here(128), here(128)]
        + [pl.BlockSpec(memory_space=pl.ANY)] * len(held),
        out_specs=[here(n) for n in lanes],
        out_shape=[jax.ShapeDtypeStruct((rows, n), kind) for n, kind in zip(lanes, types)],
        input_output_aliases={11 + i: i for i in range(len(held))},
        scratch_shapes=[pltpu.VMEM((block, width), BF)],
        compiler_params=pltpu.CompilerParams(vmem_limit_bytes=VMEM_LIMIT),
        cost_estimate=pl.CostEstimate(
            flops=rows * width * cols + 6 * rows * width, bytes_accessed=rows * width * 3, transcendentals=rows * wide
        ),
    )(*pieces, gain, shift, weight, bias, cosine, sine, *held)


def two_heads(value):
    lane = lax.broadcasted_iota(jnp.int32, value.shape, 1)
    zero = jnp.zeros_like(value)
    return jnp.concatenate([jnp.where(lane < HEAD_DIM, value, zero), jnp.where(lane < HEAD_DIM, zero, value)], 0)


def one_row(value):
    half = value.shape[0] // 2
    lane = lax.broadcasted_iota(jnp.int32, (half, 128), 1)
    return jnp.where(lane < HEAD_DIM, value[:half], value[half:])


def allowed_pairs(meta_ref, block, query_at, key_at):
    turned, length = meta_ref[0], meta_ref[1]
    shape = (2 * block, block)
    query = query_at * block + ((lax.broadcasted_iota(jnp.int32, shape, 0) & (block - 1)) ^ turned)
    key = key_at * block + (lax.broadcasted_iota(jnp.int32, shape, 1) ^ turned)
    return (key <= query) & (key < length)


def key_ranges(meta_ref, block, query_at):
    length = meta_ref[1]
    plain = jnp.minimum(query_at, length // block)
    last = jnp.minimum(query_at + 1, (length + block - 1) // block)
    return plain, last


def spot_of(at):
    near = 2 * Z_LEN
    spot = lax.rem(at, near)
    return lax.div(at, near) * 4 + lax.div(spot, 4) * 2 + lax.rem(spot, 2), slice(None), lax.rem(lax.div(spot, 2), 2)


def rows_of(ref, at):
    value = ref[spot_of(at)]
    return value.reshape(value.shape[0] * value.shape[1], value.shape[2])


def add_rows(ref, at, value):
    ref[spot_of(at)] += value.reshape(4, value.shape[0] // 4, value.shape[1])


def flat(ref):
    value = ref[0, :, 0]
    return value.reshape(value.shape[0] * value.shape[1], value.shape[2])


def attend_kernel(block, meta_ref, query_ref, order_ref, q_ref, kv_ref, full_ref, low_ref, lse_ref):
    query_at = query_ref[pl.program_id(0)]
    queries = two_heads(flat(q_ref))

    def step(masked, at, state):
        top, total, mixed = state
        both = rows_of(kv_ref, order_ref[at])
        scores = dot_rows(queries, both[:, :128])
        if masked:
            allowed = allowed_pairs(meta_ref, block, query_at, at)
            scores = jnp.where(allowed, scores, NEG)
        fresh = jnp.maximum(top, jnp.max(scores, -1, keepdims=True))
        factor = jnp.exp(top - fresh)
        weights = jnp.exp(scores - fresh)
        if masked:
            weights = jnp.where(allowed, weights, 0.0)
        total = total * factor + jnp.sum(weights, -1, keepdims=True)
        return fresh, total, mixed * factor + dot(weights.astype(BF), both[:, 128:])

    state = (
        jnp.full((2 * block, 1), NEG, F32),
        jnp.zeros((2 * block, 1), F32),
        jnp.zeros((2 * block, 128), F32),
    )
    plain, last = key_ranges(meta_ref, block, query_at)
    state = lax.fori_loop(0, plain, functools.partial(step, False), state)
    top, total, mixed = lax.fori_loop(plain, last, functools.partial(step, True), state)
    full = one_row(mixed / total)
    shape = full_ref.shape[1:2] + full_ref.shape[3:]
    full_ref[0, :, 0] = full.reshape(shape)
    low_ref[0, :, 0] = full.astype(BF).reshape(shape)
    lse_ref[...] = jnp.broadcast_to(top + jnp.log(total), lse_ref.shape)


def placed(share, lanes):
    return pl.BlockSpec((1, 4, 1, share, lanes), lambda i, *_: ((i // 4) * 2 + i % 2, 0, (i // 2) % 2, 0, 0))


def attend(table, q, kv, share):
    block = 4 * share
    blocks = 2 * Z_LEN
    rows, keys = q.shape[0], kv.shape[0]
    shape = (4, 4, Z_LEN // 2, share, 128)
    kv_shape = (keys // (2 * Z_LEN * share), 4, Z_LEN // 2, share, 256)
    full, low, lse = pl.pallas_call(
        functools.partial(attend_kernel, block),
        grid_spec=pltpu.PrefetchScalarGridSpec(
            num_scalar_prefetch=3,
            grid=(blocks,),
            in_specs=[placed(share, 128), pl.BlockSpec(kv_shape, lambda i, *_: (0, 0, 0, 0, 0))],
            out_specs=[placed(share, 128), placed(share, 128), pl.BlockSpec((2 * block, 128), lambda i, *_: (i, 0))],
        ),
        out_shape=[
            jax.ShapeDtypeStruct(shape, F32),
            jax.ShapeDtypeStruct(shape, BF),
            jax.ShapeDtypeStruct((2 * rows, 128), F32),
        ],
        compiler_params=pltpu.CompilerParams(vmem_limit_bytes=VMEM_LIMIT),
        cost_estimate=pl.CostEstimate(
            flops=16 * rows * keys * 128, bytes_accessed=rows * 128 * 16, transcendentals=rows * keys
        ),
    )(*table, q.reshape(shape), kv.reshape(kv_shape))
    return full, low.reshape(rows, 128), lse


def attend_back_kernel(blocks, block, meta_ref, query_ref, order_ref, q_ref, kv_ref, full_ref, lse_ref, grad_ref, dq_ref, dkv_ref, dk_acc, dv_acc):
    at_block = pl.program_id(0)
    query_at = query_ref[at_block]
    queries = two_heads(flat(q_ref))
    grads = two_heads(flat(grad_ref))
    full = flat(full_ref)
    delta = jnp.sum(grads.astype(F32) * jnp.concatenate([full, full], 0), -1, keepdims=True)
    lse = lse_ref[:, :1]

    @pl.when(at_block == 0)
    def _():
        dk_acc[...] = jnp.zeros_like(dk_acc)
        dv_acc[...] = jnp.zeros_like(dv_acc)

    def step(masked, at, grad_query):
        spot = order_ref[at]
        both = rows_of(kv_ref, spot)
        keys = both[:, :128]
        scores = dot_rows(queries, keys)
        if masked:
            allowed = allowed_pairs(meta_ref, block, query_at, at)
            scores = jnp.where(allowed, scores, NEG)
        weights = jnp.exp(scores - lse)
        if masked:
            weights = jnp.where(allowed, weights, 0.0)
        grad_scores = (weights * (dot_rows(grads, both[:, 128:]) - delta)).astype(BF)
        add_rows(dk_acc, spot, dot_cols(grad_scores, queries))
        add_rows(dv_acc, spot, dot_cols(weights.astype(BF), grads))
        return grad_query + dot(grad_scores, keys)

    plain, last = key_ranges(meta_ref, block, query_at)
    grad_query = jnp.zeros((2 * block, 128), F32)
    grad_query = lax.fori_loop(0, plain, functools.partial(step, False), grad_query)
    grad_query = lax.fori_loop(plain, last, functools.partial(step, True), grad_query)
    shape = dq_ref.shape[1:2] + dq_ref.shape[3:]
    dq_ref[0, :, 0] = (one_row(grad_query) * HEAD_DIM**-0.5).astype(BF).reshape(shape)

    @pl.when(at_block == blocks - 1)
    def _():
        dkv_ref[..., :128] = dk_acc[...].astype(BF)
        dkv_ref[..., 128:] = dv_acc[...].astype(BF)


def attend_back(table, q, kv, full, lse, grad, share):
    block = 4 * share
    blocks = 2 * Z_LEN
    rows, keys = q.shape[0], kv.shape[0]
    shape = (4, 4, Z_LEN // 2, share, 128)
    kv_shape = (keys // (2 * Z_LEN * share), 4, Z_LEN // 2, share, 256)
    kv_spec = pl.BlockSpec(kv_shape, lambda i, *_: (0, 0, 0, 0, 0))
    dq, dkv = pl.pallas_call(
        functools.partial(attend_back_kernel, blocks, block),
        grid_spec=pltpu.PrefetchScalarGridSpec(
            num_scalar_prefetch=3,
            grid=(blocks,),
            in_specs=[
                placed(share, 128),
                kv_spec,
                placed(share, 128),
                pl.BlockSpec((2 * block, 128), lambda i, *_: (i, 0)),
                placed(share, 128),
            ],
            out_specs=[placed(share, 128), kv_spec],
            scratch_shapes=[pltpu.VMEM(kv_shape[:-1] + (128,), F32), pltpu.VMEM(kv_shape[:-1] + (128,), F32)],
        ),
        out_shape=[jax.ShapeDtypeStruct(shape, BF), jax.ShapeDtypeStruct(kv_shape, BF)],
        compiler_params=pltpu.CompilerParams(vmem_limit_bytes=VMEM_LIMIT),
        cost_estimate=pl.CostEstimate(
            flops=40 * rows * keys * 128, bytes_accessed=rows * 128 * 24, transcendentals=rows * keys
        ),
    )(*table, q.reshape(shape), kv.reshape(kv_shape), full, lse, grad.reshape(shape))
    return dq.reshape(rows, 128), dkv.reshape(keys, 256)


def store_spots(parts, total):
    to_x, to_y, rest = parts
    half = total.shape[0] // 2
    total = total.astype(BF)
    places = (((rest, 0), (rest, 1)), ((to_x, 1), (rest, 3)), ((rest, 2), (to_y, 1)), ((to_x, 0), (to_y, 0)))
    for at, (low, high) in enumerate(places):

        @pl.when(pl.program_id(0) == at)
        def _(low=low, high=high):
            low[0][low[1] * half : (low[1] + 1) * half] = total[:half]
            high[0][high[1] * half : (high[1] + 1) * half] = total[half:]


def spot_specs(block, width):
    return [whole(block, width), whole(block, width), whole(2 * block, width)]


def spot_shapes(block, width):
    return [jax.ShapeDtypeStruct((rows, width), BF) for rows in (block, block, 2 * block)]


def out_kernel(attn_ref, units_ref, w_ref, *parts):
    store_spots(parts, dot_rows(attn_ref[...], w_ref[:, :128]) + dot_rows(units_ref[...], w_ref[:, 128:]))


def out_partial(attn, units, weight, block, begin):
    rows, width = attn.shape[0], weight.shape[0]
    return pl.pallas_call(
        out_kernel,
        grid=(4,),
        in_specs=[half_rows(begin, block, 128), half_rows(begin, block, units.shape[1]), whole(*weight.shape)],
        out_specs=spot_specs(block, width),
        out_shape=spot_shapes(block, width),
        compiler_params=pltpu.CompilerParams(vmem_limit_bytes=VMEM_LIMIT),
        cost_estimate=pl.CostEstimate(
            flops=rows * width * weight.shape[1], bytes_accessed=rows * width, transcendentals=0
        ),
    )(attn, units, weight)


def branch_kernel(*refs):
    one, two, (w_ref, pre_ref, attn_ref, grad_ref, g_ref) = refs[:5], refs[5:10], refs[10:]
    take_rows(g_ref, one, 0)
    take_rows(g_ref, two, 4)
    both = dot(g_ref[...], w_ref[...])
    attn_ref[...] = both[:, :128].astype(BF)
    u = pre_ref[...]
    square = u * u
    bend = jnp.tanh(0.7978845608 * u * (1.0 + 0.044715 * square))
    slope = 0.5 * (1.0 + bend) + 0.5 * u * (1.0 - bend * bend) * (0.7978845608 * (1.0 + 3 * 0.044715 * square))
    grad_ref[...] = (both[:, 128:] * slope).astype(BF)


def branch_grads(pieces, weight, pre, block):
    width = weight.shape[0]
    rows, wide = pre.shape
    return pl.pallas_call(
        branch_kernel,
        grid=(rows // block,),
        in_specs=piece_specs(pieces) + [whole(*weight.shape), by_row(block, wide)],
        out_specs=[by_row(block, 128), by_row(block, wide), by_row(block, width)],
        out_shape=[
            jax.ShapeDtypeStruct((rows, 128), BF),
            jax.ShapeDtypeStruct((rows, wide), BF),
            jax.ShapeDtypeStruct((rows, width), BF),
        ],
        compiler_params=pltpu.CompilerParams(vmem_limit_bytes=VMEM_LIMIT),
        cost_estimate=pl.CostEstimate(
            flops=2 * rows * width * weight.shape[1], bytes_accessed=rows * width * 4, transcendentals=rows * wide
        ),
    )(*pieces, weight, pre)


def turn_back(value, cosine, sine, lane):
    return turn(value.astype(F32), cosine, -sine, lane).astype(BF)


def back_kernel(*refs):
    pieces, refs = refs[:5], refs[5:]
    dq_ref, dkv_ref, units_ref, w_ref, cos_ref, sin_ref, mean_ref, scale_ref = refs[:8]
    parts, (linear_ref, gain_ref, shift_ref, small_ref, x_ref) = refs[-8:-5], refs[-5:]
    take_rows(x_ref, pieces, 0)
    lane = lax.broadcasted_iota(jnp.int32, dq_ref.shape, 1)
    cosine, sine = cos_ref[...], sin_ref[...]
    linear_ref[:, :128] = turn_back(dq_ref[...], cosine, sine, lane)
    linear_ref[:, 128:256] = turn_back(dkv_ref[:, :128], cosine, sine, lane)
    linear_ref[:, 256:] = dkv_ref[:, 128:]
    linear = linear_ref[...]
    units = units_ref[...]
    total = dot_rows(linear, w_ref[:, :384]) + dot_rows(units, w_ref[:, 384:])
    store_spots(parts, total)
    normed = (x_ref[...].astype(F32) - mean_ref[...]) * scale_ref[...]

    @pl.when(pl.program_id(0) == 0)
    def _():
        gain_ref[...] = jnp.zeros_like(gain_ref)
        shift_ref[...] = jnp.zeros_like(shift_ref)
        small_ref[...] = jnp.zeros_like(small_ref)

    gain_ref[...] += jnp.sum(total * normed, 0, keepdims=True)
    shift_ref[...] += jnp.sum(total, 0, keepdims=True)
    small_ref[:, :384] += jnp.sum(linear.astype(F32), 0, keepdims=True)
    small_ref[:, 384:] += jnp.sum(units.astype(F32), 0, keepdims=True)


def back_partial(pieces, dq, dkv, units, weight, cosine, sine, mean, scale, block, begin, held):
    rows = dq.shape[0]
    width, cols = weight.shape
    here = lambda lanes: half_rows(begin, block, lanes)
    *parts, linear, gain, shift, small = pl.pallas_call(
        back_kernel,
        grid=(4,),
        in_specs=piece_specs(pieces)
        + [here(128), here(256), here(units.shape[1]), whole(*weight.shape), here(128), here(128), here(1), here(1)]
        + [pl.BlockSpec(memory_space=pl.ANY)] * len(held),
        out_specs=spot_specs(block, width) + [here(384), whole(1, width), whole(1, width), whole(1, cols)],
        out_shape=spot_shapes(block, width)
        + [
            jax.ShapeDtypeStruct((rows, 384), BF),
            jax.ShapeDtypeStruct((1, width), F32),
            jax.ShapeDtypeStruct((1, width), F32),
            jax.ShapeDtypeStruct((1, cols), F32),
        ],
        input_output_aliases={13 + i: 3 + i for i in range(len(held))},
        scratch_shapes=[pltpu.VMEM((block, width), BF)],
        compiler_params=pltpu.CompilerParams(vmem_limit_bytes=VMEM_LIMIT),
        cost_estimate=pl.CostEstimate(
            flops=rows * width * cols, bytes_accessed=rows * width * 2, transcendentals=0
        ),
    )(*pieces, dq, dkv, units, weight, cosine, sine, mean, scale, *held)
    return parts, linear, jnp.concatenate([gain, shift, small], 1)


def weight_kernel(core_ref, rows_ref, *refs):
    *others, out_ref = refs
    rows = rows_ref[...]
    begin = 0
    for other in others:
        end = begin + other.shape[1]
        out_ref[0, 0, :, begin:end] = dot_cols(rows, other[...]).astype(BF)
        begin = end


def weight_grads(core, left, *rights):
    rows, width = left.shape
    cols = sum(right.shape[1] for right in rights)
    quarter = width // 4
    return pl.pallas_call(
        weight_kernel,
        grid_spec=pltpu.PrefetchScalarGridSpec(
            num_scalar_prefetch=1,
            grid=(4,),
            in_specs=[pl.BlockSpec((rows, quarter), lambda i, c: (0, i))]
            + [pl.BlockSpec(right.shape, lambda i, c: (0, 0)) for right in rights],
            out_specs=pl.BlockSpec((1, 1, quarter, cols), lambda i, c: ((i + c[0]) % 2, i // 2, 0, 0)),
        ),
        out_shape=jax.ShapeDtypeStruct((2, 2, quarter, cols), BF),
        compiler_params=pltpu.CompilerParams(vmem_limit_bytes=VMEM_LIMIT),
        cost_estimate=pl.CostEstimate(
            flops=2 * rows * width * cols, bytes_accessed=2 * rows * width, transcendentals=0
        ),
    )(core[None], left, *rights)


def pack_kernel(triple_ref, expand_ref, shrink_ref, in_ref, out_ref):
    ranks = in_ref.shape[0]
    near = ranks // 2
    wide = out_ref.shape[2]
    for rank in range(ranks):
        hx, b8 = rank // near, rank % near
        for s in range(3):
            pair = [
                triple_ref[:, pl.ds((s * HEADS + hx * 2 * near + c * near + b8) * HEAD_DIM, HEAD_DIM)] for c in range(2)
            ]
            in_ref[rank, :, s * 128 : (s + 1) * 128] = jnp.concatenate(pair, 1)
        in_ref[rank, :, 384:] = expand_ref[:, rank * wide : (rank + 1) * wide]
        out_ref[rank] = shrink_ref[:, rank * wide : (rank + 1) * wide]


def pack(triple, expand, shrink, ranks):
    held = triple.shape[0]
    wide = expand.shape[1] // ranks
    return pl.pallas_call(
        pack_kernel,
        out_shape=[
            jax.ShapeDtypeStruct((ranks, held, 384 + wide), BF),
            jax.ShapeDtypeStruct((ranks, held, wide), BF),
        ],
        compiler_params=pltpu.CompilerParams(vmem_limit_bytes=VMEM_LIMIT),
    )(triple, expand, shrink)


def unpack_in_kernel(back_ref, triple_ref, expand_ref):
    ranks = back_ref.shape[0]
    near = ranks // 2
    wide = back_ref.shape[2] - 384
    for rank in range(ranks):
        expand_ref[:, rank * wide : (rank + 1) * wide] = back_ref[rank, :, 384:].astype(F32)
    for rank in range(0, ranks, 2):
        hx, b8 = rank // near, rank % near
        for s in range(3):
            for c in range(2):
                lanes = slice(s * 128 + c * HEAD_DIM, s * 128 + (c + 1) * HEAD_DIM)
                pair = jnp.concatenate([back_ref[rank, :, lanes], back_ref[rank + 1, :, lanes]], 1)
                at = (s * HEADS + hx * 2 * near + c * near + b8) * HEAD_DIM
                triple_ref[:, at : at + 128] = pair.astype(F32)


def unpack_in(back):
    ranks, held, cols = back.shape
    return pl.pallas_call(
        unpack_in_kernel,
        out_shape=[
            jax.ShapeDtypeStruct((held, 3 * HEADS * HEAD_DIM), F32),
            jax.ShapeDtypeStruct((held, ranks * (cols - 384)), F32),
        ],
        compiler_params=pltpu.CompilerParams(vmem_limit_bytes=VMEM_LIMIT),
    )(back)


def unpack_out_kernel(back_ref, shrink_ref):
    wide = back_ref.shape[2]
    for rank in range(back_ref.shape[0]):
        shrink_ref[:, rank * wide : (rank + 1) * wide] = back_ref[rank].astype(F32)


def unpack_out(back):
    ranks, held, cols = back.shape
    return pl.pallas_call(
        unpack_out_kernel,
        out_shape=jax.ShapeDtypeStruct((held, ranks * cols), F32),
        compiler_params=pltpu.CompilerParams(vmem_limit_bytes=VMEM_LIMIT),
    )(back)


def turn_tables(positions):
    half = ROT // 2
    inverse = 10000.0 ** (-(jnp.arange(half, dtype=F32) * 2.0) / ROT)
    angles = positions.astype(F32)[:, None] * inverse[None, :]
    cosine, sine = jnp.cos(angles), jnp.sin(angles)
    rest = (positions.shape[0], HEAD_DIM - ROT)
    cosine = jnp.concatenate([cosine, cosine, jnp.ones(rest, F32)], 1)
    sine = jnp.concatenate([-sine, sine, jnp.zeros(rest, F32)], 1)
    return jnp.tile(cosine, (1, 2)), jnp.tile(sine, (1, 2))


def core_pair(own, other, core):
    return jnp.where(core == 0, jnp.stack([own, other], 1), jnp.stack([other, own], 1))


def body(
    inputs,
    norm_gain,
    norm_bias,
    triple_weight,
    triple_bias,
    dense_weight,
    dense_bias,
    expand_weight,
    expand_bias,
    shrink_weight,
    shrink_bias,
    lengths,
    block_order,
    cotangent,
):
    share, width = inputs.shape[2], inputs.shape[3]
    hx, core, bs, bz, by = (lax.axis_index(name) for name in ALL)
    spread = lax.axis_size("bs")
    ranks = 2 * Z_LEN * 2
    devices = 2 * ranks * spread
    block = 4 * share
    rows = ranks * 2 * share
    near_blocks = Z_LEN * 2
    blocks = block_order.shape[0]
    held = width // devices
    ff = expand_weight.shape[1]
    ff_here = ff // ranks
    length = lengths[core]

    def block_at(index):
        return jnp.sum(jnp.where(jnp.arange(blocks, dtype=jnp.int32) == index, block_order, 0))

    token_pos = (
        block_at(bs * near_blocks + bz * 2 + by) * block
        + (hx * 2 + core) * share
        + jnp.arange(share, dtype=jnp.int32)
    )
    valid = (token_pos[None, :] < lengths[:, None]).astype(F32)[:, :, None]

    spots = jnp.arange(blocks, dtype=jnp.int32)
    within = spots % near_blocks
    index = spots - within + ((bz + Z_LEN - within // 2) % Z_LEN) * 2 + (by + within) % 2
    key_at = jnp.sum(jnp.where(index[:, None] == spots[None, :], block_order[None, :], 0), 1)
    query_at = lax.dynamic_slice_in_dim(key_at, bs * near_blocks, near_blocks)
    turned = hx * 2 * share + core * share
    inside = (jnp.arange(block, dtype=jnp.int32) ^ turned).reshape(1, 1, 4, 1, share)
    block_pos = query_at.reshape(2, Z_LEN // 2, 2).transpose(0, 2, 1)[:, :, None, :, None]
    row_pos = (block_pos * block + inside).reshape(rows)
    order = jnp.sum(jnp.where(key_at[None, :] == spots[:, None], spots[None, :], 0), 1)
    table = jnp.where(jnp.arange(2) == 0, turned, length).astype(jnp.int32), query_at, order
    cosine, sine = turn_tables(row_pos)

    def to_cols(sent):
        got = lax.all_to_all(sent, RANK, split_axis=0, concat_axis=0, tiled=True)
        got = got.reshape(2, 1, near_blocks, held, sent.shape[2])
        return lax.all_gather(got, "bs", axis=1, tiled=True) if spread > 1 else got

    def to_rows(mine):
        cols = mine.shape[-1]
        if spread > 1:
            mine = mine.reshape(2, spread, near_blocks, held, cols)
            mine = lax.psum_scatter(mine, "bs", scatter_dimension=1, tiled=True)
        return lax.all_to_all(mine.reshape(ranks, held, cols), RANK, split_axis=0, concat_axis=0, tiled=True)

    x_a = lax.dynamic_index_in_dim(inputs[:, 0], core, 0, keepdims=False)
    x_b = swap(lax.dynamic_index_in_dim(inputs[:, 0], 1 - core, 0, keepdims=False), "core")
    x_a1, x_b1 = ring(x_a), ring(x_b)
    grad_y = (cotangent[:, 0].astype(F32) * valid).astype(BF)
    g_a = lax.dynamic_index_in_dim(grad_y, core, 0, keepdims=False)
    g_b = swap(lax.dynamic_index_in_dim(grad_y, 1 - core, 0, keepdims=False), "core")
    sent_in, sent_out = pack(triple_weight, expand_weight, shrink_weight, ranks)
    small = jnp.concatenate([norm_gain, norm_bias, triple_bias, expand_bias, dense_bias, shrink_bias])
    g_0 = jnp.stack([g_a, g_b])

    x_1 = jnp.stack([x_a1, x_b1])
    x_1, own_one = fence((x_1, pair((x_a, x_b), x_1)), g_0, sent_in)
    got_one = both_ways(own_one)
    x_2 = ring(x_1)
    x_3 = ring(x_2)

    got_one, own_two, sent_in, small = fence((got_one, pair(x_2, x_3), sent_in, small))
    got_in = to_cols(sent_in)
    far_one = far_ways(*got_one)
    got_two = both_ways(own_two)
    small = gather_small(small, devices)
    x_one = (own_one, *got_one, *far_one)

    got_two, g_0, small = fence((got_two, g_0, small), far_one)
    far_two = far_ways(*got_two)
    g_1 = ring(g_0)
    x_two = (own_two, *got_two, *far_two)
    got_in = fence((got_in,), g_1)[0]
    weight_in = core_pair(got_in, swap(got_in, "core"), core).reshape(width, -1)

    cuts = [0]
    for leaf in (norm_gain, norm_bias, triple_bias, expand_bias, dense_bias, shrink_bias):
        cuts.append(cuts[-1] + leaf.shape[0])
    gain, shift, triple_b, expand_b, dense_b, shrink_b = (
        small[:, low:high].reshape(-1).astype(F32) for low, high in zip(cuts[:-1], cuts[1:])
    )
    rank = hx * near_blocks + bz * 2 + by
    bias_triple = lax.dynamic_index_in_dim(
        triple_b.reshape(3, 2, 2, near_blocks, HEAD_DIM).transpose(1, 3, 0, 2, 4).reshape(ranks, 384), rank, 0
    )
    bias_expand = lax.dynamic_index_in_dim(expand_b.reshape(ranks, ff_here), rank, 0)
    bias_in = jnp.concatenate([bias_triple, bias_expand], 1)

    weight_in, g_1, own_one = fence((weight_in, g_1, pair(g_0, g_1)), far_two)
    got_one = both_ways(own_one)
    g_2 = ring(g_1)
    g_3 = ring(g_2)
    into = (gain[None], shift[None], weight_in, bias_in, cosine, sine)
    h, q, kv, pre, expand_out, mean, scale = front(x_two, front(x_one, (), *into), *into)

    q, got_one, own_two, sent_out = fence((q, got_one, pair(g_2, g_3), sent_out))
    got_out = to_cols(sent_out)
    far_one = far_ways(*got_one)
    got_two = both_ways(own_two)
    g_one = (own_one, *got_one, *far_one)
    kv_all = kv if spread == 1 else lax.all_gather(kv, "bs", axis=0, tiled=True)
    attn_full, attn_low, lse = attend(table, q, kv_all, share)

    attn_low, got_out, got_two = fence((attn_low, got_out, got_two), far_one)
    far_two = far_ways(*got_two)
    g_two = (own_two, *got_two, *far_two)
    shrink_here = core_pair(got_out, swap(got_out, "core"), core).reshape(width, -1)
    if spread == 1:
        dense_pair = core_pair(dense_weight[None], swap(dense_weight, "core")[None], core).reshape(128, width)
    else:
        dense_all = lax.all_gather(dense_weight, ALL, axis=0, tiled=True).reshape(2, 2, near_blocks, HEAD_DIM, width)
        dense_pair = lax.dynamic_index_in_dim(
            lax.dynamic_index_in_dim(dense_all, hx, 0, keepdims=False), bz * 2 + by, 1, keepdims=False
        ).reshape(128, width)
    weight_out = jnp.concatenate([dense_pair.T, shrink_here], 1)
    o_two = out_partial(attn_low, expand_out, weight_out, block, 4)
    o_one = out_partial(attn_low, expand_out, weight_out, block, 0)

    o_one, o_two, g_one, g_two = fence((o_one, o_two, g_one, g_two))
    got_two = swap(o_two[0], "hx"), swap(o_two[1], "by")
    grad_attention, grad_pre, g_all = branch_grads(g_one + g_two, weight_out, pre, block)
    shrink_grads = weight_grads(core, g_all, expand_out)

    grad_attention, shrink_grads, o_one, terms = fence((grad_attention, shrink_grads, o_one, far_terms(o_two[2], got_two)))
    far_two = far_back(terms)
    got_one_out = swap(o_one[0], "hx"), swap(o_one[1], "by")
    dq, dkv = attend_back(table, q, kv_all, attn_full, lse, grad_attention, share)
    if spread > 1:
        dkv = lax.psum_scatter(dkv, "bs", scatter_dimension=0, tiled=True)
    mine = add_low(shrink_grads[0], swap(shrink_grads[1], "core"))

    dq, mine, terms, out_two = fence((dq, mine, far_terms(o_one[2], got_one_out), square_sums(o_two[2], got_two, far_two, share)))
    shrink_rows = to_rows(mine)
    far_one = far_back(terms)
    out_sum = ring_back(out_two[1])
    from_back = (dq, dkv, grad_pre, weight_in, cosine, sine, mean, scale, block)
    h_two, grad_linear, sums_two = back_partial(x_two, *from_back, 4, ())

    h_two, grad_linear, out_sum = fence((h_two, grad_linear, out_sum), far_one)
    got_two = swap(h_two[0], "hx"), swap(h_two[1], "by")
    out_sum = ring_back(out_sum + out_two[0])
    h_one, grad_linear, sums_one = back_partial(x_one, *from_back, 0, (grad_linear,))

    grad_linear, h, h_one, terms, out_sum = fence((grad_linear, h, h_one, far_terms(h_two[2], got_two), out_sum))
    far_two = far_back(terms)
    got_one = swap(h_one[0], "hx"), swap(h_one[1], "by")
    in_grads = weight_grads(core, h, grad_linear, grad_pre)
    mine = add_low(in_grads[0], swap(in_grads[1], "core"))
    in_rows = to_rows(mine)
    out_one = square_sums(o_one[2], got_one_out, far_one, share)
    out_sum = ring_back(out_sum + out_one[1]) + out_one[0]
    sum_gain, sum_shift, sum_in = jnp.split(sums_one + sums_two, [width, 2 * width], 1)

    terms, h_sums, sum_in, g_all = fence(
        (far_terms(h_one[2], got_one), square_sums(h_two[2], got_two, far_two, share), sum_in, g_all), shrink_rows
    )
    far_one = far_back(terms)
    h_sum = ring_back(h_sums[1])
    grad_dense_here = dot_cols(g_all, attn_low)
    grad_shrink = unpack_out(shrink_rows)

    h_sums, h_sum, h_more, out_sum = fence((h_sums, h_sum, square_sums(h_one[2], got_one, far_one, share), out_sum))
    h_sum = ring_back(ring_back(h_sum + h_sums[0]) + h_more[1]) + h_more[0]
    grad_triple, grad_expand = unpack_in(in_rows)

    dense_grads = grad_dense_here.T.reshape(2, HEAD_DIM, width)
    if spread == 1:
        dense_mine = lax.dynamic_index_in_dim(dense_grads, core, 0, keepdims=False)
        dense_away = lax.dynamic_index_in_dim(dense_grads, 1 - core, 0, keepdims=False)
        grad_dense = dense_mine + swap(dense_away.astype(BF), "core").astype(F32)
    else:
        spot = jnp.arange(ranks, dtype=jnp.int32).reshape(2, 1, near_blocks, 1, 1) == rank
        dense_whole = jnp.where(spot, dense_grads[None, :, None], 0.0).reshape(width, width)
        grad_dense = lax.psum_scatter(dense_whole, ALL, scatter_dimension=0, tiled=True)

    here = jnp.arange(ranks, dtype=jnp.int32)[:, None] == rank
    sum_triple = (
        jnp.where(here, sum_in[:, :384], 0.0)
        .reshape(2, near_blocks, 3, 2, HEAD_DIM)
        .transpose(2, 0, 3, 1, 4)
        .reshape(3 * width)
    )
    sum_expand = jnp.where(here, sum_in[:, 384:], 0.0).reshape(ff)
    sum_y = jnp.sum(grad_y.astype(F32), (0, 1))
    pieces = [leaf.reshape(devices, -1) for leaf in (sum_gain, sum_shift, sum_triple, sum_expand, sum_y)]
    terms = scatter_small(jnp.concatenate(pieces, 1), devices)
    terms = fence(terms, h_sum)
    small_all = small_sum(terms, devices)
    small_grads = []
    begin = 0
    for piece in pieces:
        small_grads.append(small_all[begin : begin + piece.shape[1]])
        begin += piece.shape[1]
    small_gain, small_shift, small_triple, small_expand, small_out = small_grads

    source = inputs[:, 0].astype(F32)
    out_away = swap(out_sum[1].astype(BF), "core").astype(F32)
    mixed = jnp.where(core == 0, jnp.stack([out_sum[0], out_away]), jnp.stack([out_away, out_sum[0]]))
    output = (valid * (source + mixed + dense_b + shrink_b)).astype(BF).reshape(inputs.shape)

    h_away = swap(h_sum[1].astype(BF), "core").astype(F32)
    grad_h = jnp.where(core == 0, jnp.stack([h_sum[0], h_away]), jnp.stack([h_away, h_sum[0]]))
    centred = source - jnp.mean(source, -1, keepdims=True)
    scale = lax.rsqrt(jnp.mean(centred * centred, -1, keepdims=True) + EPS)
    normed = centred * scale
    g = grad_h * gain
    grad_source = scale * (
        g - jnp.mean(g, -1, keepdims=True) - normed * jnp.mean(g * normed, -1, keepdims=True)
    )
    grad_inputs = (grad_y.astype(F32) + grad_source).astype(BF).reshape(inputs.shape)
    return (
        output,
        grad_inputs,
        small_gain,
        small_shift,
        grad_triple,
        small_triple,
        grad_dense,
        small_out,
        grad_expand,
        small_expand,
        grad_shrink,
        small_out,
    )


def solution(mesh):
    head, blk = mesh.devices.shape
    split = Mesh(mesh.devices.reshape(head // 2, 2, blk // (2 * Z_LEN), Z_LEN, 2), ALL)
    tokens = P(None, ("bs", "bz", "by"), ("hx", "core"), None)
    vector = P(ALL)
    matrix = P(ALL, None)
    return jax.shard_map(
        body,
        mesh=split,
        in_specs=(
            tokens,
            vector,
            vector,
            matrix,
            vector,
            matrix,
            vector,
            matrix,
            vector,
            matrix,
            vector,
            P(),
            P(),
            tokens,
        ),
        out_specs=(
            tokens,
            tokens,
            vector,
            vector,
            matrix,
            vector,
            matrix,
            vector,
            matrix,
            vector,
            matrix,
            vector,
        ),
        check_vma=False,
    )
```

```python
import functools

import jax
import jax.numpy as jnp
from jax import lax
from jax.experimental import pallas as pl
from jax.experimental.pallas import tpu as pltpu
from jax.sharding import Mesh
from jax.sharding import PartitionSpec as P

HEADS = 32
HEAD_DIM = 64
ROT = 32
EPS = 1e-05
NEG = -1e30
BF = jnp.bfloat16
F32 = jnp.float32

RANK = ("core", "bz", "by")
ALL = ("hx", "core", "bs", "bz", "by")
Z_LEN = 4
SWAP = [(0, 1), (1, 0)]
UP = [(i, (i + 1) % Z_LEN) for i in range(Z_LEN)]
DOWN = [((i + 1) % Z_LEN, i) for i in range(Z_LEN)]
VMEM_LIMIT = 60 * 1024 * 1024


def around(far):
    return [(i, (i + far) % Z_LEN) for i in range(Z_LEN)]


def swap(value, axis):
    return lax.ppermute(value, axis, SWAP)


def dot_rows(left, right):
    return lax.dot_general(left, right, (((1,), (1,)), ((), ())), preferred_element_type=F32)


def dot_cols(left, right):
    return lax.dot_general(left, right, (((0,), (0,)), ((), ())), preferred_element_type=F32)


def dot(left, right):
    return jnp.dot(left, right, preferred_element_type=F32)


def fence(now, *then):
    return lax.optimization_barrier((tuple(now),) + then)[0]


def ring(value):
    return lax.ppermute(value, "bz", UP)


def flatten(steps):
    return [piece for step in steps for piece in step]


def like(steps, refs):
    refs = list(refs)
    return [[refs.pop(0) for _ in step] for step in steps]


def add_low(left, right):
    return (left.astype(F32) + right.astype(F32)).astype(BF)


def ring_back(total):
    return lax.ppermute(total.astype(BF), "bz", DOWN)


def joined(index, own, other):
    return jnp.where(index == 0, jnp.concatenate([own, other], 0), jnp.concatenate([other, own], 0))


def across(value, far):
    return lax.ppermute(value, "bz", [(i, i ^ far) for i in range(Z_LEN)])


def in_all(value, spread):
    value = value.reshape(1, Z_LEN, 2, 2, 2, -1)
    if spread > 1:
        value = lax.all_gather(value, "bs", axis=0, tiled=True)
    return value.transpose(2, 3, 0, 1, 4, 5).reshape(8 * Z_LEN * spread, -1)


def halved(value, name, axis):
    index = lax.axis_index(name)
    return (
        lax.dynamic_index_in_dim(value, index, axis, keepdims=False),
        lax.dynamic_index_in_dim(value, 1 - index, axis, keepdims=False),
    )


def turn(value, cosine, sine, lane):
    near = jnp.where(
        (lane % HEAD_DIM) < ROT // 2,
        pltpu.roll(value, 128 - ROT // 2, 1),
        pltpu.roll(value, ROT // 2, 1),
    )
    return value * cosine + near * sine


def take_rows(rows_ref, steps, begin):
    for at, pieces in enumerate(steps):

        @pl.when(pl.program_id(0) == begin + at)
        def _(pieces=pieces):
            row = 0
            for piece in pieces:
                rows_ref[row : row + piece.shape[0]] = piece[...]
                row += piece.shape[0]


def by_row(block, lanes, begin=0):
    return pl.BlockSpec((block, lanes), lambda i, *_: (i + begin, 0))


def fixed(*values):
    def spec(value):
        rank = len(value.shape)
        return pl.BlockSpec(value.shape, lambda i, *_: (0,) * rank)

    return [spec(value) for value in values]


def halves(hx, width):
    half = width // 2
    return [pl.ds(pl.multiple_of(at * half, half), half) for at in (hx, 1 - hx)]


def dot_halves(left_ref, hx, own_ref, other_ref):
    own, other = halves(hx, left_ref.shape[1])
    return dot(left_ref[:, own], own_ref[...]) + dot(left_ref[:, other], other_ref[...])


def front_kernel(steps, plane_ref, *refs):
    count = len(flatten(steps))
    pieces, refs = like(steps, refs[:count]), refs[count:]
    gain_ref, shift_ref, own_ref, other_ref, bias_ref, cos_ref, sin_ref = refs[:7]
    h_ref, q_ref, kv_ref, pre_ref, out_ref, mean_ref, scale_ref, x_ref = refs[-8:]
    take_rows(x_ref, pieces, 0)
    x = x_ref[...].astype(F32)
    mean = jnp.mean(x, -1, keepdims=True)
    centred = x - mean
    scale = lax.rsqrt(jnp.mean(centred * centred, -1, keepdims=True) + EPS)
    mean_ref[...] = mean
    scale_ref[...] = scale
    h_ref[...] = (centred * scale * gain_ref[...] + shift_ref[...]).astype(BF)
    linear = dot_halves(h_ref, plane_ref[0], own_ref, other_ref) + bias_ref[...]
    lane = lax.broadcasted_iota(jnp.int32, (x.shape[0], 128), 1)
    cosine, sine = cos_ref[...], sin_ref[...]
    q_ref[...] = turn(linear[:, :128], cosine, sine, lane).astype(BF) * BF(HEAD_DIM**-0.5)
    kv_ref[:, :128] = turn(linear[:, 128:256], cosine, sine, lane).astype(BF)
    kv_ref[:, 128:] = linear[:, 256:384].astype(BF)
    pre = linear[:, 384:]
    pre_ref[...] = pre
    out_ref[...] = (0.5 * pre * (1.0 + jnp.tanh(0.7978845608 * (pre + 0.044715 * pre * pre * pre)))).astype(BF)


def front(plane, pieces, held, gain, shift, own, other, bias, cosine, sine):
    block, width = sum(piece.shape[0] for piece in pieces[0]), gain.shape[1]
    rows = 8 * block
    cols = own.shape[1]
    wide = cols - 384
    flat_pieces = flatten(pieces)
    here = functools.partial(by_row, block, begin=4 if held else 0)
    lanes = (width, 128, 256, wide, wide, 1, 1)
    types = (BF, BF, BF, F32, BF, F32, F32)
    return pl.pallas_call(
        functools.partial(front_kernel, pieces),
        grid_spec=pltpu.PrefetchScalarGridSpec(
            num_scalar_prefetch=1,
            grid=(4,),
            in_specs=fixed(*flat_pieces, gain, shift, own, other, bias)
            + [here(128), here(128)]
            + [pl.BlockSpec(memory_space=pl.ANY)] * len(held),
            out_specs=[here(n) for n in lanes],
            scratch_shapes=[pltpu.VMEM((block, width), BF)],
        ),
        out_shape=[jax.ShapeDtypeStruct((rows, n), kind) for n, kind in zip(lanes, types)],
        input_output_aliases={len(flat_pieces) + 8 + i: i for i in range(len(held))},
        compiler_params=pltpu.CompilerParams(vmem_limit_bytes=VMEM_LIMIT),
        cost_estimate=pl.CostEstimate(
            flops=rows * width * cols + 6 * rows * width, bytes_accessed=rows * width * 3, transcendentals=rows * wide
        ),
    )(plane[None], *flat_pieces, gain, shift, own, other, bias, cosine, sine, *held)


def two_heads(value):
    lane = lax.broadcasted_iota(jnp.int32, value.shape, 1)
    zero = jnp.zeros_like(value)
    return jnp.concatenate([jnp.where(lane < HEAD_DIM, value, zero), jnp.where(lane < HEAD_DIM, zero, value)], 0)


def one_row(value):
    half = value.shape[0] // 2
    lane = lax.broadcasted_iota(jnp.int32, (half, 128), 1)
    return jnp.where(lane < HEAD_DIM, value[:half], value[half:])


def place_in(row, share):
    return ((row & share) << 1) | ((row & (2 * share)) >> 1) | (row & (share - 1))


def allowed_pairs(meta_ref, block, query_at, key_at):
    turned, length = meta_ref[0], meta_ref[1]
    shape = (block, 2 * block)
    row = lax.broadcasted_iota(jnp.int32, shape, 1) & (block - 1)
    query = query_at * block + (place_in(row, block // 4) ^ turned)
    key = key_at * block + (place_in(lax.broadcasted_iota(jnp.int32, shape, 0), block // 4) ^ turned)
    return (key <= query) & (key < length)


def key_ranges(meta_ref, block, query_at):
    length = meta_ref[1]
    plain = jnp.minimum(query_at, length // block)
    last = jnp.minimum(query_at + 1, (length + block - 1) // block)
    return plain, last


def spot_of(at):
    near = 2 * Z_LEN
    spot = lax.rem(at, near)
    return lax.div(at, near) * 2 + lax.div(spot, 4), slice(None), lax.rem(spot, 2), lax.rem(lax.div(spot, 2), 2)


def rows_of(ref, at):
    value = ref[spot_of(at)]
    return value.reshape(value.shape[0] * value.shape[1], value.shape[2])


def add_rows(ref, at, value):
    ref[spot_of(at)] += value.reshape(2, value.shape[0] // 2, value.shape[1])


def flat(ref):
    value = ref[0, :, 0, 0]
    return value.reshape(value.shape[0] * value.shape[1], value.shape[2])


def key_rows(kv_ref, order_ref, at, count):
    return jnp.concatenate([rows_of(kv_ref, order_ref[at + i]) for i in range(count)], 0)


def over_keys(meta_ref, block, query_at, step, state):
    plain, last = key_ranges(meta_ref, block, query_at)
    pairs = plain // 2
    state = lax.fori_loop(0, pairs, lambda i, carried: step(False, 2, 2 * i, carried), state)
    state = lax.fori_loop(2 * pairs, plain, functools.partial(step, False, 1), state)
    return lax.fori_loop(plain, last, functools.partial(step, True, 1), state)


def attend_kernel(block, meta_ref, query_ref, order_ref, q_ref, kv_ref, full_ref, low_ref, lse_ref):
    query_at = query_ref[pl.program_id(0)]
    queries = two_heads(flat(q_ref))

    def step(masked, count, at, state):
        top, total, mixed = state
        both = key_rows(kv_ref, order_ref, at, count)
        scores = dot_rows(both[:, :128], queries)
        if masked:
            allowed = allowed_pairs(meta_ref, block, query_at, at)
            scores = jnp.where(allowed, scores, NEG)
        fresh = jnp.maximum(top, jnp.max(scores, 0, keepdims=True))
        factor = jnp.exp(top - fresh)
        weights = jnp.exp(scores - fresh)
        if masked:
            weights = jnp.where(allowed, weights, 0.0)
        total = total * factor + jnp.sum(weights, 0, keepdims=True)
        return fresh, total, mixed * factor + dot_cols(both[:, 128:], weights.astype(BF))

    state = (
        jnp.full((1, 2 * block), NEG, F32),
        jnp.zeros((1, 2 * block), F32),
        jnp.zeros((128, 2 * block), F32),
    )
    top, total, mixed = over_keys(meta_ref, block, query_at, step, state)
    mixed = mixed / total
    full = jnp.concatenate([mixed[:HEAD_DIM, :block], mixed[HEAD_DIM:, block:]], 0).T
    shape = full_ref.shape[1:2] + full_ref.shape[4:]
    full_ref[0, :, 0, 0] = full.reshape(shape)
    low_ref[0, :, 0, 0] = full.astype(BF).reshape(shape)
    lse_ref[...] = jnp.broadcast_to((top + jnp.log(total))[None], lse_ref.shape)


def placed(share, lanes):
    return pl.BlockSpec((1, 2, 1, 1, 2 * share, lanes), lambda i, *_: (i // 4, 0, i % 2, (i // 2) % 2, 0, 0))


def attend(table, q, kv, share):
    block = 4 * share
    blocks = 2 * Z_LEN
    rows, keys = q.shape[0], kv.shape[0]
    shape = (2, 2, 2, Z_LEN // 2, 2 * share, 128)
    kv_shape = (keys // (4 * Z_LEN * share), 2, 2, Z_LEN // 2, 2 * share, 256)
    full, low, lse = pl.pallas_call(
        functools.partial(attend_kernel, block),
        grid_spec=pltpu.PrefetchScalarGridSpec(
            num_scalar_prefetch=3,
            grid=(blocks,),
            in_specs=[placed(share, 128), pl.BlockSpec(kv_shape, lambda i, *_: (0, 0, 0, 0, 0, 0))],
            out_specs=[placed(share, 128), placed(share, 128), pl.BlockSpec((1, 8, 2 * block), lambda i, *_: (i, 0, 0))],
        ),
        out_shape=[
            jax.ShapeDtypeStruct(shape, F32),
            jax.ShapeDtypeStruct(shape, BF),
            jax.ShapeDtypeStruct((blocks, 8, 2 * block), F32),
        ],
        compiler_params=pltpu.CompilerParams(vmem_limit_bytes=VMEM_LIMIT),
        cost_estimate=pl.CostEstimate(
            flops=16 * rows * keys * 128, bytes_accessed=rows * 128 * 16, transcendentals=rows * keys
        ),
    )(*table, q.reshape(shape), kv.reshape(kv_shape))
    return full, low.reshape(rows, 128), lse


def attend_back_kernel(blocks, block, meta_ref, query_ref, order_ref, q_ref, kv_ref, full_ref, lse_ref, grad_ref, dq_ref, dkv_ref, dk_acc, dv_acc):
    at_block = pl.program_id(0)
    query_at = query_ref[at_block]
    queries = two_heads(flat(q_ref))
    grads = two_heads(flat(grad_ref))
    full = flat(full_ref)
    delta = jnp.sum(grads.astype(F32) * jnp.concatenate([full, full], 0), -1, keepdims=True)
    delta = jnp.broadcast_to(delta, (2 * block, 128)).T[:1]
    lse = lse_ref[0, :1]

    @pl.when(at_block == 0)
    def _():
        dk_acc[...] = jnp.zeros_like(dk_acc)
        dv_acc[...] = jnp.zeros_like(dv_acc)

    def step(masked, count, at, grad_query):
        both = key_rows(kv_ref, order_ref, at, count)
        keys = both[:, :128]
        scores = dot_rows(keys, queries)
        if masked:
            allowed = allowed_pairs(meta_ref, block, query_at, at)
            scores = jnp.where(allowed, scores, NEG)
        weights = jnp.exp(scores - lse)
        if masked:
            weights = jnp.where(allowed, weights, 0.0)
        grad_scores = (weights * (dot_rows(both[:, 128:], grads) - delta)).astype(BF)
        grad_keys = dot(grad_scores, queries)
        grad_values = dot(weights.astype(BF), grads)
        for i in range(count):
            spot = order_ref[at + i]
            add_rows(dk_acc, spot, grad_keys[i * block : (i + 1) * block])
            add_rows(dv_acc, spot, grad_values[i * block : (i + 1) * block])
        return grad_query + dot_cols(grad_scores, keys)

    grad_query = over_keys(meta_ref, block, query_at, step, jnp.zeros((2 * block, 128), F32))
    shape = dq_ref.shape[1:2] + dq_ref.shape[4:]
    dq_ref[0, :, 0, 0] = (one_row(grad_query) * HEAD_DIM**-0.5).astype(BF).reshape(shape)

    @pl.when(at_block == blocks - 1)
    def _():
        dkv_ref[..., :128] = dk_acc[...].astype(BF)
        dkv_ref[..., 128:] = dv_acc[...].astype(BF)


def attend_back(table, q, kv, full, lse, grad, share):
    block = 4 * share
    blocks = 2 * Z_LEN
    rows, keys = q.shape[0], kv.shape[0]
    shape = (2, 2, 2, Z_LEN // 2, 2 * share, 128)
    kv_shape = (keys // (4 * Z_LEN * share), 2, 2, Z_LEN // 2, 2 * share, 256)
    kv_spec = pl.BlockSpec(kv_shape, lambda i, *_: (0, 0, 0, 0, 0, 0))
    dq, dkv = pl.pallas_call(
        functools.partial(attend_back_kernel, blocks, block),
        grid_spec=pltpu.PrefetchScalarGridSpec(
            num_scalar_prefetch=3,
            grid=(blocks,),
            in_specs=[
                placed(share, 128),
                kv_spec,
                placed(share, 128),
                pl.BlockSpec((1, 8, 2 * block), lambda i, *_: (i, 0, 0)),
                placed(share, 128),
            ],
            out_specs=[placed(share, 128), kv_spec],
            scratch_shapes=[pltpu.VMEM(kv_shape[:-1] + (128,), F32), pltpu.VMEM(kv_shape[:-1] + (128,), F32)],
        ),
        out_shape=[jax.ShapeDtypeStruct(shape, BF), jax.ShapeDtypeStruct(kv_shape, BF)],
        compiler_params=pltpu.CompilerParams(vmem_limit_bytes=VMEM_LIMIT),
        cost_estimate=pl.CostEstimate(
            flops=40 * rows * keys * 128, bytes_accessed=rows * 128 * 24, transcendentals=rows * keys
        ),
    )(*table, q.reshape(shape), kv.reshape(kv_shape), full, lse, grad.reshape(shape))
    return dq.reshape(rows, 128), dkv.reshape(keys, 256)


def store_parts(parts, total_ref):
    rows = total_ref.shape[0]
    for at in range(8):
        half, core, ky = at // 4, at // 2 % 2, at % 2

        @pl.when(pl.program_id(0) == at)
        def _(ref=parts[2 - 2 * core + 1 - ky], half=half):
            ref[half * rows : (half + 1) * rows] = total_ref[...]


def part_shapes(rows, width):
    return [jax.ShapeDtypeStruct((2 * rows, width), BF)] * 4


def out_kernel(plane_ref, attn_ref, units_ref, dense_ref, own_ref, other_ref, *refs):
    parts, total_ref = refs[:-1], refs[-1]
    attn, units = attn_ref[...], units_ref[...]
    for part, weight_ref in zip(halves(plane_ref[0], total_ref.shape[1]), (own_ref, other_ref)):
        total_ref[:, part] = (dot(attn, dense_ref[:, part]) + dot_rows(units, weight_ref[...])).astype(BF)
    store_parts(parts, total_ref)


def out_partial(plane, attn, units, dense, own, other, block):
    rows, width = attn.shape[0], dense.shape[1]
    wide = units.shape[1]
    shapes = part_shapes(block, width)
    return pl.pallas_call(
        out_kernel,
        grid_spec=pltpu.PrefetchScalarGridSpec(
            num_scalar_prefetch=1,
            grid=(rows // block,),
            in_specs=[by_row(block, 128), by_row(block, wide)] + fixed(dense, own, other),
            out_specs=fixed(*shapes),
            scratch_shapes=[pltpu.VMEM((block, width), BF)],
        ),
        out_shape=shapes,
        compiler_params=pltpu.CompilerParams(vmem_limit_bytes=VMEM_LIMIT),
        cost_estimate=pl.CostEstimate(
            flops=2 * rows * width * (128 + wide), bytes_accessed=2 * rows * width, transcendentals=0
        ),
    )(plane[None], attn, units, dense, own, other)


def branch_kernel(steps, plane_ref, *refs):
    count = len(flatten(steps))
    pieces, refs = like(steps, refs[:count]), refs[count:]
    dense_ref, own_ref, other_ref, pre_ref, attn_ref, grad_ref, g_ref = refs
    take_rows(g_ref, pieces, 0)
    attn_ref[...] = dot_rows(g_ref[...], dense_ref[...]).astype(BF)
    grad = dot_halves(g_ref, plane_ref[0], own_ref, other_ref)
    u = pre_ref[...]
    square = u * u
    bend = jnp.tanh(0.7978845608 * u * (1.0 + 0.044715 * square))
    slope = 0.5 * (1.0 + bend) + 0.5 * u * (1.0 - bend * bend) * (0.7978845608 * (1.0 + 3 * 0.044715 * square))
    grad_ref[...] = (grad * slope).astype(BF)


def branch_grads(plane, pieces, dense, own, other, pre, block):
    width = dense.shape[1]
    rows, wide = pre.shape
    flat_pieces = flatten(pieces)
    return pl.pallas_call(
        functools.partial(branch_kernel, pieces),
        grid_spec=pltpu.PrefetchScalarGridSpec(
            num_scalar_prefetch=1,
            grid=(rows // block,),
            in_specs=fixed(*flat_pieces, dense, own, other) + [by_row(block, wide)],
            out_specs=[by_row(block, 128), by_row(block, wide), by_row(block, width)],
        ),
        out_shape=[
            jax.ShapeDtypeStruct((rows, 128), BF),
            jax.ShapeDtypeStruct((rows, wide), BF),
            jax.ShapeDtypeStruct((rows, width), BF),
        ],
        compiler_params=pltpu.CompilerParams(vmem_limit_bytes=VMEM_LIMIT),
        cost_estimate=pl.CostEstimate(
            flops=2 * rows * width * (128 + wide), bytes_accessed=rows * width * 4, transcendentals=rows * wide
        ),
    )(plane[None], *flat_pieces, dense, own, other, pre)


def turn_back(value, cosine, sine, lane):
    return turn(value.astype(F32), cosine, -sine, lane).astype(BF)


def back_kernel(steps, plane_ref, *refs):
    count = len(flatten(steps))
    pieces, refs = like(steps, refs[:count]), refs[count:]
    linear_ref, units_ref, own_ref, other_ref, mean_ref, scale_ref = refs[:6]
    parts, (gain_ref, shift_ref, small_ref, x_ref, total_ref) = refs[6:10], refs[10:]
    take_rows(x_ref, pieces, 0)
    linear, units = linear_ref[...], units_ref[...]

    @pl.when(pl.program_id(0) == 0)
    def _():
        gain_ref[...] = jnp.zeros_like(gain_ref)
        shift_ref[...] = jnp.zeros_like(shift_ref)
        small_ref[...] = jnp.zeros_like(small_ref)

    small_ref[:, :384] += jnp.sum(linear.astype(F32), 0, keepdims=True)
    small_ref[:, 384:] += jnp.sum(units.astype(F32), 0, keepdims=True)
    mean, scale = mean_ref[...], scale_ref[...]
    for part, weight_ref in zip(halves(plane_ref[0], total_ref.shape[1]), (own_ref, other_ref)):
        total = dot_rows(linear, weight_ref[:, :384]) + dot_rows(units, weight_ref[:, 384:])
        total_ref[:, part] = total.astype(BF)
        gain_ref[:, part] += jnp.sum(total * ((x_ref[:, part].astype(F32) - mean) * scale), 0, keepdims=True)
        shift_ref[:, part] += jnp.sum(total, 0, keepdims=True)
    store_parts(parts, total_ref)


def back_partial(plane, pieces, linear, units, own, other, mean, scale):
    rows = linear.shape[0]
    block = sum(piece.shape[0] for piece in pieces[0])
    width, cols = 2 * own.shape[0], own.shape[1]
    flat_pieces = flatten(pieces)
    shapes = part_shapes(block, width)
    sums = [jax.ShapeDtypeStruct((1, n), F32) for n in (width, width, cols)]
    *parts, gain, shift, small = pl.pallas_call(
        functools.partial(back_kernel, pieces),
        grid_spec=pltpu.PrefetchScalarGridSpec(
            num_scalar_prefetch=1,
            grid=(rows // block,),
            in_specs=fixed(*flat_pieces)
            + [by_row(block, 384), by_row(block, cols - 384)]
            + fixed(own, other)
            + [by_row(block, 1), by_row(block, 1)],
            out_specs=fixed(*shapes) + fixed(*sums),
            scratch_shapes=[pltpu.VMEM((block, width), BF), pltpu.VMEM((block, width), BF)],
        ),
        out_shape=shapes + sums,
        compiler_params=pltpu.CompilerParams(vmem_limit_bytes=VMEM_LIMIT),
        cost_estimate=pl.CostEstimate(
            flops=2 * rows * width * cols, bytes_accessed=4 * rows * width, transcendentals=0
        ),
    )(plane[None], *flat_pieces, linear, units, own, other, mean, scale)
    return parts, (gain, shift, small)


def weight_kernel(plane_ref, *refs):
    *pairs, away_ref, mine_ref = refs
    for out_ref, this in ((away_ref, pl.program_id(0) < 2), (mine_ref, pl.program_id(0) >= 2)):

        @pl.when(this)
        def _(out_ref=out_ref):
            begin = 0
            for left, right in zip(pairs[::2], pairs[1::2]):
                end = begin + right.shape[1]
                out_ref[:, begin:end] = dot_cols(left[...], right[...]).astype(BF)
                begin = end


def weight_rows(rows, quarter):
    return pl.BlockSpec((rows, quarter), lambda i, p: (0, ((p[0] + 1 - i // 2) % 2) * 2 + i % 2))


def weight_outs(quarter, cols):
    return [
        pl.BlockSpec((quarter, cols), lambda i, p: (jnp.minimum(i, 1), 0)),
        pl.BlockSpec((quarter, cols), lambda i, p: (jnp.maximum(i - 2, 0), 0)),
    ]


def weight_grads(plane, *pairs):
    rows, width = pairs[0][0].shape
    cols = sum(right.shape[1] for _, right in pairs)
    quarter = width // 4
    out = jax.ShapeDtypeStruct((2 * quarter, cols), BF)
    specs = [spec for _, right in pairs for spec in (weight_rows(rows, quarter), *fixed(right))]
    return pl.pallas_call(
        weight_kernel,
        grid_spec=pltpu.PrefetchScalarGridSpec(
            num_scalar_prefetch=1,
            grid=(4,),
            in_specs=specs,
            out_specs=weight_outs(quarter, cols),
        ),
        out_shape=[out, out],
        compiler_params=pltpu.CompilerParams(vmem_limit_bytes=VMEM_LIMIT),
        cost_estimate=pl.CostEstimate(
            flops=2 * rows * width * cols, bytes_accessed=2 * rows * width, transcendentals=0
        ),
    )(plane[None], *[value for pair in pairs for value in pair])


def triple_grads_kernel(plane_ref, h_ref, dq_ref, dkv_ref, cos_ref, sin_ref, away_ref, mine_ref, linear_ref):
    @pl.when(pl.program_id(0) == 0)
    def _():
        rows = 256

        def step(at, carry):
            here = pl.ds(pl.multiple_of(at * rows, rows), rows)
            lane = lax.broadcasted_iota(jnp.int32, (rows, 128), 1)
            cosine, sine = cos_ref[here, :], sin_ref[here, :]
            linear_ref[here, :128] = turn_back(dq_ref[here, :], cosine, sine, lane)
            linear_ref[here, 128:256] = turn_back(dkv_ref[here, :128], cosine, sine, lane)
            linear_ref[here, 256:] = dkv_ref[here, 128:]
            return carry

        lax.fori_loop(0, dq_ref.shape[0] // rows, step, 0)

    weight_kernel(plane_ref, h_ref, linear_ref, away_ref, mine_ref)


def triple_grads(plane, h, dq, dkv, cosine, sine):
    rows, width = h.shape
    quarter = width // 4
    out = jax.ShapeDtypeStruct((2 * quarter, 384), BF)
    linear = jax.ShapeDtypeStruct((rows, 384), BF)
    return pl.pallas_call(
        triple_grads_kernel,
        grid_spec=pltpu.PrefetchScalarGridSpec(
            num_scalar_prefetch=1,
            grid=(4,),
            in_specs=[weight_rows(rows, quarter)] + fixed(dq, dkv, cosine, sine),
            out_specs=weight_outs(quarter, 384) + fixed(linear),
        ),
        out_shape=[out, out, linear],
        compiler_params=pltpu.CompilerParams(vmem_limit_bytes=VMEM_LIMIT),
        cost_estimate=pl.CostEstimate(
            flops=2 * rows * width * 384, bytes_accessed=2 * rows * width, transcendentals=0
        ),
    )(plane[None], h, dq, dkv, cosine, sine)


def pack_kernel(triple_ref, expand_ref, shrink_ref, in_ref, out_ref):
    ranks, wide = in_ref.shape[0], out_ref.shape[2]
    for rank in range(ranks):
        for s in range(3):
            pair = [triple_ref[:, pl.ds((s * HEADS + x * ranks + rank) * HEAD_DIM, HEAD_DIM)] for x in range(2)]
            in_ref[rank, :, s * 128 : (s + 1) * 128] = jnp.concatenate(pair, 1)
        in_ref[rank, :, 384:] = expand_ref[:, rank * wide : (rank + 1) * wide]
        out_ref[rank] = shrink_ref[:, rank * wide : (rank + 1) * wide]


def pack(triple, expand, shrink, ranks):
    held = triple.shape[0]
    wide = expand.shape[1] // ranks
    return pl.pallas_call(
        pack_kernel,
        out_shape=[
            jax.ShapeDtypeStruct((ranks, held, 384 + wide), BF),
            jax.ShapeDtypeStruct((ranks, held, wide), BF),
        ],
        compiler_params=pltpu.CompilerParams(vmem_limit_bytes=VMEM_LIMIT),
    )(triple, expand, shrink)


def unpack_triple_kernel(back_ref, triple_ref):
    ranks = back_ref.shape[0]
    for rank in range(0, ranks, 2):
        for s in range(3):
            for x in range(2):
                lanes = slice(s * 128 + x * HEAD_DIM, s * 128 + (x + 1) * HEAD_DIM)
                pair = jnp.concatenate([back_ref[rank, :, lanes], back_ref[rank + 1, :, lanes]], 1)
                at = (s * HEADS + x * ranks + rank) * HEAD_DIM
                triple_ref[:, at : at + 128] = pair.astype(F32)


def unpack_triple(back):
    held = back.shape[1]
    return pl.pallas_call(
        unpack_triple_kernel,
        out_shape=jax.ShapeDtypeStruct((held, 3 * HEADS * HEAD_DIM), F32),
        compiler_params=pltpu.CompilerParams(vmem_limit_bytes=VMEM_LIMIT),
    )(back)


def unpack_units_kernel(back_ref, shrink_ref, expand_ref):
    wide = back_ref.shape[2] // 2
    for rank in range(back_ref.shape[0]):
        shrink_ref[:, rank * wide : (rank + 1) * wide] = back_ref[rank, :, :wide].astype(F32)
        expand_ref[:, rank * wide : (rank + 1) * wide] = back_ref[rank, :, wide:].astype(F32)


def unpack_units(back):
    ranks, held, cols = back.shape
    out = jax.ShapeDtypeStruct((held, ranks * cols // 2), F32)
    return pl.pallas_call(
        unpack_units_kernel,
        out_shape=[out, out],
        compiler_params=pltpu.CompilerParams(vmem_limit_bytes=VMEM_LIMIT),
    )(back)


def turn_tables(positions):
    half = ROT // 2
    inverse = 10000.0 ** (-(jnp.arange(half, dtype=F32) * 2.0) / ROT)
    angles = positions.astype(F32)[:, None] * inverse[None, :]
    cosine, sine = jnp.cos(angles), jnp.sin(angles)
    rest = (positions.shape[0], HEAD_DIM - ROT)
    cosine = jnp.concatenate([cosine, cosine, jnp.ones(rest, F32)], 1)
    sine = jnp.concatenate([-sine, sine, jnp.zeros(rest, F32)], 1)
    return jnp.tile(cosine, (1, 2)), jnp.tile(sine, (1, 2))


def core_pair(own, other, core):
    return jnp.where(core == 0, jnp.stack([own, other], 1), jnp.stack([other, own], 1))


def body(
    inputs,
    norm_gain,
    norm_bias,
    triple_weight,
    triple_bias,
    dense_weight,
    dense_bias,
    expand_weight,
    expand_bias,
    shrink_weight,
    shrink_bias,
    lengths,
    block_order,
    cotangent,
):
    share, width = inputs.shape[2], inputs.shape[3]
    hx, core, bs, bz, by = (lax.axis_index(name) for name in ALL)
    spread = lax.axis_size("bs")
    ranks = 2 * Z_LEN * 2
    devices = 2 * ranks * spread
    block = 4 * share
    rows = ranks * 2 * share
    near_blocks = Z_LEN * 2
    blocks = block_order.shape[0]
    held = width // devices
    ff = expand_weight.shape[1]
    ff_here = ff // ranks
    length = lengths[hx]

    def block_at(index):
        return jnp.sum(jnp.where(jnp.arange(blocks, dtype=jnp.int32) == index, block_order, 0))

    token_pos = (
        block_at(bs * near_blocks + bz * 2 + by) * block
        + (hx * 2 + core) * share
        + jnp.arange(share, dtype=jnp.int32)
    )
    valid = (token_pos[None, :] < lengths[:, None]).astype(F32)[:, :, None]

    spots = jnp.arange(blocks, dtype=jnp.int32)
    within = spots % near_blocks
    index = spots - within + ((bz + Z_LEN - within // 2) % Z_LEN) * 2 + (by + within) % 2
    key_at = jnp.sum(jnp.where(index[:, None] == spots[None, :], block_order[None, :], 0), 1)
    query_at = lax.dynamic_slice_in_dim(key_at, bs * near_blocks, near_blocks)
    turned = hx * 2 * share + core * share
    inside = place_in(jnp.arange(block, dtype=jnp.int32), share) ^ turned
    block_pos = query_at.reshape(2, Z_LEN // 2, 2).transpose(0, 2, 1)[:, None, :, :, None]
    row_pos = (block_pos * block + inside.reshape(1, 2, 1, 1, 2 * share)).reshape(rows)
    order = jnp.sum(jnp.where(key_at[None, :] == spots[:, None], spots[None, :], 0), 1)
    table = jnp.where(jnp.arange(2) == 0, turned, length).astype(jnp.int32), query_at, order
    cosine, sine = turn_tables(row_pos)

    def to_cols(sent):
        cols = sent.shape[2]
        got = lax.all_to_all(sent, RANK, split_axis=0, concat_axis=0, tiled=True)
        if spread > 1:
            got = lax.all_gather(got.reshape(2, 1, near_blocks, held, cols), "bs", axis=1, tiled=True)
        return got.reshape(width // 2, cols)

    def to_rows(mine):
        cols = mine.shape[-1]
        if spread > 1:
            mine = mine.reshape(2, spread, near_blocks, held, cols)
            mine = lax.psum_scatter(mine, "bs", scatter_dimension=1, tiled=True)
        return lax.all_to_all(mine.reshape(ranks, held, cols), RANK, split_axis=0, concat_axis=0, tiled=True)

    def both(low, high):
        return jnp.concatenate([low, high], 0)

    x_a = lax.dynamic_index_in_dim(inputs[:, 0], hx, 0, keepdims=False)
    x_b = swap(lax.dynamic_index_in_dim(inputs[:, 0], 1 - hx, 0, keepdims=False), "hx")
    vectors = (norm_gain, norm_bias, triple_bias, expand_bias, dense_bias, shrink_bias)
    sent_in, sent_out = pack(triple_weight, expand_weight, shrink_weight, ranks)
    small = jnp.concatenate(vectors)[None]

    x_b, small, cotangent, sent_in, sent_out = fence((x_b, small, cotangent, sent_in, sent_out))
    in_own = to_cols(sent_in)
    x_0 = both(x_a, x_b)
    grad_y = (cotangent[:, 0].astype(F32) * valid).astype(BF)
    g_a = lax.dynamic_index_in_dim(grad_y, hx, 0, keepdims=False)
    g_b = swap(lax.dynamic_index_in_dim(grad_y, 1 - hx, 0, keepdims=False), "hx")
    small = joined(by, small, swap(small, "by"))
    small = joined(core, small, swap(small, "core"))
    more = swap(small, "hx")
    cosine, sine = turn_tables(row_pos)

    x_0, in_own, g_b, small, more, cosine, sine = fence((x_0, in_own, g_b, small, more, cosine, sine), table)
    in_other = swap(in_own, "hx")
    y_0 = swap(x_0, "by")
    x_1 = ring(x_0)
    g_0 = both(g_a, g_b)
    small = joined(hx, small, more)
    more = across(small, 1)

    y_0, x_1, g_0, small, more = fence((y_0, x_1, g_0, small, more))
    y_1 = swap(x_1, "by")
    x_2 = ring(x_1)
    small = joined(bz % 2, small, more)
    more = across(small, 2)

    y_1, x_2, small, more = fence((y_1, x_2, small, more))
    y_2 = swap(x_2, "by")
    x_3 = ring(x_2)
    own_one, y_one = both(x_0, x_1), both(y_0, y_1)
    c_one = swap(own_one, "core"), swap(y_one, "core")
    small = in_all(joined(bz // 2, small, more), spread)

    cuts = [0]
    for leaf in (norm_gain, norm_bias, triple_bias, expand_bias, dense_bias, shrink_bias):
        cuts.append(cuts[-1] + leaf.shape[0])
    gain, shift, triple_b, expand_b, dense_b, shrink_b = (
        small[:, low:high].reshape(-1).astype(F32) for low, high in zip(cuts[:-1], cuts[1:])
    )
    rank = core * near_blocks + bz * 2 + by
    bias_triple = lax.dynamic_index_in_dim(
        triple_b.reshape(3, 2, ranks, HEAD_DIM).transpose(2, 0, 1, 3).reshape(ranks, 384), rank, 0
    )
    bias_expand = lax.dynamic_index_in_dim(expand_b.reshape(ranks, ff_here), rank, 0)
    bias_in = jnp.concatenate([bias_triple, bias_expand], 1)

    y_2, x_3, c_one, in_other, bias_in = fence((y_2, x_3, c_one, in_other, bias_in))
    y_3 = swap(x_3, "by")
    g_1 = ring(g_0)
    own_two = both(x_2, x_3)
    c_two = (swap(own_two, "core"),)
    x_one = ((own_one,), (y_one,), (c_one[0],), (c_one[1],))
    into = (gain[None], shift[None], in_own, in_other, bias_in, cosine, sine)
    held_one = front(hx, x_one, (), *into)

    held_one, y_3, g_1, c_two, sent_out = fence((held_one, y_3, g_1, c_two, sent_out))
    y_two = both(y_2, y_3)
    out_own = to_cols(sent_out)
    c_two = c_two[0], swap(y_two, "core")

    held_one, c_two = fence((held_one, c_two))
    x_two = ((own_two,), (y_two,), (c_two[0],), (c_two[1],))
    h, q, kv, pre, expand_out, mean, scale = front(hx, x_two, held_one, *into)

    q, g_0, g_1, out_own = fence((q, g_0, g_1, out_own))
    out_other = swap(out_own, "hx")
    own_one = both(g_0, g_1)
    y_one = swap(own_one, "by")
    g_2 = ring(g_1)
    g_3 = lax.ppermute(g_0, "bz", around(3))
    kv_all = kv if spread == 1 else lax.all_gather(kv, "bs", axis=0, tiled=True)
    attn_full, attn_low, lse = attend(table, q, kv_all, share)
    if spread == 1:
        dense_away = swap(dense_weight, "hx")
        dense_pair = jnp.where(hx == 0, both(dense_weight, dense_away), both(dense_away, dense_weight))
    else:
        dense_all = lax.all_gather(dense_weight, ALL, axis=0, tiled=True).reshape(2, ranks, HEAD_DIM, width)
        dense_pair = lax.dynamic_index_in_dim(dense_all, rank, 1, keepdims=False).reshape(128, width)

    attn_low, y_one, g_2, g_3, own_one, out_other, dense_pair = fence(
        (attn_low, y_one, g_2, g_3, own_one, out_other, dense_pair)
    )
    own_two = both(g_2, g_3)
    y_two = swap(own_two, "by")
    c_one = swap(own_one, "core"), swap(y_one, "core")
    c_two = (swap(own_two, "core"),)
    onto = (dense_pair, out_own, out_other)
    out_parts = out_partial(hx, attn_low, expand_out, *onto, block)

    y_two, c_one, c_two, out_parts = fence((y_two, c_one, c_two, out_parts))
    g_one = own_one, y_one
    c_two = c_two[0], swap(y_two, "core")
    g_pieces = tuple((piece,) for piece in g_one + c_one + (own_two, y_two) + c_two)

    out_parts, g_pieces = fence((out_parts, g_pieces))
    got_far, got_near = swap(out_parts[0], "core"), swap(out_parts[1], "core")
    grad_attention, grad_pre, g_all = branch_grads(hx, g_pieces, *onto, pre, block)

    grad_attention, grad_pre, g_all, got_far, got_near = fence((grad_attention, grad_pre, g_all, got_far, got_near))
    far = add_low(out_parts[2], got_far)

    grad_attention, grad_pre, g_all, far = fence((grad_attention, grad_pre, g_all, far))
    out_y = swap(far, "by")
    units_away, units_mine = weight_grads(hx, (g_all, expand_out), (h, grad_pre))

    grad_attention, units_away = fence((grad_attention, units_away))
    units_away = swap(units_away, "hx")
    dq, dkv = attend_back(table, q, kv_all, attn_full, lse, grad_attention, share)
    if spread > 1:
        dkv = lax.psum_scatter(dkv, "bs", scatter_dimension=0, tiled=True)

    def three(at, near_part, got, y_part):
        rows = slice(at * 2 * share, (at + 1) * 2 * share)
        return near_part[rows].astype(F32) + got[rows].astype(F32) + y_part[rows].astype(F32)

    dq, out_y, stay_near, got_near = fence((dq, out_y, out_parts[3], got_near))
    out_sum = three(3, stay_near, got_near, out_y)

    dq, out_sum = fence((dq, out_sum))
    ringed = ring_back(out_sum)
    triple_away, triple_mine, grad_linear = triple_grads(hx, h, dq, dkv, cosine, sine)

    units_away, triple_away, grad_linear, ringed = fence((units_away, triple_away, grad_linear, ringed))
    mine = add_low(units_mine, units_away)

    mine, triple_away, grad_linear = fence((mine, triple_away, grad_linear))
    units_rows = to_rows(mine)
    triple_away = swap(triple_away, "hx")
    h_parts, sums = back_partial(hx, x_one + x_two, grad_linear, grad_pre, in_own, in_other, mean, scale)

    sum_gain, sum_shift, sum_in = sums
    here = jnp.arange(ranks, dtype=jnp.int32)[:, None] == rank
    sum_triple = (
        jnp.where(here, sum_in[:, :384], 0.0)
        .reshape(ranks, 3, 2, HEAD_DIM)
        .transpose(1, 2, 0, 3)
        .reshape(3 * width)
    )
    sum_expand = jnp.where(here, sum_in[:, 384:], 0.0).reshape(ff)
    sum_y = jnp.sum(grad_y.astype(F32), (0, 1))
    pieces = [leaf.reshape(devices, -1) for leaf in (sum_gain, sum_shift, sum_triple, sum_expand, sum_y)]
    small = jnp.concatenate(pieces, 1).reshape(2, 2, spread, Z_LEN, 2, -1)

    grad_dense_here = dot_cols(g_all, attn_low)

    h_parts, small, units_rows, triple_away, ringed = fence(
        (h_parts, small, units_rows, triple_away, ringed), grad_dense_here
    )
    h_got_far, h_got_near = swap(h_parts[0], "core"), swap(h_parts[1], "core")
    small, away = halved(small, "core", 1)

    h_got_far, h_got_near, small, away = fence((h_got_far, h_got_near, small, away))
    one, two = slice(0, block), slice(block, 2 * block)
    far_two, far_one = add_low(h_parts[2][two], h_got_far[two]), add_low(h_parts[2][one], h_got_far[one])

    far_one, far_two, small, away = fence((far_one, far_two, small, away))
    h_y_two = swap(far_two, "by")
    away = swap(away, "core")
    mine = add_low(triple_mine, triple_away)
    out_ringed = ring_back(three(2, stay_near, got_near, out_y) + ringed)
    grad_shrink, grad_expand = unpack_units(units_rows)

    h_y_two, far_one, small, away, mine, out_ringed = fence(
        (h_y_two, far_one, small, away, mine, out_ringed), grad_shrink
    )
    h_sum = three(1, h_parts[3][two], h_got_near[two], h_y_two)
    small, away = halved(small + away, "hx", 0)

    h_sum, far_one, small, away, mine = fence((h_sum, far_one, small, away, mine))
    h_y_one = swap(far_one, "by")
    ringed = ring_back(h_sum)
    triple_rows = to_rows(mine)
    away = swap(away, "hx")
    out_sum = three(1, stay_near, got_near, out_y) + out_ringed

    h_y_one, ringed, small, away, out_sum, triple_rows = fence((h_y_one, ringed, small, away, out_sum, triple_rows))
    h_sum = three(0, h_parts[3][two], h_got_near[two], h_y_two) + ringed
    small, away = halved(small + away, "by", 2)

    h_sum, small, away, out_sum = fence((h_sum, small, away, out_sum))
    ringed = ring_back(h_sum)
    away = swap(away, "by")
    h_last = [three(at, h_parts[3][one], h_got_near[one], h_y_one) for at in (0, 1)]
    grad_triple = unpack_triple(triple_rows)

    ringed, small, away, h_last, out_sum = fence((ringed, small, away, h_last, out_sum), grad_triple)
    h_sum = h_last[1] + ringed
    small = small + away

    h_sum, small, out_sum = fence((h_sum, small, out_sum))
    ringed = ring_back(h_sum)
    out_ringed = ring_back(out_sum)
    terms = [lax.dynamic_index_in_dim(small, (bz + kz) % Z_LEN, 1, keepdims=False) for kz in range(Z_LEN)]
    terms = terms[:1] + [lax.ppermute(terms[kz], "bz", around(kz)) for kz in range(1, Z_LEN)]

    ringed, out_ringed, terms = fence((ringed, out_ringed, terms))
    h_sum = (h_last[0] + ringed).reshape(2, share, width)
    out_sum = (three(0, stay_near, got_near, out_y) + out_ringed).reshape(2, share, width)

    dense_grads = grad_dense_here.T.reshape(2, HEAD_DIM, width)
    if spread == 1:
        dense_mine = lax.dynamic_index_in_dim(dense_grads, hx, 0, keepdims=False)
        dense_away = lax.dynamic_index_in_dim(dense_grads, 1 - hx, 0, keepdims=False)
        grad_dense = dense_mine + swap(dense_away.astype(BF), "hx").astype(F32)
    else:
        spot = jnp.arange(ranks, dtype=jnp.int32)[None, :, None, None] == rank
        dense_whole = jnp.where(spot, dense_grads[:, None], 0.0).reshape(width, width)
        grad_dense = lax.psum_scatter(dense_whole, ALL, scatter_dimension=0, tiled=True)

    small = sum(terms)
    if spread > 1:
        small = lax.psum_scatter(small, "bs", scatter_dimension=0, tiled=True)
    small = small.reshape(-1)
    small_grads = []
    begin = 0
    for piece in pieces:
        small_grads.append(small[begin : begin + piece.shape[1]])
        begin += piece.shape[1]
    small_gain, small_shift, small_triple, small_expand, small_out = small_grads

    source = inputs[:, 0].astype(F32)
    out_away = swap(out_sum[1].astype(BF), "hx").astype(F32)
    mixed = jnp.where(hx == 0, jnp.stack([out_sum[0], out_away]), jnp.stack([out_away, out_sum[0]]))
    output = (valid * (source + mixed + dense_b + shrink_b)).astype(BF).reshape(inputs.shape)

    h_away = swap(h_sum[1].astype(BF), "hx").astype(F32)
    grad_h = jnp.where(hx == 0, jnp.stack([h_sum[0], h_away]), jnp.stack([h_away, h_sum[0]]))
    centred = source - jnp.mean(source, -1, keepdims=True)
    scale = lax.rsqrt(jnp.mean(centred * centred, -1, keepdims=True) + EPS)
    normed = centred * scale
    g = grad_h * gain
    grad_source = scale * (
        g - jnp.mean(g, -1, keepdims=True) - normed * jnp.mean(g * normed, -1, keepdims=True)
    )
    grad_inputs = (grad_y.astype(F32) + grad_source).astype(BF).reshape(inputs.shape)
    return (
        output,
        grad_inputs,
        small_gain,
        small_shift,
        grad_triple,
        small_triple,
        grad_dense,
        small_out,
        grad_expand,
        small_expand,
        grad_shrink,
        small_out,
    )


def solution(mesh):
    head, blk = mesh.devices.shape
    split = Mesh(mesh.devices.reshape(head // 2, 2, blk // (2 * Z_LEN), Z_LEN, 2), ALL)
    tokens = P(None, ("bs", "bz", "by"), ("hx", "core"), None)
    vector = P(ALL)
    matrix = P(ALL, None)
    return jax.shard_map(
        body,
        mesh=split,
        in_specs=(
            tokens,
            vector,
            vector,
            matrix,
            vector,
            matrix,
            vector,
            matrix,
            vector,
            matrix,
            vector,
            P(),
            P(),
            tokens,
        ),
        out_specs=(
            tokens,
            tokens,
            vector,
            vector,
            matrix,
            vector,
            matrix,
            vector,
            matrix,
            vector,
            matrix,
            vector,
        ),
        check_vma=False,
    )
```

```python
import functools

import jax
import jax.numpy as jnp
from jax import lax
from jax.experimental import pallas as pl
from jax.experimental.pallas import tpu as pltpu
from jax.sharding import Mesh
from jax.sharding import PartitionSpec as P

HEADS = 32
HEAD_DIM = 64
ROT = 32
EPS = 1e-05
NEG = -1e30
BF = jnp.bfloat16
F32 = jnp.float32

RANK = ("core", "bz", "by")
ALL = ("hx", "core", "bs", "bz", "by")
Z_LEN = 4
SWAP = [(0, 1), (1, 0)]
UP = [(i, (i + 1) % Z_LEN) for i in range(Z_LEN)]
DOWN = [((i + 1) % Z_LEN, i) for i in range(Z_LEN)]
VMEM_LIMIT = 60 * 1024 * 1024


def around(far):
    return [(i, (i + far) % Z_LEN) for i in range(Z_LEN)]


def swap(value, axis):
    return lax.ppermute(value, axis, SWAP)


def dot_rows(left, right):
    return lax.dot_general(left, right, (((1,), (1,)), ((), ())), preferred_element_type=F32)


def dot_cols(left, right):
    return lax.dot_general(left, right, (((0,), (0,)), ((), ())), preferred_element_type=F32)


def dot(left, right):
    return jnp.dot(left, right, preferred_element_type=F32)


def fence(now, *then):
    return lax.optimization_barrier((tuple(now),) + then)[0]


def ring(value):
    return lax.ppermute(value, "bz", UP)


def flatten(steps):
    return [piece for step in steps for piece in step]


def like(steps, refs):
    refs = list(refs)
    return [[refs.pop(0) for _ in step] for step in steps]


def add_low(left, right):
    return (left.astype(F32) + right.astype(F32)).astype(BF)


def ring_back(total):
    return lax.ppermute(total.astype(BF), "bz", DOWN)


def joined(index, own, other):
    return jnp.where(index == 0, jnp.concatenate([own, other], 0), jnp.concatenate([other, own], 0))


def across(value, far):
    return lax.ppermute(value, "bz", [(i, i ^ far) for i in range(Z_LEN)])


def in_all(value, spread):
    value = value.reshape(1, Z_LEN, 2, 2, 2, -1)
    if spread > 1:
        value = lax.all_gather(value, "bs", axis=0, tiled=True)
    return value.transpose(2, 3, 0, 1, 4, 5).reshape(8 * Z_LEN * spread, -1)


def halved(value, name, axis):
    index = lax.axis_index(name)
    return (
        lax.dynamic_index_in_dim(value, index, axis, keepdims=False),
        lax.dynamic_index_in_dim(value, 1 - index, axis, keepdims=False),
    )


def turn(value, cosine, sine, lane):
    near = jnp.where(
        (lane % HEAD_DIM) < ROT // 2,
        pltpu.roll(value, 128 - ROT // 2, 1),
        pltpu.roll(value, ROT // 2, 1),
    )
    return value * cosine + near * sine


def take_rows(rows_ref, steps, begin):
    for at, pieces in enumerate(steps):

        @pl.when(pl.program_id(0) == begin + at)
        def _(pieces=pieces):
            row = 0
            for piece in pieces:
                rows_ref[row : row + piece.shape[0]] = piece[...]
                row += piece.shape[0]


def by_row(block, lanes, begin=0):
    return pl.BlockSpec((block, lanes), lambda i, *_: (i + begin, 0))


def fixed(*values):
    def spec(value):
        rank = len(value.shape)
        return pl.BlockSpec(value.shape, lambda i, *_: (0,) * rank)

    return [spec(value) for value in values]


def halves(hx, width):
    half = width // 2
    return [pl.ds(pl.multiple_of(at * half, half), half) for at in (hx, 1 - hx)]


def dot_halves(left_ref, hx, own_ref, other_ref):
    own, other = halves(hx, left_ref.shape[1])
    return dot(left_ref[:, own], own_ref[...]) + dot(left_ref[:, other], other_ref[...])


def front_kernel(steps, plane_ref, *refs):
    count = len(flatten(steps))
    pieces, refs = like(steps, refs[:count]), refs[count:]
    gain_ref, shift_ref, own_ref, other_ref, bias_ref, cos_ref, sin_ref = refs[:7]
    h_ref, q_ref, kv_ref, pre_ref, out_ref, mean_ref, scale_ref, x_ref = refs[-8:]
    take_rows(x_ref, pieces, 0)
    x = x_ref[...].astype(F32)
    mean = jnp.mean(x, -1, keepdims=True)
    centred = x - mean
    scale = lax.rsqrt(jnp.mean(centred * centred, -1, keepdims=True) + EPS)
    mean_ref[...] = mean
    scale_ref[...] = scale
    h_ref[...] = (centred * scale * gain_ref[...] + shift_ref[...]).astype(BF)
    linear = dot_halves(h_ref, plane_ref[0], own_ref, other_ref) + bias_ref[...]
    lane = lax.broadcasted_iota(jnp.int32, (x.shape[0], 128), 1)
    cosine, sine = cos_ref[...], sin_ref[...]
    q_ref[...] = turn(linear[:, :128], cosine, sine, lane).astype(BF) * BF(HEAD_DIM**-0.5)
    kv_ref[:, :128] = turn(linear[:, 128:256], cosine, sine, lane).astype(BF)
    kv_ref[:, 128:] = linear[:, 256:384].astype(BF)
    pre = linear[:, 384:]
    pre_ref[...] = pre
    out_ref[...] = (0.5 * pre * (1.0 + jnp.tanh(0.7978845608 * (pre + 0.044715 * pre * pre * pre)))).astype(BF)


def front(plane, pieces, held, gain, shift, own, other, bias, cosine, sine):
    block, width = sum(piece.shape[0] for piece in pieces[0]), gain.shape[1]
    rows = 8 * block
    cols = own.shape[1]
    wide = cols - 384
    flat_pieces = flatten(pieces)
    here = functools.partial(by_row, block, begin=4 if held else 0)
    lanes = (width, 128, 256, wide, wide, 1, 1)
    types = (BF, BF, BF, F32, BF, F32, F32)
    return pl.pallas_call(
        functools.partial(front_kernel, pieces),
        grid_spec=pltpu.PrefetchScalarGridSpec(
            num_scalar_prefetch=1,
            grid=(4,),
            in_specs=fixed(*flat_pieces, gain, shift, own, other, bias)
            + [here(128), here(128)]
            + [pl.BlockSpec(memory_space=pl.ANY)] * len(held),
            out_specs=[here(n) for n in lanes],
            scratch_shapes=[pltpu.VMEM((block, width), BF)],
        ),
        out_shape=[jax.ShapeDtypeStruct((rows, n), kind) for n, kind in zip(lanes, types)],
        input_output_aliases={len(flat_pieces) + 8 + i: i for i in range(len(held))},
        compiler_params=pltpu.CompilerParams(vmem_limit_bytes=VMEM_LIMIT),
        cost_estimate=pl.CostEstimate(
            flops=rows * width * cols + 6 * rows * width, bytes_accessed=rows * width * 3, transcendentals=rows * wide
        ),
    )(plane[None], *flat_pieces, gain, shift, own, other, bias, cosine, sine, *held)


def two_heads(value):
    lane = lax.broadcasted_iota(jnp.int32, value.shape, 1)
    zero = jnp.zeros_like(value)
    return jnp.concatenate([jnp.where(lane < HEAD_DIM, value, zero), jnp.where(lane < HEAD_DIM, zero, value)], 0)


def one_row(value):
    half = value.shape[0] // 2
    lane = lax.broadcasted_iota(jnp.int32, (half, 128), 1)
    return jnp.where(lane < HEAD_DIM, value[:half], value[half:])


def place_in(row, share):
    return ((row & share) << 1) | ((row & (2 * share)) >> 1) | (row & (share - 1))


def allowed_pairs(meta_ref, block, query_at, key_at):
    turned, length = meta_ref[0], meta_ref[1]
    shape = (block, 2 * block)
    row = lax.broadcasted_iota(jnp.int32, shape, 1) & (block - 1)
    query = query_at * block + (place_in(row, block // 4) ^ turned)
    key = key_at * block + (place_in(lax.broadcasted_iota(jnp.int32, shape, 0), block // 4) ^ turned)
    return (key <= query) & (key < length)


def key_ranges(meta_ref, block, query_at):
    length = meta_ref[1]
    plain = jnp.minimum(query_at, length // block)
    last = jnp.minimum(query_at + 1, (length + block - 1) // block)
    return plain, last


def spot_of(at):
    near = 2 * Z_LEN
    spot = lax.rem(at, near)
    return lax.div(at, near) * 2 + lax.div(spot, 4), slice(None), lax.rem(spot, 2), lax.rem(lax.div(spot, 2), 2)


def rows_of(ref, at):
    value = ref[spot_of(at)]
    return value.reshape(value.shape[0] * value.shape[1], value.shape[2])


def add_rows(ref, at, value):
    ref[spot_of(at)] += value.reshape(2, value.shape[0] // 2, value.shape[1])


def flat(ref):
    value = ref[0, :, 0, 0]
    return value.reshape(value.shape[0] * value.shape[1], value.shape[2])


def key_rows(kv_ref, order_ref, at, count):
    return jnp.concatenate([rows_of(kv_ref, order_ref[at + i]) for i in range(count)], 0)


def over_keys(meta_ref, block, query_at, step, state):
    plain, last = key_ranges(meta_ref, block, query_at)
    pairs = plain // 2
    state = lax.fori_loop(0, pairs, lambda i, carried: step(False, 2, 2 * i, carried), state)
    state = lax.fori_loop(2 * pairs, plain, functools.partial(step, False, 1), state)
    return lax.fori_loop(plain, last, functools.partial(step, True, 1), state)


def attend_kernel(block, meta_ref, query_ref, order_ref, q_ref, kv_ref, full_ref, low_ref, lse_ref):
    query_at = query_ref[pl.program_id(0)]
    queries = two_heads(flat(q_ref))

    def step(masked, count, at, state):
        top, total, mixed = state
        both = key_rows(kv_ref, order_ref, at, count)
        scores = dot_rows(both[:, :128], queries)
        if masked:
            allowed = allowed_pairs(meta_ref, block, query_at, at)
            scores = jnp.where(allowed, scores, NEG)
        fresh = jnp.maximum(top, jnp.max(scores, 0, keepdims=True))
        factor = jnp.exp(top - fresh)
        weights = jnp.exp(scores - fresh)
        if masked:
            weights = jnp.where(allowed, weights, 0.0)
        total = total * factor + jnp.sum(weights, 0, keepdims=True)
        return fresh, total, mixed * factor + dot_cols(both[:, 128:], weights.astype(BF))

    state = (
        jnp.full((1, 2 * block), NEG, F32),
        jnp.zeros((1, 2 * block), F32),
        jnp.zeros((128, 2 * block), F32),
    )
    top, total, mixed = over_keys(meta_ref, block, query_at, step, state)
    mixed = mixed / total
    full = jnp.concatenate([mixed[:HEAD_DIM, :block], mixed[HEAD_DIM:, block:]], 0).T
    shape = full_ref.shape[1:2] + full_ref.shape[4:]
    full_ref[0, :, 0, 0] = full.reshape(shape)
    low_ref[0, :, 0, 0] = full.astype(BF).reshape(shape)
    lse_ref[...] = jnp.broadcast_to((top + jnp.log(total))[None], lse_ref.shape)


def placed(share, lanes):
    return pl.BlockSpec((1, 2, 1, 1, 2 * share, lanes), lambda i, *_: (i // 4, 0, i % 2, (i // 2) % 2, 0, 0))


def attend(table, q, kv, share):
    block = 4 * share
    blocks = 2 * Z_LEN
    rows, keys = q.shape[0], kv.shape[0]
    shape = (2, 2, 2, Z_LEN // 2, 2 * share, 128)
    kv_shape = (keys // (4 * Z_LEN * share), 2, 2, Z_LEN // 2, 2 * share, 256)
    full, low, lse = pl.pallas_call(
        functools.partial(attend_kernel, block),
        grid_spec=pltpu.PrefetchScalarGridSpec(
            num_scalar_prefetch=3,
            grid=(blocks,),
            in_specs=[placed(share, 128), pl.BlockSpec(kv_shape, lambda i, *_: (0, 0, 0, 0, 0, 0))],
            out_specs=[placed(share, 128), placed(share, 128), pl.BlockSpec((1, 8, 2 * block), lambda i, *_: (i, 0, 0))],
        ),
        out_shape=[
            jax.ShapeDtypeStruct(shape, F32),
            jax.ShapeDtypeStruct(shape, BF),
            jax.ShapeDtypeStruct((blocks, 8, 2 * block), F32),
        ],
        compiler_params=pltpu.CompilerParams(vmem_limit_bytes=VMEM_LIMIT),
        cost_estimate=pl.CostEstimate(
            flops=16 * rows * keys * 128, bytes_accessed=rows * 128 * 16, transcendentals=rows * keys
        ),
    )(*table, q.reshape(shape), kv.reshape(kv_shape))
    return full, low.reshape(rows, 128), lse


def attend_back_kernel(blocks, block, meta_ref, query_ref, order_ref, q_ref, kv_ref, full_ref, lse_ref, grad_ref, dq_ref, dkv_ref, dk_acc, dv_acc):
    at_block = pl.program_id(0)
    query_at = query_ref[at_block]
    queries = two_heads(flat(q_ref))
    grads = two_heads(flat(grad_ref))
    full = flat(full_ref)
    delta = jnp.sum(grads.astype(F32) * jnp.concatenate([full, full], 0), -1, keepdims=True)
    delta = jnp.broadcast_to(delta, (2 * block, 128)).T[:1]
    lse = lse_ref[0, :1]

    @pl.when(at_block == 0)
    def _():
        dk_acc[...] = jnp.zeros_like(dk_acc)
        dv_acc[...] = jnp.zeros_like(dv_acc)

    def step(masked, count, at, grad_query):
        both = key_rows(kv_ref, order_ref, at, count)
        keys = both[:, :128]
        scores = dot_rows(keys, queries)
        if masked:
            allowed = allowed_pairs(meta_ref, block, query_at, at)
            scores = jnp.where(allowed, scores, NEG)
        weights = jnp.exp(scores - lse)
        if masked:
            weights = jnp.where(allowed, weights, 0.0)
        grad_scores = (weights * (dot_rows(both[:, 128:], grads) - delta)).astype(BF)
        grad_keys = dot(grad_scores, queries)
        grad_values = dot(weights.astype(BF), grads)
        for i in range(count):
            spot = order_ref[at + i]
            add_rows(dk_acc, spot, grad_keys[i * block : (i + 1) * block])
            add_rows(dv_acc, spot, grad_values[i * block : (i + 1) * block])
        return grad_query + dot_cols(grad_scores, keys)

    grad_query = over_keys(meta_ref, block, query_at, step, jnp.zeros((2 * block, 128), F32))
    shape = dq_ref.shape[1:2] + dq_ref.shape[4:]
    dq_ref[0, :, 0, 0] = (one_row(grad_query) * HEAD_DIM**-0.5).astype(BF).reshape(shape)

    @pl.when(at_block == blocks - 1)
    def _():
        dkv_ref[..., :128] = dk_acc[...].astype(BF)
        dkv_ref[..., 128:] = dv_acc[...].astype(BF)


def attend_back(table, q, kv, full, lse, grad, share):
    block = 4 * share
    blocks = 2 * Z_LEN
    rows, keys = q.shape[0], kv.shape[0]
    shape = (2, 2, 2, Z_LEN // 2, 2 * share, 128)
    kv_shape = (keys // (4 * Z_LEN * share), 2, 2, Z_LEN // 2, 2 * share, 256)
    kv_spec = pl.BlockSpec(kv_shape, lambda i, *_: (0, 0, 0, 0, 0, 0))
    dq, dkv = pl.pallas_call(
        functools.partial(attend_back_kernel, blocks, block),
        grid_spec=pltpu.PrefetchScalarGridSpec(
            num_scalar_prefetch=3,
            grid=(blocks,),
            in_specs=[
                placed(share, 128),
                kv_spec,
                placed(share, 128),
                pl.BlockSpec((1, 8, 2 * block), lambda i, *_: (i, 0, 0)),
                placed(share, 128),
            ],
            out_specs=[placed(share, 128), kv_spec],
            scratch_shapes=[pltpu.VMEM(kv_shape[:-1] + (128,), F32), pltpu.VMEM(kv_shape[:-1] + (128,), F32)],
        ),
        out_shape=[jax.ShapeDtypeStruct(shape, BF), jax.ShapeDtypeStruct(kv_shape, BF)],
        compiler_params=pltpu.CompilerParams(vmem_limit_bytes=VMEM_LIMIT),
        cost_estimate=pl.CostEstimate(
            flops=40 * rows * keys * 128, bytes_accessed=rows * 128 * 24, transcendentals=rows * keys
        ),
    )(*table, q.reshape(shape), kv.reshape(kv_shape), full, lse, grad.reshape(shape))
    return dq.reshape(rows, 128), dkv.reshape(keys, 256)


def store_parts(parts, total_ref):
    for at in range(8):
        half, core, ky = at // 4, at // 2 % 2, at % 2

        @pl.when(pl.program_id(0) == at)
        def _(ref=parts[4 * (1 - core) + 2 * (1 - ky) + half]):
            ref[...] = total_ref[...]


def part_shapes(rows, width):
    return [jax.ShapeDtypeStruct((rows, width), BF)] * 8


def out_kernel(plane_ref, attn_ref, units_ref, dense_ref, own_ref, other_ref, *refs):
    parts, total_ref = refs[:-1], refs[-1]
    attn, units = attn_ref[...], units_ref[...]
    for part, weight_ref in zip(halves(plane_ref[0], total_ref.shape[1]), (own_ref, other_ref)):
        total_ref[:, part] = (dot(attn, dense_ref[:, part]) + dot_rows(units, weight_ref[...])).astype(BF)
    store_parts(parts, total_ref)


def out_partial(plane, attn, units, dense, own, other, block):
    rows, width = attn.shape[0], dense.shape[1]
    wide = units.shape[1]
    shapes = part_shapes(block, width)
    return pl.pallas_call(
        out_kernel,
        grid_spec=pltpu.PrefetchScalarGridSpec(
            num_scalar_prefetch=1,
            grid=(rows // block,),
            in_specs=[by_row(block, 128), by_row(block, wide)] + fixed(dense, own, other),
            out_specs=fixed(*shapes),
            scratch_shapes=[pltpu.VMEM((block, width), BF)],
        ),
        out_shape=shapes,
        compiler_params=pltpu.CompilerParams(vmem_limit_bytes=VMEM_LIMIT),
        cost_estimate=pl.CostEstimate(
            flops=2 * rows * width * (128 + wide), bytes_accessed=2 * rows * width, transcendentals=0
        ),
    )(plane[None], attn, units, dense, own, other)


def branch_kernel(steps, plane_ref, *refs):
    count = len(flatten(steps))
    pieces, refs = like(steps, refs[:count]), refs[count:]
    dense_ref, own_ref, other_ref, pre_ref, attn_ref, grad_ref, g_ref = refs
    take_rows(g_ref, pieces, 0)
    attn_ref[...] = dot_rows(g_ref[...], dense_ref[...]).astype(BF)
    grad = dot_halves(g_ref, plane_ref[0], own_ref, other_ref)
    u = pre_ref[...]
    square = u * u
    bend = jnp.tanh(0.7978845608 * u * (1.0 + 0.044715 * square))
    slope = 0.5 * (1.0 + bend) + 0.5 * u * (1.0 - bend * bend) * (0.7978845608 * (1.0 + 3 * 0.044715 * square))
    grad_ref[...] = (grad * slope).astype(BF)


def branch_grads(plane, pieces, dense, own, other, pre, block):
    width = dense.shape[1]
    rows, wide = pre.shape
    flat_pieces = flatten(pieces)
    return pl.pallas_call(
        functools.partial(branch_kernel, pieces),
        grid_spec=pltpu.PrefetchScalarGridSpec(
            num_scalar_prefetch=1,
            grid=(rows // block,),
            in_specs=fixed(*flat_pieces, dense, own, other) + [by_row(block, wide)],
            out_specs=[by_row(block, 128), by_row(block, wide), by_row(block, width)],
        ),
        out_shape=[
            jax.ShapeDtypeStruct((rows, 128), BF),
            jax.ShapeDtypeStruct((rows, wide), BF),
            jax.ShapeDtypeStruct((rows, width), BF),
        ],
        compiler_params=pltpu.CompilerParams(vmem_limit_bytes=VMEM_LIMIT),
        cost_estimate=pl.CostEstimate(
            flops=2 * rows * width * (128 + wide), bytes_accessed=rows * width * 4, transcendentals=rows * wide
        ),
    )(plane[None], *flat_pieces, dense, own, other, pre)


def turn_back(value, cosine, sine, lane):
    return turn(value.astype(F32), cosine, -sine, lane).astype(BF)


def back_kernel(steps, plane_ref, *refs):
    count = len(flatten(steps))
    pieces, refs = like(steps, refs[:count]), refs[count:]
    linear_ref, units_ref, own_ref, other_ref, mean_ref, scale_ref = refs[:6]
    parts, (gain_ref, shift_ref, small_ref, x_ref, total_ref) = refs[6:14], refs[14:]
    take_rows(x_ref, pieces, 0)
    linear, units = linear_ref[...], units_ref[...]

    @pl.when(pl.program_id(0) == 0)
    def _():
        gain_ref[...] = jnp.zeros_like(gain_ref)
        shift_ref[...] = jnp.zeros_like(shift_ref)
        small_ref[...] = jnp.zeros_like(small_ref)

    small_ref[:, :384] += jnp.sum(linear.astype(F32), 0, keepdims=True)
    small_ref[:, 384:] += jnp.sum(units.astype(F32), 0, keepdims=True)
    mean, scale = mean_ref[...], scale_ref[...]
    for part, weight_ref in zip(halves(plane_ref[0], total_ref.shape[1]), (own_ref, other_ref)):
        total = dot_rows(linear, weight_ref[:, :384]) + dot_rows(units, weight_ref[:, 384:])
        total_ref[:, part] = total.astype(BF)
        gain_ref[:, part] += jnp.sum(total * ((x_ref[:, part].astype(F32) - mean) * scale), 0, keepdims=True)
        shift_ref[:, part] += jnp.sum(total, 0, keepdims=True)
    store_parts(parts, total_ref)


def back_partial(plane, pieces, linear, units, own, other, mean, scale):
    rows = linear.shape[0]
    block = sum(piece.shape[0] for piece in pieces[0])
    width, cols = 2 * own.shape[0], own.shape[1]
    flat_pieces = flatten(pieces)
    shapes = part_shapes(block, width)
    sums = [jax.ShapeDtypeStruct((1, n), F32) for n in (width, width, cols)]
    *parts, gain, shift, small = pl.pallas_call(
        functools.partial(back_kernel, pieces),
        grid_spec=pltpu.PrefetchScalarGridSpec(
            num_scalar_prefetch=1,
            grid=(rows // block,),
            in_specs=fixed(*flat_pieces)
            + [by_row(block, 384), by_row(block, cols - 384)]
            + fixed(own, other)
            + [by_row(block, 1), by_row(block, 1)],
            out_specs=fixed(*shapes) + fixed(*sums),
            scratch_shapes=[pltpu.VMEM((block, width), BF), pltpu.VMEM((block, width), BF)],
        ),
        out_shape=shapes + sums,
        compiler_params=pltpu.CompilerParams(vmem_limit_bytes=VMEM_LIMIT),
        cost_estimate=pl.CostEstimate(
            flops=2 * rows * width * cols, bytes_accessed=4 * rows * width, transcendentals=0
        ),
    )(plane[None], *flat_pieces, linear, units, own, other, mean, scale)
    return parts, (gain, shift, small)


def weight_kernel(plane_ref, *refs):
    *pairs, away_ref, mine_ref = refs
    for out_ref, this in ((away_ref, pl.program_id(0) < 2), (mine_ref, pl.program_id(0) >= 2)):

        @pl.when(this)
        def _(out_ref=out_ref):
            begin = 0
            for left, right in zip(pairs[::2], pairs[1::2]):
                end = begin + right.shape[1]
                value = dot_cols(left[...], right[...]).astype(BF)
                out_ref[:, 0, :, begin:end] = value.reshape(out_ref.shape[0], out_ref.shape[2], end - begin)
                begin = end


def weight_rows(rows, quarter):
    return pl.BlockSpec((rows, quarter), lambda i, p: (0, ((p[0] + 1 - i // 2) % 2) * 2 + i % 2))


def weight_shape(quarter, cols):
    return jax.ShapeDtypeStruct((Z_LEN, 2, quarter // Z_LEN, cols), BF)


def weight_outs(quarter, cols):
    shape = (Z_LEN, 1, quarter // Z_LEN, cols)
    return [
        pl.BlockSpec(shape, lambda i, p: (0, jnp.minimum(i, 1), 0, 0)),
        pl.BlockSpec(shape, lambda i, p: (0, jnp.maximum(i - 2, 0), 0, 0)),
    ]


def weight_grads(plane, *pairs):
    rows, width = pairs[0][0].shape
    cols = sum(right.shape[1] for _, right in pairs)
    quarter = width // 4
    out = weight_shape(quarter, cols)
    specs = [spec for _, right in pairs for spec in (weight_rows(rows, quarter), *fixed(right))]
    return pl.pallas_call(
        weight_kernel,
        grid_spec=pltpu.PrefetchScalarGridSpec(
            num_scalar_prefetch=1,
            grid=(4,),
            in_specs=specs,
            out_specs=weight_outs(quarter, cols),
        ),
        out_shape=[out, out],
        compiler_params=pltpu.CompilerParams(vmem_limit_bytes=VMEM_LIMIT),
        cost_estimate=pl.CostEstimate(
            flops=2 * rows * width * cols, bytes_accessed=2 * rows * width, transcendentals=0
        ),
    )(plane[None], *[value for pair in pairs for value in pair])


def triple_grads_kernel(plane_ref, h_ref, dq_ref, dkv_ref, cos_ref, sin_ref, away_ref, mine_ref, linear_ref):
    @pl.when(pl.program_id(0) == 0)
    def _():
        rows = 256

        def step(at, carry):
            here = pl.ds(pl.multiple_of(at * rows, rows), rows)
            lane = lax.broadcasted_iota(jnp.int32, (rows, 128), 1)
            cosine, sine = cos_ref[here, :], sin_ref[here, :]
            linear_ref[here, :128] = turn_back(dq_ref[here, :], cosine, sine, lane)
            linear_ref[here, 128:256] = turn_back(dkv_ref[here, :128], cosine, sine, lane)
            linear_ref[here, 256:] = dkv_ref[here, 128:]
            return carry

        lax.fori_loop(0, dq_ref.shape[0] // rows, step, 0)

    weight_kernel(plane_ref, h_ref, linear_ref, away_ref, mine_ref)


def triple_grads(plane, h, dq, dkv, cosine, sine):
    rows, width = h.shape
    quarter = width // 4
    out = weight_shape(quarter, 384)
    linear = jax.ShapeDtypeStruct((rows, 384), BF)
    return pl.pallas_call(
        triple_grads_kernel,
        grid_spec=pltpu.PrefetchScalarGridSpec(
            num_scalar_prefetch=1,
            grid=(4,),
            in_specs=[weight_rows(rows, quarter)] + fixed(dq, dkv, cosine, sine),
            out_specs=weight_outs(quarter, 384) + fixed(linear),
        ),
        out_shape=[out, out, linear],
        compiler_params=pltpu.CompilerParams(vmem_limit_bytes=VMEM_LIMIT),
        cost_estimate=pl.CostEstimate(
            flops=2 * rows * width * 384, bytes_accessed=2 * rows * width, transcendentals=0
        ),
    )(plane[None], h, dq, dkv, cosine, sine)


def pack_kernel(triple_ref, expand_ref, shrink_ref, in_ref, out_ref):
    ranks, wide = in_ref.shape[0], out_ref.shape[2]
    for rank in range(ranks):
        for s in range(3):
            pair = [triple_ref[:, pl.ds((s * HEADS + x * ranks + rank) * HEAD_DIM, HEAD_DIM)] for x in range(2)]
            in_ref[rank, :, s * 128 : (s + 1) * 128] = jnp.concatenate(pair, 1)
        in_ref[rank, :, 384:] = expand_ref[:, rank * wide : (rank + 1) * wide]
        out_ref[rank] = shrink_ref[:, rank * wide : (rank + 1) * wide]


def pack(triple, expand, shrink, ranks):
    held = triple.shape[0]
    wide = expand.shape[1] // ranks
    return pl.pallas_call(
        pack_kernel,
        out_shape=[
            jax.ShapeDtypeStruct((ranks, held, 384 + wide), BF),
            jax.ShapeDtypeStruct((ranks, held, wide), BF),
        ],
        compiler_params=pltpu.CompilerParams(vmem_limit_bytes=VMEM_LIMIT),
    )(triple, expand, shrink)


def from_rank(rank):
    return rank // (2 * Z_LEN) * 2 + rank % 2, rank // 2 % Z_LEN


def unpack_kernel(back_ref, shrink_ref, expand_ref, triple_ref):
    ranks = back_ref.shape[0] * back_ref.shape[1]
    wide = (back_ref.shape[3] - 384) // 2
    for rank in range(ranks):
        for out_ref, begin in ((shrink_ref, 0), (expand_ref, wide)):
            value = back_ref[(*from_rank(rank), slice(None), slice(begin, begin + wide))]
            out_ref[:, rank * wide : (rank + 1) * wide] = value.astype(F32)
    for rank in range(0, ranks, 2):
        for s in range(3):
            for x in range(2):
                begin = 2 * wide + s * 128 + x * HEAD_DIM
                pair = jnp.concatenate(
                    [back_ref[(*from_rank(one), slice(None), slice(begin, begin + HEAD_DIM))] for one in (rank, rank + 1)],
                    1,
                )
                at = (s * HEADS + x * ranks + rank) * HEAD_DIM
                triple_ref[:, at : at + 128] = pair.astype(F32)


def unpack(back):
    four, along, held, cols = back.shape
    wide = jax.ShapeDtypeStruct((held, four * along * (cols - 384) // 2), F32)
    return pl.pallas_call(
        unpack_kernel,
        out_shape=[wide, wide, jax.ShapeDtypeStruct((held, 3 * HEADS * HEAD_DIM), F32)],
        compiler_params=pltpu.CompilerParams(vmem_limit_bytes=VMEM_LIMIT),
    )(back)


def turn_tables(positions):
    half = ROT // 2
    inverse = 10000.0 ** (-(jnp.arange(half, dtype=F32) * 2.0) / ROT)
    angles = positions.astype(F32)[:, None] * inverse[None, :]
    cosine, sine = jnp.cos(angles), jnp.sin(angles)
    rest = (positions.shape[0], HEAD_DIM - ROT)
    cosine = jnp.concatenate([cosine, cosine, jnp.ones(rest, F32)], 1)
    sine = jnp.concatenate([-sine, sine, jnp.zeros(rest, F32)], 1)
    return jnp.tile(cosine, (1, 2)), jnp.tile(sine, (1, 2))


def core_pair(own, other, core):
    return jnp.where(core == 0, jnp.stack([own, other], 1), jnp.stack([other, own], 1))


def body(
    inputs,
    norm_gain,
    norm_bias,
    triple_weight,
    triple_bias,
    dense_weight,
    dense_bias,
    expand_weight,
    expand_bias,
    shrink_weight,
    shrink_bias,
    lengths,
    block_order,
    cotangent,
):
    share, width = inputs.shape[2], inputs.shape[3]
    hx, core, bs, bz, by = (lax.axis_index(name) for name in ALL)
    spread = lax.axis_size("bs")
    ranks = 2 * Z_LEN * 2
    devices = 2 * ranks * spread
    block = 4 * share
    rows = ranks * 2 * share
    near_blocks = Z_LEN * 2
    blocks = block_order.shape[0]
    held = width // devices
    ff = expand_weight.shape[1]
    ff_here = ff // ranks
    length = lengths[hx]

    def block_at(index):
        return jnp.sum(jnp.where(jnp.arange(blocks, dtype=jnp.int32) == index, block_order, 0))

    token_pos = (
        block_at(bs * near_blocks + bz * 2 + by) * block
        + (hx * 2 + core) * share
        + jnp.arange(share, dtype=jnp.int32)
    )
    valid = (token_pos[None, :] < lengths[:, None]).astype(F32)[:, :, None]

    spots = jnp.arange(blocks, dtype=jnp.int32)
    within = spots % near_blocks
    index = spots - within + ((bz + Z_LEN - within // 2) % Z_LEN) * 2 + (by + within) % 2
    key_at = jnp.sum(jnp.where(index[:, None] == spots[None, :], block_order[None, :], 0), 1)
    query_at = lax.dynamic_slice_in_dim(key_at, bs * near_blocks, near_blocks)
    turned = hx * 2 * share + core * share
    inside = place_in(jnp.arange(block, dtype=jnp.int32), share) ^ turned
    block_pos = query_at.reshape(2, Z_LEN // 2, 2).transpose(0, 2, 1)[:, None, :, :, None]
    row_pos = (block_pos * block + inside.reshape(1, 2, 1, 1, 2 * share)).reshape(rows)
    order = jnp.sum(jnp.where(key_at[None, :] == spots[:, None], spots[None, :], 0), 1)
    table = jnp.where(jnp.arange(2) == 0, turned, length).astype(jnp.int32), query_at, order
    cosine, sine = turn_tables(row_pos)

    def to_cols(sent):
        cols = sent.shape[2]
        got = lax.all_to_all(sent, RANK, split_axis=0, concat_axis=0, tiled=True)
        if spread > 1:
            got = lax.all_gather(got.reshape(2, 1, near_blocks, held, cols), "bs", axis=1, tiled=True)
        return got.reshape(width // 2, cols)

    def to_rows_z(mine):
        cols = mine.shape[-1]
        got = lax.all_to_all(mine, "bz", split_axis=0, concat_axis=0, tiled=True)
        return got.reshape(Z_LEN, 2, 2, held, cols)

    def over_bs(mine):
        if spread == 1:
            return mine
        cols = mine.shape[-1]
        mine = mine.transpose(1, 0, 2, 3).reshape(2, spread, Z_LEN, 2 * held, cols)
        mine = lax.psum_scatter(mine, "bs", scatter_dimension=1, tiled=True)
        return mine.reshape(2, Z_LEN, 2 * held, cols).transpose(1, 0, 2, 3)

    def to_send(got):
        return got.transpose(1, 2, 0, 3, 4).reshape(4, Z_LEN, held, got.shape[-1])

    def to_rows_y(got):
        return lax.all_to_all(got, ("core", "by"), split_axis=0, concat_axis=0, tiled=True)

    def both(low, high):
        return jnp.concatenate([low, high], 0)

    x_a = lax.dynamic_index_in_dim(inputs[:, 0], hx, 0, keepdims=False)
    x_b = lax.dynamic_index_in_dim(inputs[:, 0], 1 - hx, 0, keepdims=False)
    vectors = (norm_gain, norm_bias, triple_bias, expand_bias, dense_bias, shrink_bias)
    sent_in, sent_out = pack(triple_weight, expand_weight, shrink_weight, ranks)

    sent_in, sent_out, vectors, cotangent, x_b = fence((sent_in, sent_out, vectors, cotangent, x_b))
    in_own = to_cols(sent_in)
    x_b = swap(x_b, "hx")
    small = jnp.concatenate(vectors)[None]
    x_0 = both(x_a, x_b)
    grad_y = (cotangent[:, 0].astype(F32) * valid).astype(BF)
    g_a = lax.dynamic_index_in_dim(grad_y, hx, 0, keepdims=False)
    g_b = swap(lax.dynamic_index_in_dim(grad_y, 1 - hx, 0, keepdims=False), "hx")
    small = joined(by, small, swap(small, "by"))
    small = joined(core, small, swap(small, "core"))
    more = swap(small, "hx")
    cosine, sine = turn_tables(row_pos)

    x_0, in_own, g_b, small, more, cosine, sine = fence((x_0, in_own, g_b, small, more, cosine, sine), table)
    in_other = swap(in_own, "hx")
    y_0 = swap(x_0, "by")
    x_1 = ring(x_0)
    g_0 = both(g_a, g_b)
    small = joined(hx, small, more)
    more = across(small, 1)

    y_0, x_1, g_0, small, more = fence((y_0, x_1, g_0, small, more))
    y_1 = swap(x_1, "by")
    x_2 = ring(x_1)
    small = joined(bz % 2, small, more)
    more = across(small, 2)

    y_1, x_2, small, more = fence((y_1, x_2, small, more))
    y_2 = swap(x_2, "by")
    x_3 = ring(x_2)
    own_one, y_one = both(x_0, x_1), both(y_0, y_1)
    c_one = swap(own_one, "core"), swap(y_one, "core")
    small = in_all(joined(bz // 2, small, more), spread)

    cuts = [0]
    for leaf in (norm_gain, norm_bias, triple_bias, expand_bias, dense_bias, shrink_bias):
        cuts.append(cuts[-1] + leaf.shape[0])
    gain, shift, triple_b, expand_b, dense_b, shrink_b = (
        small[:, low:high].reshape(-1).astype(F32) for low, high in zip(cuts[:-1], cuts[1:])
    )
    rank = core * near_blocks + bz * 2 + by
    bias_triple = lax.dynamic_index_in_dim(
        triple_b.reshape(3, 2, ranks, HEAD_DIM).transpose(2, 0, 1, 3).reshape(ranks, 384), rank, 0
    )
    bias_expand = lax.dynamic_index_in_dim(expand_b.reshape(ranks, ff_here), rank, 0)
    bias_in = jnp.concatenate([bias_triple, bias_expand], 1)

    y_2, x_3, c_one, in_other, bias_in = fence((y_2, x_3, c_one, in_other, bias_in))
    y_3 = swap(x_3, "by")
    g_1 = ring(g_0)
    own_two = both(x_2, x_3)
    c_two = (swap(own_two, "core"),)
    x_one = ((own_one,), (y_one,), (c_one[0],), (c_one[1],))
    into = (gain[None], shift[None], in_own, in_other, bias_in, cosine, sine)
    held_one = front(hx, x_one, (), *into)

    held_one, y_3, g_1, c_two, sent_out = fence((held_one, y_3, g_1, c_two, sent_out))
    y_two = both(y_2, y_3)
    out_own = to_cols(sent_out)
    c_two = c_two[0], swap(y_two, "core")

    held_one, c_two = fence((held_one, c_two))
    x_two = ((own_two,), (y_two,), (c_two[0],), (c_two[1],))
    h, q, kv, pre, expand_out, mean, scale = front(hx, x_two, held_one, *into)

    q, g_0, g_1, out_own = fence((q, g_0, g_1, out_own))
    out_other = swap(out_own, "hx")
    own_one = both(g_0, g_1)
    y_one = swap(own_one, "by")
    g_2 = ring(g_1)
    g_3 = lax.ppermute(g_0, "bz", around(3))
    kv_all = kv if spread == 1 else lax.all_gather(kv, "bs", axis=0, tiled=True)
    attn_full, attn_low, lse = attend(table, q, kv_all, share)
    if spread == 1:
        dense_away = swap(dense_weight, "hx")
        dense_pair = jnp.where(hx == 0, both(dense_weight, dense_away), both(dense_away, dense_weight))
    else:
        dense_all = lax.all_gather(dense_weight, ALL, axis=0, tiled=True).reshape(2, ranks, HEAD_DIM, width)
        dense_pair = lax.dynamic_index_in_dim(dense_all, rank, 1, keepdims=False).reshape(128, width)

    attn_low, y_one, g_2, g_3, own_one, out_other, dense_pair = fence(
        (attn_low, y_one, g_2, g_3, own_one, out_other, dense_pair)
    )
    own_two = both(g_2, g_3)
    y_two = swap(own_two, "by")
    c_one = swap(own_one, "core"), swap(y_one, "core")
    c_two = (swap(own_two, "core"),)
    onto = (dense_pair, out_own, out_other)
    out_parts = out_partial(hx, attn_low, expand_out, *onto, block)

    y_two, c_one, c_two, out_parts = fence((y_two, c_one, c_two, out_parts))
    g_one = own_one, y_one
    c_two = c_two[0], swap(y_two, "core")
    g_pieces = tuple((piece,) for piece in g_one + c_one + (own_two, y_two) + c_two)

    out_parts, g_pieces = fence((out_parts, g_pieces))
    got = [swap(part, "core") for part in out_parts[:4]]
    grad_attention, grad_pre, g_all = branch_grads(hx, g_pieces, *onto, pre, block)

    grad_attention, grad_pre, g_all, got = fence((grad_attention, grad_pre, g_all, got))
    far = add_low(both(*out_parts[4:6]), both(*got[:2]))

    grad_attention, grad_pre, g_all, far = fence((grad_attention, grad_pre, g_all, far))
    out_y = swap(far, "by")
    units_away, units_mine = weight_grads(hx, (g_all, expand_out), (h, grad_pre))

    grad_attention, units_away = fence((grad_attention, units_away))
    units_away = swap(units_away, "hx")
    dq, dkv = attend_back(table, q, kv_all, attn_full, lse, grad_attention, share)
    if spread > 1:
        dkv = lax.psum_scatter(dkv, "bs", scatter_dimension=0, tiled=True)

    def three(k, near_part, got_part, y_part):
        rows = slice(k * 2 * share, (k + 1) * 2 * share)
        return near_part[rows].astype(F32) + got_part[rows].astype(F32) + y_part[rows].astype(F32)

    def out_three(kz):
        half = kz // 2
        return three(kz % 2, out_parts[6 + half], got[2 + half], out_y[half * block : (half + 1) * block])

    dq, out_y, out_parts, got = fence((dq, out_y, out_parts, got))
    out_sum = out_three(3)

    dq, out_sum = fence((dq, out_sum))
    ringed = ring_back(out_sum)
    triple_away, triple_mine, grad_linear = triple_grads(hx, h, dq, dkv, cosine, sine)

    units_away, triple_away, grad_linear, ringed = fence((units_away, triple_away, grad_linear, ringed))
    mine = add_low(units_mine, units_away)

    mine, triple_away, grad_linear = fence((mine, triple_away, grad_linear))
    units_rows = to_rows_z(over_bs(mine))
    triple_away = swap(triple_away, "hx")
    h_parts, sums = back_partial(hx, x_one + x_two, grad_linear, grad_pre, in_own, in_other, mean, scale)

    h_parts, sums, triple_away, ringed, g_all = fence((h_parts, sums, triple_away, ringed, g_all))
    h_got = [swap(part, "core") for part in h_parts[:4]]
    mine = add_low(triple_mine, triple_away)
    grad_dense_here = dot_cols(g_all, attn_low)
    out_sum = out_three(2) + ringed

    sum_gain, sum_shift, sum_in = sums
    here = jnp.arange(ranks, dtype=jnp.int32)[:, None] == rank
    sum_triple = (
        jnp.where(here, sum_in[:, :384], 0.0)
        .reshape(ranks, 3, 2, HEAD_DIM)
        .transpose(1, 2, 0, 3)
        .reshape(3 * width)
    )
    sum_expand = jnp.where(here, sum_in[:, 384:], 0.0).reshape(ff)
    sum_y = jnp.sum(grad_y.astype(F32), (0, 1))
    pieces = [leaf.reshape(devices, -1) for leaf in (sum_gain, sum_shift, sum_triple, sum_expand, sum_y)]
    small = jnp.concatenate(pieces, 1).reshape(2, 2, spread, Z_LEN, 2, -1)


    h_got, units_rows, out_sum, small, mine = fence((h_got, units_rows, out_sum, small, mine), grad_dense_here)
    far_one, far_two = add_low(h_parts[4], h_got[0]), add_low(h_parts[5], h_got[1])

    far_one, far_two, out_sum, small, mine = fence((far_one, far_two, out_sum, small, mine))
    h_y_two = swap(far_two, "by")
    triple_rows = to_rows_z(over_bs(mine))
    ringed = ring_back(out_sum)
    small, away = halved(small, "core", 1)

    h_y_two, far_one, small, away, ringed, triple_rows = fence((h_y_two, far_one, small, away, ringed, triple_rows))
    h_sum = three(1, h_parts[7], h_got[3], h_y_two)
    out_sum = out_three(1) + ringed

    h_sum, far_one, small, away, out_sum = fence((h_sum, far_one, small, away, out_sum))
    h_y_one = swap(far_one, "by")
    ringed, out_ringed = ring_back(h_sum), ring_back(out_sum)
    away = swap(away, "core")
    all_rows = jnp.concatenate([to_send(units_rows), to_send(triple_rows)], 3)

    h_y_one, ringed, out_ringed, small, away, all_rows = fence((h_y_one, ringed, out_ringed, small, away, all_rows))
    h_sum = three(0, h_parts[7], h_got[3], h_y_two) + ringed
    out_sum = (out_three(0) + out_ringed).reshape(2, share, width)
    out_away = out_sum[1].astype(BF)
    small, away = halved(small + away, "hx", 0)

    h_sum, out_sum, out_away, small, away, all_rows = fence((h_sum, out_sum, out_away, small, away, all_rows))
    ringed = ring_back(h_sum)
    all_rows = to_rows_y(all_rows)
    out_away = swap(out_away, "hx")
    away = swap(away, "hx")
    h_last = [three(at, h_parts[6], h_got[2], h_y_one) for at in (0, 1)]

    ringed, out_away, small, away, h_last = fence((ringed, out_away, small, away, h_last))
    h_sum = h_last[1] + ringed
    small, away = halved(small + away, "by", 2)

    h_sum, small, away = fence((h_sum, small, away))
    ringed = ring_back(h_sum)
    small = small + swap(away, "by")
    terms = [lax.dynamic_index_in_dim(small, (bz + kz) % Z_LEN, 1, keepdims=False) for kz in range(Z_LEN)]
    terms = terms[:1] + [lax.ppermute(terms[kz], "bz", around(kz)) for kz in range(1, Z_LEN)]

    source = inputs[:, 0].astype(F32)
    out_away = out_away.astype(F32)
    mixed = jnp.where(hx == 0, jnp.stack([out_sum[0], out_away]), jnp.stack([out_away, out_sum[0]]))
    output = (valid * (source + mixed + dense_b + shrink_b)).astype(BF).reshape(inputs.shape)

    ringed, terms, output, all_rows = fence((ringed, terms, output, all_rows))
    grad_shrink, grad_expand, grad_triple = unpack(all_rows)
    h_sum = (h_last[0] + ringed).reshape(2, share, width)

    dense_grads = grad_dense_here.T.reshape(2, HEAD_DIM, width)
    if spread == 1:
        dense_mine = lax.dynamic_index_in_dim(dense_grads, hx, 0, keepdims=False)
        dense_away = lax.dynamic_index_in_dim(dense_grads, 1 - hx, 0, keepdims=False)
        grad_dense = dense_mine + swap(dense_away.astype(BF), "hx").astype(F32)
    else:
        spot = jnp.arange(ranks, dtype=jnp.int32)[None, :, None, None] == rank
        dense_whole = jnp.where(spot, dense_grads[:, None], 0.0).reshape(width, width)
        grad_dense = lax.psum_scatter(dense_whole, ALL, scatter_dimension=0, tiled=True)

    small = sum(terms)
    if spread > 1:
        small = lax.psum_scatter(small, "bs", scatter_dimension=0, tiled=True)
    small = small.reshape(-1)
    small_grads = []
    begin = 0
    for piece in pieces:
        small_grads.append(small[begin : begin + piece.shape[1]])
        begin += piece.shape[1]
    small_gain, small_shift, small_triple, small_expand, small_out = small_grads

    h_away = swap(h_sum[1].astype(BF), "hx").astype(F32)
    grad_h = jnp.where(hx == 0, jnp.stack([h_sum[0], h_away]), jnp.stack([h_away, h_sum[0]]))
    centred = source - jnp.mean(source, -1, keepdims=True)
    scale = lax.rsqrt(jnp.mean(centred * centred, -1, keepdims=True) + EPS)
    normed = centred * scale
    g = grad_h * gain
    grad_source = scale * (
        g - jnp.mean(g, -1, keepdims=True) - normed * jnp.mean(g * normed, -1, keepdims=True)
    )
    grad_inputs = (grad_y.astype(F32) + grad_source).astype(BF).reshape(inputs.shape)
    return (
        output,
        grad_inputs,
        small_gain,
        small_shift,
        grad_triple,
        small_triple,
        grad_dense,
        small_out,
        grad_expand,
        small_expand,
        grad_shrink,
        small_out,
    )


def solution(mesh):
    head, blk = mesh.devices.shape
    split = Mesh(mesh.devices.reshape(head // 2, 2, blk // (2 * Z_LEN), Z_LEN, 2), ALL)
    tokens = P(None, ("bs", "bz", "by"), ("hx", "core"), None)
    vector = P(ALL)
    matrix = P(ALL, None)
    return jax.shard_map(
        body,
        mesh=split,
        in_specs=(
            tokens,
            vector,
            vector,
            matrix,
            vector,
            matrix,
            vector,
            matrix,
            vector,
            matrix,
            vector,
            P(),
            P(),
            tokens,
        ),
        out_specs=(
            tokens,
            tokens,
            vector,
            vector,
            matrix,
            vector,
            matrix,
            vector,
            matrix,
            vector,
            matrix,
            vector,
        ),
        check_vma=False,
    )
```

```python
import functools

import jax
import jax.numpy as jnp
from jax import lax
from jax.experimental import pallas as pl
from jax.experimental.pallas import tpu as pltpu
from jax.sharding import Mesh
from jax.sharding import PartitionSpec as P

HEADS = 32
HEAD_DIM = 64
ROT = 32
EPS = 1e-05
NEG = -1e30
BF = jnp.bfloat16
F32 = jnp.float32

RANK = ("core", "bz", "by")
ALL = ("hx", "core", "bs", "bz", "by")
Z_LEN = 4
SWAP = [(0, 1), (1, 0)]
UP = [(i, (i + 1) % Z_LEN) for i in range(Z_LEN)]
DOWN = [((i + 1) % Z_LEN, i) for i in range(Z_LEN)]
VMEM_LIMIT = 60 * 1024 * 1024


def around(far):
    return [(i, (i + far) % Z_LEN) for i in range(Z_LEN)]


def swap(value, axis):
    return lax.ppermute(value, axis, SWAP)


def dot_rows(left, right):
    return lax.dot_general(left, right, (((1,), (1,)), ((), ())), preferred_element_type=F32)


def dot_cols(left, right):
    return lax.dot_general(left, right, (((0,), (0,)), ((), ())), preferred_element_type=F32)


def dot(left, right):
    return jnp.dot(left, right, preferred_element_type=F32)


def fence(now, *then):
    return lax.optimization_barrier((tuple(now),) + then)[0]


def ring(value):
    return lax.ppermute(value, "bz", UP)


def flatten(steps):
    return [piece for step in steps for piece in step]


def like(steps, refs):
    refs = list(refs)
    return [[refs.pop(0) for _ in step] for step in steps]


def add_low(left, right):
    return (left.astype(F32) + right.astype(F32)).astype(BF)


def ring_back(total):
    return lax.ppermute(total.astype(BF), "bz", DOWN)


def joined(index, own, other):
    return jnp.where(index == 0, jnp.concatenate([own, other], 0), jnp.concatenate([other, own], 0))


def across(value, far):
    return lax.ppermute(value, "bz", [(i, i ^ far) for i in range(Z_LEN)])


def in_all(value, spread):
    value = value.reshape(1, Z_LEN, 2, 2, 2, -1)
    if spread > 1:
        value = lax.all_gather(value, "bs", axis=0, tiled=True)
    return value.transpose(2, 3, 0, 1, 4, 5).reshape(8 * Z_LEN * spread, -1)


def halved(value, name, axis):
    index = lax.axis_index(name)
    return (
        lax.dynamic_index_in_dim(value, index, axis, keepdims=False),
        lax.dynamic_index_in_dim(value, 1 - index, axis, keepdims=False),
    )


def turn(value, cosine, sine, lane):
    near = jnp.where(
        (lane % HEAD_DIM) < ROT // 2,
        pltpu.roll(value, 128 - ROT // 2, 1),
        pltpu.roll(value, ROT // 2, 1),
    )
    return value * cosine + near * sine


def take_rows(rows_ref, steps, begin):
    for at, pieces in enumerate(steps):

        @pl.when(pl.program_id(0) == begin + at)
        def _(pieces=pieces):
            row = 0
            for piece in pieces:
                rows_ref[row : row + piece.shape[0]] = piece[...]
                row += piece.shape[0]


def by_row(block, lanes, begin=0):
    return pl.BlockSpec((block, lanes), lambda i, *_: (i + begin, 0))


def fixed(*values):
    def spec(value):
        rank = len(value.shape)
        return pl.BlockSpec(value.shape, lambda i, *_: (0,) * rank)

    return [spec(value) for value in values]


def halves(hx, width):
    half = width // 2
    return [pl.ds(pl.multiple_of(at * half, half), half) for at in (hx, 1 - hx)]


def dot_halves(left_ref, hx, own_ref, other_ref):
    own, other = halves(hx, left_ref.shape[1])
    return dot(left_ref[:, own], own_ref[...]) + dot(left_ref[:, other], other_ref[...])


def front_kernel(steps, plane_ref, *refs):
    count = len(flatten(steps))
    pieces, refs = like(steps, refs[:count]), refs[count:]
    gain_ref, shift_ref, own_ref, other_ref, bias_ref, cos_ref, sin_ref = refs[:7]
    h_ref, q_ref, kv_ref, pre_ref, out_ref, mean_ref, scale_ref, x_ref = refs[-8:]
    take_rows(x_ref, pieces, 0)
    x = x_ref[...].astype(F32)
    mean = jnp.mean(x, -1, keepdims=True)
    centred = x - mean
    scale = lax.rsqrt(jnp.mean(centred * centred, -1, keepdims=True) + EPS)
    mean_ref[...] = mean
    scale_ref[...] = scale
    h_ref[...] = (centred * scale * gain_ref[...] + shift_ref[...]).astype(BF)
    linear = dot_halves(h_ref, plane_ref[0], own_ref, other_ref) + bias_ref[...]
    lane = lax.broadcasted_iota(jnp.int32, (x.shape[0], 128), 1)
    cosine, sine = cos_ref[...], sin_ref[...]
    q_ref[...] = turn(linear[:, :128], cosine, sine, lane).astype(BF) * BF(HEAD_DIM**-0.5)
    kv_ref[:, :128] = turn(linear[:, 128:256], cosine, sine, lane).astype(BF)
    kv_ref[:, 128:] = linear[:, 256:384].astype(BF)
    pre = linear[:, 384:]
    pre_ref[...] = pre
    out_ref[...] = (0.5 * pre * (1.0 + jnp.tanh(0.7978845608 * (pre + 0.044715 * pre * pre * pre)))).astype(BF)


def front(plane, pieces, held, gain, shift, own, other, bias, cosine, sine):
    block, width = sum(piece.shape[0] for piece in pieces[0]), gain.shape[1]
    rows = 8 * block
    cols = own.shape[1]
    wide = cols - 384
    flat_pieces = flatten(pieces)
    here = functools.partial(by_row, block, begin=4 if held else 0)
    lanes = (width, 128, 256, wide, wide, 1, 1)
    types = (BF, BF, BF, F32, BF, F32, F32)
    return pl.pallas_call(
        functools.partial(front_kernel, pieces),
        grid_spec=pltpu.PrefetchScalarGridSpec(
            num_scalar_prefetch=1,
            grid=(4,),
            in_specs=fixed(*flat_pieces, gain, shift, own, other, bias)
            + [here(128), here(128)]
            + [pl.BlockSpec(memory_space=pl.ANY)] * len(held),
            out_specs=[here(n) for n in lanes],
            scratch_shapes=[pltpu.VMEM((block, width), BF)],
        ),
        out_shape=[jax.ShapeDtypeStruct((rows, n), kind) for n, kind in zip(lanes, types)],
        input_output_aliases={len(flat_pieces) + 8 + i: i for i in range(len(held))},
        compiler_params=pltpu.CompilerParams(vmem_limit_bytes=VMEM_LIMIT),
        cost_estimate=pl.CostEstimate(
            flops=rows * width * cols + 6 * rows * width, bytes_accessed=rows * width * 3, transcendentals=rows * wide
        ),
    )(plane[None], *flat_pieces, gain, shift, own, other, bias, cosine, sine, *held)


def two_heads(value):
    lane = lax.broadcasted_iota(jnp.int32, value.shape, 1)
    zero = jnp.zeros_like(value)
    return jnp.concatenate([jnp.where(lane < HEAD_DIM, value, zero), jnp.where(lane < HEAD_DIM, zero, value)], 0)


def one_row(value):
    half = value.shape[0] // 2
    lane = lax.broadcasted_iota(jnp.int32, (half, 128), 1)
    return jnp.where(lane < HEAD_DIM, value[:half], value[half:])


def place_in(row, share):
    return ((row & share) << 1) | ((row & (2 * share)) >> 1) | (row & (share - 1))


def allowed_pairs(meta_ref, block, query_at, key_at):
    turned, length = meta_ref[0], meta_ref[1]
    shape = (block, 2 * block)
    row = lax.broadcasted_iota(jnp.int32, shape, 1) & (block - 1)
    query = query_at * block + (place_in(row, block // 4) ^ turned)
    key = key_at * block + (place_in(lax.broadcasted_iota(jnp.int32, shape, 0), block // 4) ^ turned)
    return (key <= query) & (key < length)


def key_ranges(meta_ref, block, query_at):
    length = meta_ref[1]
    plain = jnp.minimum(query_at, length // block)
    last = jnp.minimum(query_at + 1, (length + block - 1) // block)
    return plain, last


def spot_of(at):
    near = 2 * Z_LEN
    spot = lax.rem(at, near)
    return lax.div(at, near) * 2 + lax.div(spot, 4), slice(None), lax.rem(spot, 2), lax.rem(lax.div(spot, 2), 2)


def rows_of(ref, at):
    value = ref[spot_of(at)]
    return value.reshape(value.shape[0] * value.shape[1], value.shape[2])


def add_rows(ref, at, value):
    ref[spot_of(at)] += value.reshape(2, value.shape[0] // 2, value.shape[1])


def flat(ref):
    value = ref[0, :, 0, 0]
    return value.reshape(value.shape[0] * value.shape[1], value.shape[2])


def key_rows(kv_ref, order_ref, at, count):
    return jnp.concatenate([rows_of(kv_ref, order_ref[at + i]) for i in range(count)], 0)


def over_keys(meta_ref, block, query_at, step, state):
    plain, last = key_ranges(meta_ref, block, query_at)
    pairs = plain // 2
    state = lax.fori_loop(0, pairs, lambda i, carried: step(False, 2, 2 * i, carried), state)
    state = lax.fori_loop(2 * pairs, plain, functools.partial(step, False, 1), state)
    return lax.fori_loop(plain, last, functools.partial(step, True, 1), state)


def attend_kernel(block, meta_ref, query_ref, order_ref, q_ref, kv_ref, full_ref, low_ref, lse_ref):
    query_at = query_ref[pl.program_id(0)]
    queries = two_heads(flat(q_ref))

    def step(masked, count, at, state):
        top, total, mixed = state
        both = key_rows(kv_ref, order_ref, at, count)
        scores = dot_rows(both[:, :128], queries)
        if masked:
            allowed = allowed_pairs(meta_ref, block, query_at, at)
            scores = jnp.where(allowed, scores, NEG)
        fresh = jnp.maximum(top, jnp.max(scores, 0, keepdims=True))
        factor = jnp.exp(top - fresh)
        weights = jnp.exp(scores - fresh)
        if masked:
            weights = jnp.where(allowed, weights, 0.0)
        total = total * factor + jnp.sum(weights, 0, keepdims=True)
        return fresh, total, mixed * factor + dot_cols(both[:, 128:], weights.astype(BF))

    state = (
        jnp.full((1, 2 * block), NEG, F32),
        jnp.zeros((1, 2 * block), F32),
        jnp.zeros((128, 2 * block), F32),
    )
    top, total, mixed = over_keys(meta_ref, block, query_at, step, state)
    mixed = mixed / total
    full = jnp.concatenate([mixed[:HEAD_DIM, :block], mixed[HEAD_DIM:, block:]], 0).T
    shape = full_ref.shape[1:2] + full_ref.shape[4:]
    full_ref[0, :, 0, 0] = full.reshape(shape)
    low_ref[0, :, 0, 0] = full.astype(BF).reshape(shape)
    lse_ref[...] = jnp.broadcast_to((top + jnp.log(total))[None], lse_ref.shape)


def placed(share, lanes):
    return pl.BlockSpec((1, 2, 1, 1, 2 * share, lanes), lambda i, *_: (i // 4, 0, i % 2, (i // 2) % 2, 0, 0))


def attend(table, q, kv, share):
    block = 4 * share
    blocks = 2 * Z_LEN
    rows, keys = q.shape[0], kv.shape[0]
    shape = (2, 2, 2, Z_LEN // 2, 2 * share, 128)
    kv_shape = (keys // (4 * Z_LEN * share), 2, 2, Z_LEN // 2, 2 * share, 256)
    full, low, lse = pl.pallas_call(
        functools.partial(attend_kernel, block),
        grid_spec=pltpu.PrefetchScalarGridSpec(
            num_scalar_prefetch=3,
            grid=(blocks,),
            in_specs=[placed(share, 128), pl.BlockSpec(kv_shape, lambda i, *_: (0, 0, 0, 0, 0, 0))],
            out_specs=[placed(share, 128), placed(share, 128), pl.BlockSpec((1, 8, 2 * block), lambda i, *_: (i, 0, 0))],
        ),
        out_shape=[
            jax.ShapeDtypeStruct(shape, F32),
            jax.ShapeDtypeStruct(shape, BF),
            jax.ShapeDtypeStruct((blocks, 8, 2 * block), F32),
        ],
        compiler_params=pltpu.CompilerParams(vmem_limit_bytes=VMEM_LIMIT),
        cost_estimate=pl.CostEstimate(
            flops=16 * rows * keys * 128, bytes_accessed=rows * 128 * 16, transcendentals=rows * keys
        ),
    )(*table, q.reshape(shape), kv.reshape(kv_shape))
    return full, low.reshape(rows, 128), lse


def attend_back_kernel(blocks, block, meta_ref, query_ref, order_ref, q_ref, kv_ref, full_ref, lse_ref, grad_ref, dq_ref, dkv_ref, dk_acc, dv_acc):
    at_block = pl.program_id(0)
    query_at = query_ref[at_block]
    queries = two_heads(flat(q_ref))
    grads = two_heads(flat(grad_ref))
    full = flat(full_ref)
    delta = jnp.sum(grads.astype(F32) * jnp.concatenate([full, full], 0), -1, keepdims=True)
    delta = jnp.broadcast_to(delta, (2 * block, 128)).T[:1]
    lse = lse_ref[0, :1]

    @pl.when(at_block == 0)
    def _():
        dk_acc[...] = jnp.zeros_like(dk_acc)
        dv_acc[...] = jnp.zeros_like(dv_acc)

    def step(masked, count, at, grad_query):
        both = key_rows(kv_ref, order_ref, at, count)
        keys = both[:, :128]
        scores = dot_rows(keys, queries)
        if masked:
            allowed = allowed_pairs(meta_ref, block, query_at, at)
            scores = jnp.where(allowed, scores, NEG)
        weights = jnp.exp(scores - lse)
        if masked:
            weights = jnp.where(allowed, weights, 0.0)
        grad_scores = (weights * (dot_rows(both[:, 128:], grads) - delta)).astype(BF)
        grad_keys = dot(grad_scores, queries)
        grad_values = dot(weights.astype(BF), grads)
        for i in range(count):
            spot = order_ref[at + i]
            add_rows(dk_acc, spot, grad_keys[i * block : (i + 1) * block])
            add_rows(dv_acc, spot, grad_values[i * block : (i + 1) * block])
        return grad_query + dot_cols(grad_scores, keys)

    grad_query = over_keys(meta_ref, block, query_at, step, jnp.zeros((2 * block, 128), F32))
    shape = dq_ref.shape[1:2] + dq_ref.shape[4:]
    dq_ref[0, :, 0, 0] = (one_row(grad_query) * HEAD_DIM**-0.5).astype(BF).reshape(shape)

    @pl.when(at_block == blocks - 1)
    def _():
        dkv_ref[..., :128] = dk_acc[...].astype(BF)
        dkv_ref[..., 128:] = dv_acc[...].astype(BF)


def attend_back(table, q, kv, full, lse, grad, share):
    block = 4 * share
    blocks = 2 * Z_LEN
    rows, keys = q.shape[0], kv.shape[0]
    shape = (2, 2, 2, Z_LEN // 2, 2 * share, 128)
    kv_shape = (keys // (4 * Z_LEN * share), 2, 2, Z_LEN // 2, 2 * share, 256)
    kv_spec = pl.BlockSpec(kv_shape, lambda i, *_: (0, 0, 0, 0, 0, 0))
    dq, dkv = pl.pallas_call(
        functools.partial(attend_back_kernel, blocks, block),
        grid_spec=pltpu.PrefetchScalarGridSpec(
            num_scalar_prefetch=3,
            grid=(blocks,),
            in_specs=[
                placed(share, 128),
                kv_spec,
                placed(share, 128),
                pl.BlockSpec((1, 8, 2 * block), lambda i, *_: (i, 0, 0)),
                placed(share, 128),
            ],
            out_specs=[placed(share, 128), kv_spec],
            scratch_shapes=[pltpu.VMEM(kv_shape[:-1] + (128,), F32), pltpu.VMEM(kv_shape[:-1] + (128,), F32)],
        ),
        out_shape=[jax.ShapeDtypeStruct(shape, BF), jax.ShapeDtypeStruct(kv_shape, BF)],
        compiler_params=pltpu.CompilerParams(vmem_limit_bytes=VMEM_LIMIT),
        cost_estimate=pl.CostEstimate(
            flops=40 * rows * keys * 128, bytes_accessed=rows * 128 * 24, transcendentals=rows * keys
        ),
    )(*table, q.reshape(shape), kv.reshape(kv_shape), full, lse, grad.reshape(shape))
    return dq.reshape(rows, 128), dkv.reshape(keys, 256)


def store_parts(parts, total_ref):
    for at in range(8):
        half, core, ky = at // 4, at // 2 % 2, at % 2

        @pl.when(pl.program_id(0) == at)
        def _(ref=parts[4 * (1 - core) + 2 * (1 - ky) + half]):
            ref[...] = total_ref[...]


def part_shapes(rows, width):
    return [jax.ShapeDtypeStruct((rows, width), BF)] * 8


def out_kernel(plane_ref, attn_ref, units_ref, dense_ref, own_ref, other_ref, *refs):
    parts, total_ref = refs[:-1], refs[-1]
    attn, units = attn_ref[...], units_ref[...]
    for part, weight_ref in zip(halves(plane_ref[0], total_ref.shape[1]), (own_ref, other_ref)):
        total_ref[:, part] = (dot(attn, dense_ref[:, part]) + dot_rows(units, weight_ref[...])).astype(BF)
    store_parts(parts, total_ref)


def out_partial(plane, attn, units, dense, own, other, block):
    rows, width = attn.shape[0], dense.shape[1]
    wide = units.shape[1]
    shapes = part_shapes(block, width)
    return pl.pallas_call(
        out_kernel,
        grid_spec=pltpu.PrefetchScalarGridSpec(
            num_scalar_prefetch=1,
            grid=(rows // block,),
            in_specs=[by_row(block, 128), by_row(block, wide)] + fixed(dense, own, other),
            out_specs=fixed(*shapes),
            scratch_shapes=[pltpu.VMEM((block, width), BF)],
        ),
        out_shape=shapes,
        compiler_params=pltpu.CompilerParams(vmem_limit_bytes=VMEM_LIMIT),
        cost_estimate=pl.CostEstimate(
            flops=2 * rows * width * (128 + wide), bytes_accessed=2 * rows * width, transcendentals=0
        ),
    )(plane[None], attn, units, dense, own, other)


def branch_kernel(steps, plane_ref, *refs):
    count = len(flatten(steps))
    pieces, refs = like(steps, refs[:count]), refs[count:]
    dense_ref, own_ref, other_ref, pre_ref, attn_ref, grad_ref, g_ref = refs
    take_rows(g_ref, pieces, 0)
    attn_ref[...] = dot_rows(g_ref[...], dense_ref[...]).astype(BF)
    grad = dot_halves(g_ref, plane_ref[0], own_ref, other_ref)
    u = pre_ref[...]
    square = u * u
    bend = jnp.tanh(0.7978845608 * u * (1.0 + 0.044715 * square))
    slope = 0.5 * (1.0 + bend) + 0.5 * u * (1.0 - bend * bend) * (0.7978845608 * (1.0 + 3 * 0.044715 * square))
    grad_ref[...] = (grad * slope).astype(BF)


def branch_grads(plane, pieces, dense, own, other, pre, block):
    width = dense.shape[1]
    rows, wide = pre.shape
    flat_pieces = flatten(pieces)
    return pl.pallas_call(
        functools.partial(branch_kernel, pieces),
        grid_spec=pltpu.PrefetchScalarGridSpec(
            num_scalar_prefetch=1,
            grid=(rows // block,),
            in_specs=fixed(*flat_pieces, dense, own, other) + [by_row(block, wide)],
            out_specs=[by_row(block, 128), by_row(block, wide), by_row(block, width)],
        ),
        out_shape=[
            jax.ShapeDtypeStruct((rows, 128), BF),
            jax.ShapeDtypeStruct((rows, wide), BF),
            jax.ShapeDtypeStruct((rows, width), BF),
        ],
        compiler_params=pltpu.CompilerParams(vmem_limit_bytes=VMEM_LIMIT),
        cost_estimate=pl.CostEstimate(
            flops=2 * rows * width * (128 + wide), bytes_accessed=rows * width * 4, transcendentals=rows * wide
        ),
    )(plane[None], *flat_pieces, dense, own, other, pre)


def turn_back(value, cosine, sine, lane):
    return turn(value.astype(F32), cosine, -sine, lane).astype(BF)


def back_kernel(steps, plane_ref, *refs):
    count = len(flatten(steps))
    pieces, refs = like(steps, refs[:count]), refs[count:]
    linear_ref, units_ref, own_ref, other_ref, mean_ref, scale_ref = refs[:6]
    parts, (gain_ref, shift_ref, small_ref, x_ref, total_ref) = refs[6:14], refs[14:]
    take_rows(x_ref, pieces, 0)
    linear, units = linear_ref[...], units_ref[...]

    @pl.when(pl.program_id(0) == 0)
    def _():
        gain_ref[...] = jnp.zeros_like(gain_ref)
        shift_ref[...] = jnp.zeros_like(shift_ref)
        small_ref[...] = jnp.zeros_like(small_ref)

    small_ref[:, :384] += jnp.sum(linear.astype(F32), 0, keepdims=True)
    small_ref[:, 384:] += jnp.sum(units.astype(F32), 0, keepdims=True)
    mean, scale = mean_ref[...], scale_ref[...]
    for part, weight_ref in zip(halves(plane_ref[0], total_ref.shape[1]), (own_ref, other_ref)):
        total = dot_rows(linear, weight_ref[:, :384]) + dot_rows(units, weight_ref[:, 384:])
        total_ref[:, part] = total.astype(BF)
        gain_ref[:, part] += jnp.sum(total * ((x_ref[:, part].astype(F32) - mean) * scale), 0, keepdims=True)
        shift_ref[:, part] += jnp.sum(total, 0, keepdims=True)
    store_parts(parts, total_ref)


def back_partial(plane, pieces, linear, units, own, other, mean, scale):
    rows = linear.shape[0]
    block = sum(piece.shape[0] for piece in pieces[0])
    width, cols = 2 * own.shape[0], own.shape[1]
    flat_pieces = flatten(pieces)
    shapes = part_shapes(block, width)
    sums = [jax.ShapeDtypeStruct((1, n), F32) for n in (width, width, cols)]
    *parts, gain, shift, small = pl.pallas_call(
        functools.partial(back_kernel, pieces),
        grid_spec=pltpu.PrefetchScalarGridSpec(
            num_scalar_prefetch=1,
            grid=(rows // block,),
            in_specs=fixed(*flat_pieces)
            + [by_row(block, 384), by_row(block, cols - 384)]
            + fixed(own, other)
            + [by_row(block, 1), by_row(block, 1)],
            out_specs=fixed(*shapes) + fixed(*sums),
            scratch_shapes=[pltpu.VMEM((block, width), BF), pltpu.VMEM((block, width), BF)],
        ),
        out_shape=shapes + sums,
        compiler_params=pltpu.CompilerParams(vmem_limit_bytes=VMEM_LIMIT),
        cost_estimate=pl.CostEstimate(
            flops=2 * rows * width * cols, bytes_accessed=4 * rows * width, transcendentals=0
        ),
    )(plane[None], *flat_pieces, linear, units, own, other, mean, scale)
    return parts, (gain, shift, small)


def weight_kernel(plane_ref, *refs):
    *pairs, away_ref, mine_ref = refs
    for out_ref, this in ((away_ref, pl.program_id(0) < 2), (mine_ref, pl.program_id(0) >= 2)):

        @pl.when(this)
        def _(out_ref=out_ref):
            begin = 0
            for left, right in zip(pairs[::2], pairs[1::2]):
                end = begin + right.shape[1]
                value = dot_cols(left[...], right[...]).astype(BF)
                out_ref[:, 0, :, begin:end] = value.reshape(out_ref.shape[0], out_ref.shape[2], end - begin)
                begin = end


def weight_rows(rows, quarter):
    return pl.BlockSpec((rows, quarter), lambda i, p: (0, ((p[0] + 1 - i // 2) % 2) * 2 + i % 2))


def weight_shape(quarter, cols):
    return jax.ShapeDtypeStruct((Z_LEN, 2, quarter // Z_LEN, cols), BF)


def weight_outs(quarter, cols):
    shape = (Z_LEN, 1, quarter // Z_LEN, cols)
    return [
        pl.BlockSpec(shape, lambda i, p: (0, jnp.minimum(i, 1), 0, 0)),
        pl.BlockSpec(shape, lambda i, p: (0, jnp.maximum(i - 2, 0), 0, 0)),
    ]


def weight_grads(plane, *pairs):
    rows, width = pairs[0][0].shape
    cols = sum(right.shape[1] for _, right in pairs)
    quarter = width // 4
    out = weight_shape(quarter, cols)
    specs = [spec for _, right in pairs for spec in (weight_rows(rows, quarter), *fixed(right))]
    return pl.pallas_call(
        weight_kernel,
        grid_spec=pltpu.PrefetchScalarGridSpec(
            num_scalar_prefetch=1,
            grid=(4,),
            in_specs=specs,
            out_specs=weight_outs(quarter, cols),
        ),
        out_shape=[out, out],
        compiler_params=pltpu.CompilerParams(vmem_limit_bytes=VMEM_LIMIT),
        cost_estimate=pl.CostEstimate(
            flops=2 * rows * width * cols, bytes_accessed=2 * rows * width, transcendentals=0
        ),
    )(plane[None], *[value for pair in pairs for value in pair])


def triple_grads_kernel(plane_ref, h_ref, dq_ref, dkv_ref, cos_ref, sin_ref, away_ref, mine_ref, linear_ref):
    @pl.when(pl.program_id(0) == 0)
    def _():
        rows = 256

        def step(at, carry):
            here = pl.ds(pl.multiple_of(at * rows, rows), rows)
            lane = lax.broadcasted_iota(jnp.int32, (rows, 128), 1)
            cosine, sine = cos_ref[here, :], sin_ref[here, :]
            linear_ref[here, :128] = turn_back(dq_ref[here, :], cosine, sine, lane)
            linear_ref[here, 128:256] = turn_back(dkv_ref[here, :128], cosine, sine, lane)
            linear_ref[here, 256:] = dkv_ref[here, 128:]
            return carry

        lax.fori_loop(0, dq_ref.shape[0] // rows, step, 0)

    weight_kernel(plane_ref, h_ref, linear_ref, away_ref, mine_ref)


def triple_grads(plane, h, dq, dkv, cosine, sine):
    rows, width = h.shape
    quarter = width // 4
    out = weight_shape(quarter, 384)
    linear = jax.ShapeDtypeStruct((rows, 384), BF)
    return pl.pallas_call(
        triple_grads_kernel,
        grid_spec=pltpu.PrefetchScalarGridSpec(
            num_scalar_prefetch=1,
            grid=(4,),
            in_specs=[weight_rows(rows, quarter)] + fixed(dq, dkv, cosine, sine),
            out_specs=weight_outs(quarter, 384) + fixed(linear),
        ),
        out_shape=[out, out, linear],
        compiler_params=pltpu.CompilerParams(vmem_limit_bytes=VMEM_LIMIT),
        cost_estimate=pl.CostEstimate(
            flops=2 * rows * width * 384, bytes_accessed=2 * rows * width, transcendentals=0
        ),
    )(plane[None], h, dq, dkv, cosine, sine)


def pack_kernel(triple_ref, expand_ref, shrink_ref, in_ref, out_ref):
    ranks, wide = in_ref.shape[0], out_ref.shape[2]
    for rank in range(ranks):
        for s in range(3):
            pair = [triple_ref[:, pl.ds((s * HEADS + x * ranks + rank) * HEAD_DIM, HEAD_DIM)] for x in range(2)]
            in_ref[rank, :, s * 128 : (s + 1) * 128] = jnp.concatenate(pair, 1)
        in_ref[rank, :, 384:] = expand_ref[:, rank * wide : (rank + 1) * wide]
        out_ref[rank] = shrink_ref[:, rank * wide : (rank + 1) * wide]


def pack(triple, expand, shrink, ranks):
    held = triple.shape[0]
    wide = expand.shape[1] // ranks
    return pl.pallas_call(
        pack_kernel,
        out_shape=[
            jax.ShapeDtypeStruct((ranks, held, 384 + wide), BF),
            jax.ShapeDtypeStruct((ranks, held, wide), BF),
        ],
        compiler_params=pltpu.CompilerParams(vmem_limit_bytes=VMEM_LIMIT),
    )(triple, expand, shrink)


def unpack_units_kernel(place_ref, *refs):
    units, (shrink_ref, expand_ref) = refs[:4], refs[4:]
    core, by = place_ref[0], place_ref[1]
    wide = units[0].shape[2] // 2
    for away in range(2):
        for bz in range(Z_LEN):
            first = jnp.bitwise_xor(core, away) * 2 * Z_LEN + bz * 2
            for across_y in range(2):
                value = units[2 * away + across_y][bz].astype(F32)
                at = pl.ds(pl.multiple_of((first + jnp.bitwise_xor(by, across_y)) * wide, wide), wide)
                shrink_ref[:, at] = value[:, :wide]
                expand_ref[:, at] = value[:, wide:]


def unpack_triple_kernel(place_ref, *refs):
    triples, triple_ref = refs[:4], refs[4]
    core, by = place_ref[0], place_ref[1]
    for away in range(2):
        for bz in range(Z_LEN):
            first = jnp.bitwise_xor(core, away) * 2 * Z_LEN + bz * 2
            own, other = triples[2 * away][bz].astype(F32), triples[2 * away + 1][bz].astype(F32)
            low, high = jnp.where(by == 0, own, other), jnp.where(by == 0, other, own)
            for s in range(3):
                for x in range(2):
                    lanes = slice(s * 128 + x * HEAD_DIM, s * 128 + (x + 1) * HEAD_DIM)
                    at = pl.multiple_of((s * HEADS + x * 4 * Z_LEN + first) * HEAD_DIM, 128)
                    triple_ref[:, pl.ds(at, 128)] = jnp.concatenate([low[:, lanes], high[:, lanes]], 1)


def unpack(kernel, widths, core, by, pieces):
    shapes = [jax.ShapeDtypeStruct((pieces[0].shape[1], width), F32) for width in widths]
    return pl.pallas_call(
        kernel,
        grid_spec=pltpu.PrefetchScalarGridSpec(
            num_scalar_prefetch=1,
            grid=(1,),
            in_specs=fixed(*pieces),
            out_specs=fixed(*shapes),
        ),
        out_shape=shapes,
        compiler_params=pltpu.CompilerParams(vmem_limit_bytes=VMEM_LIMIT),
    )(jnp.where(jnp.arange(2) == 0, core, by).astype(jnp.int32), *pieces)


def turn_tables(positions):
    half = ROT // 2
    inverse = 10000.0 ** (-(jnp.arange(half, dtype=F32) * 2.0) / ROT)
    angles = positions.astype(F32)[:, None] * inverse[None, :]
    cosine, sine = jnp.cos(angles), jnp.sin(angles)
    rest = (positions.shape[0], HEAD_DIM - ROT)
    cosine = jnp.concatenate([cosine, cosine, jnp.ones(rest, F32)], 1)
    sine = jnp.concatenate([-sine, sine, jnp.zeros(rest, F32)], 1)
    return jnp.tile(cosine, (1, 2)), jnp.tile(sine, (1, 2))


def core_pair(own, other, core):
    return jnp.where(core == 0, jnp.stack([own, other], 1), jnp.stack([other, own], 1))


def body(
    inputs,
    norm_gain,
    norm_bias,
    triple_weight,
    triple_bias,
    dense_weight,
    dense_bias,
    expand_weight,
    expand_bias,
    shrink_weight,
    shrink_bias,
    lengths,
    block_order,
    cotangent,
):
    share, width = inputs.shape[2], inputs.shape[3]
    hx, core, bs, bz, by = (lax.axis_index(name) for name in ALL)
    spread = lax.axis_size("bs")
    ranks = 2 * Z_LEN * 2
    devices = 2 * ranks * spread
    block = 4 * share
    rows = ranks * 2 * share
    near_blocks = Z_LEN * 2
    blocks = block_order.shape[0]
    held = width // devices
    ff = expand_weight.shape[1]
    ff_here = ff // ranks
    length = lengths[hx]

    def block_at(index):
        return jnp.sum(jnp.where(jnp.arange(blocks, dtype=jnp.int32) == index, block_order, 0))

    token_pos = (
        block_at(bs * near_blocks + bz * 2 + by) * block
        + (hx * 2 + core) * share
        + jnp.arange(share, dtype=jnp.int32)
    )
    valid = (token_pos[None, :] < lengths[:, None]).astype(F32)[:, :, None]

    spots = jnp.arange(blocks, dtype=jnp.int32)
    within = spots % near_blocks
    index = spots - within + ((bz + Z_LEN - within // 2) % Z_LEN) * 2 + (by + within) % 2
    key_at = jnp.sum(jnp.where(index[:, None] == spots[None, :], block_order[None, :], 0), 1)
    query_at = lax.dynamic_slice_in_dim(key_at, bs * near_blocks, near_blocks)
    turned = hx * 2 * share + core * share
    inside = place_in(jnp.arange(block, dtype=jnp.int32), share) ^ turned
    block_pos = query_at.reshape(2, Z_LEN // 2, 2).transpose(0, 2, 1)[:, None, :, :, None]
    row_pos = (block_pos * block + inside.reshape(1, 2, 1, 1, 2 * share)).reshape(rows)
    order = jnp.sum(jnp.where(key_at[None, :] == spots[:, None], spots[None, :], 0), 1)
    table = jnp.where(jnp.arange(2) == 0, turned, length).astype(jnp.int32), query_at, order
    cosine, sine = turn_tables(row_pos)

    def to_cols(sent):
        cols = sent.shape[2]
        got = lax.all_to_all(sent, RANK, split_axis=0, concat_axis=0, tiled=True)
        if spread > 1:
            got = lax.all_gather(got.reshape(2, 1, near_blocks, held, cols), "bs", axis=1, tiled=True)
        return got.reshape(width // 2, cols)

    def to_rows_z(mine):
        cols = mine.shape[-1]
        got = lax.all_to_all(mine, "bz", split_axis=0, concat_axis=0, tiled=True)
        return got.reshape(Z_LEN, 2, 2, held, cols)

    def over_bs(mine):
        if spread == 1:
            return mine
        cols = mine.shape[-1]
        mine = mine.transpose(1, 0, 2, 3).reshape(2, spread, Z_LEN, 2 * held, cols)
        mine = lax.psum_scatter(mine, "bs", scatter_dimension=1, tiled=True)
        return mine.reshape(2, Z_LEN, 2 * held, cols).transpose(1, 0, 2, 3)

    def split(value, index, axis):
        return (
            lax.dynamic_index_in_dim(value, index, axis, keepdims=False),
            lax.dynamic_index_in_dim(value, 1 - index, axis, keepdims=False),
        )

    def both(low, high):
        return jnp.concatenate([low, high], 0)

    x_a = lax.dynamic_index_in_dim(inputs[:, 0], hx, 0, keepdims=False)
    x_b = lax.dynamic_index_in_dim(inputs[:, 0], 1 - hx, 0, keepdims=False)
    vectors = (norm_gain, norm_bias, triple_bias, expand_bias, dense_bias, shrink_bias)
    sent_in, sent_out = pack(triple_weight, expand_weight, shrink_weight, ranks)

    sent_in, sent_out, vectors, cotangent, x_b = fence((sent_in, sent_out, vectors, cotangent, x_b))
    in_own = to_cols(sent_in)
    x_b = swap(x_b, "hx")
    small = jnp.concatenate(vectors)[None]
    x_0 = both(x_a, x_b)
    grad_y = (cotangent[:, 0].astype(F32) * valid).astype(BF)
    g_a = lax.dynamic_index_in_dim(grad_y, hx, 0, keepdims=False)
    g_b = swap(lax.dynamic_index_in_dim(grad_y, 1 - hx, 0, keepdims=False), "hx")
    small = joined(by, small, swap(small, "by"))
    small = joined(core, small, swap(small, "core"))
    more = swap(small, "hx")
    cosine, sine = turn_tables(row_pos)

    x_0, in_own, g_b, small, more, cosine, sine = fence((x_0, in_own, g_b, small, more, cosine, sine), table)
    in_other = swap(in_own, "hx")
    y_0 = swap(x_0, "by")
    x_1 = ring(x_0)
    g_0 = both(g_a, g_b)
    small = joined(hx, small, more)
    more = across(small, 1)

    y_0, x_1, g_0, small, more = fence((y_0, x_1, g_0, small, more))
    y_1 = swap(x_1, "by")
    x_2 = ring(x_1)
    small = joined(bz % 2, small, more)
    more = across(small, 2)

    y_1, x_2, small, more = fence((y_1, x_2, small, more))
    y_2 = swap(x_2, "by")
    x_3 = ring(x_2)
    own_one, y_one = both(x_0, x_1), both(y_0, y_1)
    c_one = swap(own_one, "core"), swap(y_one, "core")
    small = in_all(joined(bz // 2, small, more), spread)

    cuts = [0]
    for leaf in (norm_gain, norm_bias, triple_bias, expand_bias, dense_bias, shrink_bias):
        cuts.append(cuts[-1] + leaf.shape[0])
    gain, shift, triple_b, expand_b, dense_b, shrink_b = (
        small[:, low:high].reshape(-1).astype(F32) for low, high in zip(cuts[:-1], cuts[1:])
    )
    rank = core * near_blocks + bz * 2 + by
    bias_triple = lax.dynamic_index_in_dim(
        triple_b.reshape(3, 2, ranks, HEAD_DIM).transpose(2, 0, 1, 3).reshape(ranks, 384), rank, 0
    )
    bias_expand = lax.dynamic_index_in_dim(expand_b.reshape(ranks, ff_here), rank, 0)
    bias_in = jnp.concatenate([bias_triple, bias_expand], 1)

    y_2, x_3, c_one, in_other, bias_in = fence((y_2, x_3, c_one, in_other, bias_in))
    y_3 = swap(x_3, "by")
    g_1 = ring(g_0)
    own_two = both(x_2, x_3)
    c_two = (swap(own_two, "core"),)
    x_one = ((own_one,), (y_one,), (c_one[0],), (c_one[1],))
    into = (gain[None], shift[None], in_own, in_other, bias_in, cosine, sine)
    held_one = front(hx, x_one, (), *into)

    held_one, y_3, g_1, c_two, sent_out = fence((held_one, y_3, g_1, c_two, sent_out))
    y_two = both(y_2, y_3)
    out_own = to_cols(sent_out)
    c_two = c_two[0], swap(y_two, "core")

    held_one, c_two = fence((held_one, c_two))
    x_two = ((own_two,), (y_two,), (c_two[0],), (c_two[1],))
    h, q, kv, pre, expand_out, mean, scale = front(hx, x_two, held_one, *into)

    q, g_0, g_1, out_own = fence((q, g_0, g_1, out_own))
    out_other = swap(out_own, "hx")
    own_one = both(g_0, g_1)
    y_one = swap(own_one, "by")
    g_2 = ring(g_1)
    g_3 = lax.ppermute(g_0, "bz", around(3))
    kv_all = kv if spread == 1 else lax.all_gather(kv, "bs", axis=0, tiled=True)
    attn_full, attn_low, lse = attend(table, q, kv_all, share)
    if spread == 1:
        dense_away = swap(dense_weight, "hx")
        dense_pair = jnp.where(hx == 0, both(dense_weight, dense_away), both(dense_away, dense_weight))
    else:
        dense_all = lax.all_gather(dense_weight, ALL, axis=0, tiled=True).reshape(2, ranks, HEAD_DIM, width)
        dense_pair = lax.dynamic_index_in_dim(dense_all, rank, 1, keepdims=False).reshape(128, width)

    attn_low, y_one, g_2, g_3, own_one, out_other, dense_pair = fence(
        (attn_low, y_one, g_2, g_3, own_one, out_other, dense_pair)
    )
    own_two = both(g_2, g_3)
    y_two = swap(own_two, "by")
    c_one = swap(own_one, "core"), swap(y_one, "core")
    c_two = (swap(own_two, "core"),)
    onto = (dense_pair, out_own, out_other)
    out_parts = out_partial(hx, attn_low, expand_out, *onto, block)

    y_two, c_one, c_two, out_parts = fence((y_two, c_one, c_two, out_parts))
    g_one = own_one, y_one
    c_two = c_two[0], swap(y_two, "core")
    g_pieces = tuple((piece,) for piece in g_one + c_one + (own_two, y_two) + c_two)

    out_parts, g_pieces = fence((out_parts, g_pieces))
    got = [swap(part, "core") for part in out_parts[:4]]
    grad_attention, grad_pre, g_all = branch_grads(hx, g_pieces, *onto, pre, block)

    grad_attention, grad_pre, g_all, got = fence((grad_attention, grad_pre, g_all, got))
    far = add_low(both(*out_parts[4:6]), both(*got[:2]))

    grad_attention, grad_pre, g_all, far = fence((grad_attention, grad_pre, g_all, far))
    out_y = swap(far, "by")
    units_away, units_mine = weight_grads(hx, (g_all, expand_out), (h, grad_pre))

    grad_attention, units_away = fence((grad_attention, units_away))
    units_away = swap(units_away, "hx")
    dq, dkv = attend_back(table, q, kv_all, attn_full, lse, grad_attention, share)
    if spread > 1:
        dkv = lax.psum_scatter(dkv, "bs", scatter_dimension=0, tiled=True)

    def three(k, near_part, got_part, y_part):
        rows = slice(k * 2 * share, (k + 1) * 2 * share)
        return near_part[rows].astype(F32) + got_part[rows].astype(F32) + y_part[rows].astype(F32)

    def out_three(kz):
        half = kz // 2
        return three(kz % 2, out_parts[6 + half], got[2 + half], out_y[half * block : (half + 1) * block])

    dq, out_y, out_parts, got = fence((dq, out_y, out_parts, got))
    out_sum = out_three(3)

    dq, out_sum = fence((dq, out_sum))
    ringed = ring_back(out_sum)
    triple_away, triple_mine, grad_linear = triple_grads(hx, h, dq, dkv, cosine, sine)

    units_away, triple_away, grad_linear, ringed = fence((units_away, triple_away, grad_linear, ringed))
    mine = add_low(units_mine, units_away)

    mine, triple_away, grad_linear = fence((mine, triple_away, grad_linear))
    units_rows = to_rows_z(over_bs(mine))
    triple_away = swap(triple_away, "hx")
    h_parts, sums = back_partial(hx, x_one + x_two, grad_linear, grad_pre, in_own, in_other, mean, scale)

    h_parts, sums, triple_away, ringed, g_all = fence((h_parts, sums, triple_away, ringed, g_all))
    h_got = [swap(part, "core") for part in h_parts[:4]]
    mine = add_low(triple_mine, triple_away)
    grad_dense_here = dot_cols(g_all, attn_low)
    out_sum = out_three(2) + ringed

    sum_gain, sum_shift, sum_in = sums
    here = jnp.arange(ranks, dtype=jnp.int32)[:, None] == rank
    sum_triple = (
        jnp.where(here, sum_in[:, :384], 0.0)
        .reshape(ranks, 3, 2, HEAD_DIM)
        .transpose(1, 2, 0, 3)
        .reshape(3 * width)
    )
    sum_expand = jnp.where(here, sum_in[:, 384:], 0.0).reshape(ff)
    sum_y = jnp.sum(grad_y.astype(F32), (0, 1))
    pieces = [leaf.reshape(devices, -1) for leaf in (sum_gain, sum_shift, sum_triple, sum_expand, sum_y)]
    small = jnp.concatenate(pieces, 1).reshape(2, 2, spread, Z_LEN, 2, -1)


    h_got, units_rows, out_sum, small, mine = fence((h_got, units_rows, out_sum, small, mine), grad_dense_here)
    far_one, far_two = add_low(h_parts[4], h_got[0]), add_low(h_parts[5], h_got[1])

    far_one, far_two, out_sum, small, mine = fence((far_one, far_two, out_sum, small, mine))
    h_y_two = swap(far_two, "by")
    triple_rows = to_rows_z(over_bs(mine))
    ringed = ring_back(out_sum)
    small, away = halved(small, "core", 1)

    h_y_two, far_one, small, away, ringed, triple_rows = fence((h_y_two, far_one, small, away, ringed, triple_rows))
    h_sum = three(1, h_parts[7], h_got[3], h_y_two)
    out_sum = out_three(1) + ringed

    h_sum, far_one, small, away, out_sum = fence((h_sum, far_one, small, away, out_sum))
    h_y_one = swap(far_one, "by")
    ringed, out_ringed = ring_back(h_sum), ring_back(out_sum)
    away = swap(away, "core")
    units_parts, triple_parts = split(units_rows, by, 2), split(triple_rows, by, 2)

    h_y_one, ringed, out_ringed, small, away, units_parts, triple_parts = fence(
        (h_y_one, ringed, out_ringed, small, away, units_parts, triple_parts)
    )
    h_sum = three(0, h_parts[7], h_got[3], h_y_two) + ringed
    out_sum = (out_three(0) + out_ringed).reshape(2, share, width)
    out_away = out_sum[1].astype(BF)
    small, away = halved(small + away, "hx", 0)

    h_sum, out_sum, out_away, small, away, units_parts = fence((h_sum, out_sum, out_away, small, away, units_parts))
    ringed = ring_back(h_sum)
    units_got = swap(units_parts[1], "by")
    out_away = swap(out_away, "hx")
    away = swap(away, "hx")
    h_last = [three(at, h_parts[6], h_got[2], h_y_one) for at in (0, 1)]

    ringed, out_away, small, away, h_last, units_got = fence((ringed, out_away, small, away, h_last, units_got))
    h_sum = h_last[1] + ringed
    small, away = halved(small + away, "by", 2)

    h_sum, small, away, triple_parts, units_got = fence((h_sum, small, away, triple_parts, units_got))
    ringed = ring_back(h_sum)
    triple_got = swap(triple_parts[1], "by")
    units_own, units_away = split(jnp.stack([units_parts[0], units_got]), core, 2)
    units_away = swap(units_away, "core")
    grad_shrink, grad_expand = unpack(unpack_units_kernel, (ff, ff), core, by, (*units_own, *units_away))
    small = small + swap(away, "by")
    terms = [lax.dynamic_index_in_dim(small, (bz + kz) % Z_LEN, 1, keepdims=False) for kz in range(Z_LEN)]
    terms = terms[:1] + [lax.ppermute(terms[kz], "bz", around(kz)) for kz in range(1, Z_LEN)]

    source = inputs[:, 0].astype(F32)
    out_away = out_away.astype(F32)
    mixed = jnp.where(hx == 0, jnp.stack([out_sum[0], out_away]), jnp.stack([out_away, out_sum[0]]))
    output = (valid * (source + mixed + dense_b + shrink_b)).astype(BF).reshape(inputs.shape)

    ringed, terms, output, triple_got = fence((ringed, terms, output, triple_got), grad_shrink, grad_expand)
    triple_own, triple_away = split(jnp.stack([triple_parts[0], triple_got]), core, 2)
    triple_away = swap(triple_away, "core")
    (grad_triple,) = unpack(unpack_triple_kernel, (3 * width,), core, by, (*triple_own, *triple_away))
    h_sum = (h_last[0] + ringed).reshape(2, share, width)

    dense_grads = grad_dense_here.T.reshape(2, HEAD_DIM, width)
    if spread == 1:
        dense_mine = lax.dynamic_index_in_dim(dense_grads, hx, 0, keepdims=False)
        dense_away = lax.dynamic_index_in_dim(dense_grads, 1 - hx, 0, keepdims=False)
        grad_dense = dense_mine + swap(dense_away.astype(BF), "hx").astype(F32)
    else:
        spot = jnp.arange(ranks, dtype=jnp.int32)[None, :, None, None] == rank
        dense_whole = jnp.where(spot, dense_grads[:, None], 0.0).reshape(width, width)
        grad_dense = lax.psum_scatter(dense_whole, ALL, scatter_dimension=0, tiled=True)

    small = sum(terms)
    if spread > 1:
        small = lax.psum_scatter(small, "bs", scatter_dimension=0, tiled=True)
    small = small.reshape(-1)
    small_grads = []
    begin = 0
    for piece in pieces:
        small_grads.append(small[begin : begin + piece.shape[1]])
        begin += piece.shape[1]
    small_gain, small_shift, small_triple, small_expand, small_out = small_grads

    h_away = swap(h_sum[1].astype(BF), "hx").astype(F32)
    grad_h = jnp.where(hx == 0, jnp.stack([h_sum[0], h_away]), jnp.stack([h_away, h_sum[0]]))
    centred = source - jnp.mean(source, -1, keepdims=True)
    scale = lax.rsqrt(jnp.mean(centred * centred, -1, keepdims=True) + EPS)
    normed = centred * scale
    g = grad_h * gain
    grad_source = scale * (
        g - jnp.mean(g, -1, keepdims=True) - normed * jnp.mean(g * normed, -1, keepdims=True)
    )
    grad_inputs = (grad_y.astype(F32) + grad_source).astype(BF).reshape(inputs.shape)
    return (
        output,
        grad_inputs,
        small_gain,
        small_shift,
        grad_triple,
        small_triple,
        grad_dense,
        small_out,
        grad_expand,
        small_expand,
        grad_shrink,
        small_out,
    )


def solution(mesh):
    head, blk = mesh.devices.shape
    split = Mesh(mesh.devices.reshape(head // 2, 2, blk // (2 * Z_LEN), Z_LEN, 2), ALL)
    tokens = P(None, ("bs", "bz", "by"), ("hx", "core"), None)
    vector = P(ALL)
    matrix = P(ALL, None)
    return jax.shard_map(
        body,
        mesh=split,
        in_specs=(
            tokens,
            vector,
            vector,
            matrix,
            vector,
            matrix,
            vector,
            matrix,
            vector,
            matrix,
            vector,
            P(),
            P(),
            tokens,
        ),
        out_specs=(
            tokens,
            tokens,
            vector,
            vector,
            matrix,
            vector,
            matrix,
            vector,
            matrix,
            vector,
            matrix,
            vector,
        ),
        check_vma=False,
    )
```

```python
import functools

import jax
import jax.numpy as jnp
from jax import lax
from jax.experimental import pallas as pl
from jax.experimental.pallas import tpu as pltpu
from jax.sharding import Mesh
from jax.sharding import PartitionSpec as P

HEADS = 32
HEAD_DIM = 64
ROT = 32
EPS = 1e-05
NEG = -1e30
BF = jnp.bfloat16
F32 = jnp.float32

RANK = ("core", "bz", "by")
ALL = ("hx", "core", "bs", "bz", "by")
Z_LEN = 4
SWAP = [(0, 1), (1, 0)]
UP = [(i, (i + 1) % Z_LEN) for i in range(Z_LEN)]
DOWN = [((i + 1) % Z_LEN, i) for i in range(Z_LEN)]
VMEM_LIMIT = 60 * 1024 * 1024


def around(far):
    return [(i, (i + far) % Z_LEN) for i in range(Z_LEN)]


def swap(value, axis):
    return lax.ppermute(value, axis, SWAP)


def dot_rows(left, right):
    return lax.dot_general(left, right, (((1,), (1,)), ((), ())), preferred_element_type=F32)


def dot_cols(left, right):
    return lax.dot_general(left, right, (((0,), (0,)), ((), ())), preferred_element_type=F32)


def dot(left, right):
    return jnp.dot(left, right, preferred_element_type=F32)


def fence(now, *then):
    return lax.optimization_barrier((tuple(now),) + then)[0]


def ring(value):
    return lax.ppermute(value, "bz", UP)


def flatten(steps):
    return [piece for step in steps for piece in step]


def like(steps, refs):
    refs = list(refs)
    return [[refs.pop(0) for _ in step] for step in steps]


def add_low(left, right):
    return (left.astype(F32) + right.astype(F32)).astype(BF)


def ring_back(total):
    return lax.ppermute(total.astype(BF), "bz", DOWN)


def joined(index, own, other):
    return jnp.where(index == 0, jnp.concatenate([own, other], 0), jnp.concatenate([other, own], 0))


def across(value, far):
    return lax.ppermute(value, "bz", [(i, i ^ far) for i in range(Z_LEN)])


def in_all(value, spread):
    value = value.reshape(1, Z_LEN, 2, 2, 2, -1)
    if spread > 1:
        value = lax.all_gather(value, "bs", axis=0, tiled=True)
    return value.transpose(2, 3, 0, 1, 4, 5).reshape(8 * Z_LEN * spread, -1)


def halved(value, name, axis):
    index = lax.axis_index(name)
    return (
        lax.dynamic_index_in_dim(value, index, axis, keepdims=False),
        lax.dynamic_index_in_dim(value, 1 - index, axis, keepdims=False),
    )


def turn(value, cosine, sine, lane):
    near = jnp.where(
        (lane % HEAD_DIM) < ROT // 2,
        pltpu.roll(value, 128 - ROT // 2, 1),
        pltpu.roll(value, ROT // 2, 1),
    )
    return value * cosine + near * sine


def take_rows(rows_ref, steps, begin):
    for at, pieces in enumerate(steps):

        @pl.when(pl.program_id(0) == begin + at)
        def _(pieces=pieces):
            row = 0
            for piece in pieces:
                rows_ref[row : row + piece.shape[0]] = piece[...]
                row += piece.shape[0]


def by_row(block, lanes, begin=0):
    return pl.BlockSpec((block, lanes), lambda i, *_: (i + begin, 0))


def fixed(*values):
    def spec(value):
        rank = len(value.shape)
        return pl.BlockSpec(value.shape, lambda i, *_: (0,) * rank)

    return [spec(value) for value in values]


def halves(hx, width):
    half = width // 2
    return [pl.ds(pl.multiple_of(at * half, half), half) for at in (hx, 1 - hx)]


def dot_halves(left_ref, hx, own_ref, other_ref):
    own, other = halves(hx, left_ref.shape[1])
    return dot(left_ref[:, own], own_ref[...]) + dot(left_ref[:, other], other_ref[...])


def front_kernel(steps, plane_ref, *refs):
    count = len(flatten(steps))
    pieces, refs = like(steps, refs[:count]), refs[count:]
    gain_ref, shift_ref, own_ref, other_ref, bias_ref, cos_ref, sin_ref = refs[:7]
    h_ref, q_ref, kv_ref, pre_ref, out_ref, mean_ref, scale_ref, x_ref = refs[-8:]
    take_rows(x_ref, pieces, 0)
    x = x_ref[...].astype(F32)
    mean = jnp.mean(x, -1, keepdims=True)
    centred = x - mean
    scale = lax.rsqrt(jnp.mean(centred * centred, -1, keepdims=True) + EPS)
    mean_ref[...] = mean
    scale_ref[...] = scale
    h_ref[...] = (centred * scale * gain_ref[...] + shift_ref[...]).astype(BF)
    linear = dot_halves(h_ref, plane_ref[0], own_ref, other_ref) + bias_ref[...]
    lane = lax.broadcasted_iota(jnp.int32, (x.shape[0], 128), 1)
    cosine, sine = cos_ref[...], sin_ref[...]
    q_ref[...] = turn(linear[:, :128], cosine, sine, lane).astype(BF) * BF(HEAD_DIM**-0.5)
    kv_ref[:, :128] = turn(linear[:, 128:256], cosine, sine, lane).astype(BF)
    kv_ref[:, 128:] = linear[:, 256:384].astype(BF)
    pre = linear[:, 384:]
    pre_ref[...] = pre
    out_ref[...] = (0.5 * pre * (1.0 + jnp.tanh(0.7978845608 * (pre + 0.044715 * pre * pre * pre)))).astype(BF)


def front(plane, pieces, held, gain, shift, own, other, bias, cosine, sine):
    block, width = sum(piece.shape[0] for piece in pieces[0]), gain.shape[1]
    rows = 8 * block
    cols = own.shape[1]
    wide = cols - 384
    flat_pieces = flatten(pieces)
    here = functools.partial(by_row, block, begin=4 if held else 0)
    lanes = (width, 128, 256, wide, wide, 1, 1)
    types = (BF, BF, BF, F32, BF, F32, F32)
    return pl.pallas_call(
        functools.partial(front_kernel, pieces),
        grid_spec=pltpu.PrefetchScalarGridSpec(
            num_scalar_prefetch=1,
            grid=(4,),
            in_specs=fixed(*flat_pieces, gain, shift, own, other, bias)
            + [here(128), here(128)]
            + [pl.BlockSpec(memory_space=pl.ANY)] * len(held),
            out_specs=[here(n) for n in lanes],
            scratch_shapes=[pltpu.VMEM((block, width), BF)],
        ),
        out_shape=[jax.ShapeDtypeStruct((rows, n), kind) for n, kind in zip(lanes, types)],
        input_output_aliases={len(flat_pieces) + 8 + i: i for i in range(len(held))},
        compiler_params=pltpu.CompilerParams(vmem_limit_bytes=VMEM_LIMIT),
        cost_estimate=pl.CostEstimate(
            flops=rows * width * cols + 6 * rows * width, bytes_accessed=rows * width * 3, transcendentals=rows * wide
        ),
    )(plane[None], *flat_pieces, gain, shift, own, other, bias, cosine, sine, *held)


def two_heads(value):
    lane = lax.broadcasted_iota(jnp.int32, value.shape, 1)
    zero = jnp.zeros_like(value)
    return jnp.concatenate([jnp.where(lane < HEAD_DIM, value, zero), jnp.where(lane < HEAD_DIM, zero, value)], 0)


def one_row(value):
    half = value.shape[0] // 2
    lane = lax.broadcasted_iota(jnp.int32, (half, 128), 1)
    return jnp.where(lane < HEAD_DIM, value[:half], value[half:])


def place_in(row, share):
    return ((row & share) << 1) | ((row & (2 * share)) >> 1) | (row & (share - 1))


def allowed_pairs(meta_ref, block, query_at, key_at):
    turned, length = meta_ref[0], meta_ref[1]
    shape = (block, 2 * block)
    row = lax.broadcasted_iota(jnp.int32, shape, 1) & (block - 1)
    query = query_at * block + (place_in(row, block // 4) ^ turned)
    key = key_at * block + (place_in(lax.broadcasted_iota(jnp.int32, shape, 0), block // 4) ^ turned)
    return (key <= query) & (key < length)


def key_ranges(meta_ref, block, query_at):
    length = meta_ref[1]
    plain = jnp.minimum(query_at, length // block)
    last = jnp.minimum(query_at + 1, (length + block - 1) // block)
    return plain, last


def spot_of(at):
    near = 2 * Z_LEN
    spot = lax.rem(at, near)
    return lax.div(at, near) * 2 + lax.div(spot, 4), slice(None), lax.rem(spot, 2), lax.rem(lax.div(spot, 2), 2)


def rows_of(ref, at):
    value = ref[spot_of(at)]
    return value.reshape(value.shape[0] * value.shape[1], value.shape[2])


def add_rows(ref, at, value):
    ref[spot_of(at)] += value.reshape(2, value.shape[0] // 2, value.shape[1])


def flat(ref):
    value = ref[0, :, 0, 0]
    return value.reshape(value.shape[0] * value.shape[1], value.shape[2])


def key_rows(kv_ref, order_ref, at, count):
    return jnp.concatenate([rows_of(kv_ref, order_ref[at + i]) for i in range(count)], 0)


def over_keys(meta_ref, block, query_at, step, state):
    plain, last = key_ranges(meta_ref, block, query_at)
    pairs = plain // 2
    state = lax.fori_loop(0, pairs, lambda i, carried: step(False, 2, 2 * i, carried), state)
    state = lax.fori_loop(2 * pairs, plain, functools.partial(step, False, 1), state)
    return lax.fori_loop(plain, last, functools.partial(step, True, 1), state)


def attend_kernel(block, meta_ref, query_ref, order_ref, q_ref, kv_ref, full_ref, low_ref, lse_ref):
    query_at = query_ref[pl.program_id(0)]
    queries = two_heads(flat(q_ref))

    def step(masked, count, at, state):
        top, total, mixed = state
        both = key_rows(kv_ref, order_ref, at, count)
        scores = dot_rows(both[:, :128], queries)
        if masked:
            allowed = allowed_pairs(meta_ref, block, query_at, at)
            scores = jnp.where(allowed, scores, NEG)
        fresh = jnp.maximum(top, jnp.max(scores, 0, keepdims=True))
        factor = jnp.exp(top - fresh)
        weights = jnp.exp(scores - fresh)
        if masked:
            weights = jnp.where(allowed, weights, 0.0)
        total = total * factor + jnp.sum(weights, 0, keepdims=True)
        return fresh, total, mixed * factor + dot_cols(both[:, 128:], weights.astype(BF))

    state = (
        jnp.full((1, 2 * block), NEG, F32),
        jnp.zeros((1, 2 * block), F32),
        jnp.zeros((128, 2 * block), F32),
    )
    top, total, mixed = over_keys(meta_ref, block, query_at, step, state)
    mixed = mixed / total
    full = jnp.concatenate([mixed[:HEAD_DIM, :block], mixed[HEAD_DIM:, block:]], 0).T
    shape = full_ref.shape[1:2] + full_ref.shape[4:]
    full_ref[0, :, 0, 0] = full.reshape(shape)
    low_ref[0, :, 0, 0] = full.astype(BF).reshape(shape)
    lse_ref[...] = jnp.broadcast_to((top + jnp.log(total))[None], lse_ref.shape)


def placed(share, lanes):
    return pl.BlockSpec((1, 2, 1, 1, 2 * share, lanes), lambda i, *_: (i // 4, 0, i % 2, (i // 2) % 2, 0, 0))


def attend(table, q, kv, share):
    block = 4 * share
    blocks = 2 * Z_LEN
    rows, keys = q.shape[0], kv.shape[0]
    shape = (2, 2, 2, Z_LEN // 2, 2 * share, 128)
    kv_shape = (keys // (4 * Z_LEN * share), 2, 2, Z_LEN // 2, 2 * share, 256)
    full, low, lse = pl.pallas_call(
        functools.partial(attend_kernel, block),
        grid_spec=pltpu.PrefetchScalarGridSpec(
            num_scalar_prefetch=3,
            grid=(blocks,),
            in_specs=[placed(share, 128), pl.BlockSpec(kv_shape, lambda i, *_: (0, 0, 0, 0, 0, 0))],
            out_specs=[placed(share, 128), placed(share, 128), pl.BlockSpec((1, 8, 2 * block), lambda i, *_: (i, 0, 0))],
        ),
        out_shape=[
            jax.ShapeDtypeStruct(shape, F32),
            jax.ShapeDtypeStruct(shape, BF),
            jax.ShapeDtypeStruct((blocks, 8, 2 * block), F32),
        ],
        compiler_params=pltpu.CompilerParams(vmem_limit_bytes=VMEM_LIMIT),
        cost_estimate=pl.CostEstimate(
            flops=16 * rows * keys * 128, bytes_accessed=rows * 128 * 16, transcendentals=rows * keys
        ),
    )(*table, q.reshape(shape), kv.reshape(kv_shape))
    return full, low.reshape(rows, 128), lse


def attend_back_kernel(blocks, block, meta_ref, query_ref, order_ref, q_ref, kv_ref, full_ref, lse_ref, grad_ref, dq_ref, dkv_ref, dk_acc, dv_acc):
    at_block = pl.program_id(0)
    query_at = query_ref[at_block]
    queries = two_heads(flat(q_ref))
    grads = two_heads(flat(grad_ref))
    full = flat(full_ref)
    delta = jnp.sum(grads.astype(F32) * jnp.concatenate([full, full], 0), -1, keepdims=True)
    delta = jnp.broadcast_to(delta, (2 * block, 128)).T[:1]
    lse = lse_ref[0, :1]

    @pl.when(at_block == 0)
    def _():
        dk_acc[...] = jnp.zeros_like(dk_acc)
        dv_acc[...] = jnp.zeros_like(dv_acc)

    def step(masked, count, at, grad_query):
        both = key_rows(kv_ref, order_ref, at, count)
        keys = both[:, :128]
        scores = dot_rows(keys, queries)
        if masked:
            allowed = allowed_pairs(meta_ref, block, query_at, at)
            scores = jnp.where(allowed, scores, NEG)
        weights = jnp.exp(scores - lse)
        if masked:
            weights = jnp.where(allowed, weights, 0.0)
        grad_scores = (weights * (dot_rows(both[:, 128:], grads) - delta)).astype(BF)
        grad_keys = dot(grad_scores, queries)
        grad_values = dot(weights.astype(BF), grads)
        for i in range(count):
            spot = order_ref[at + i]
            add_rows(dk_acc, spot, grad_keys[i * block : (i + 1) * block])
            add_rows(dv_acc, spot, grad_values[i * block : (i + 1) * block])
        return grad_query + dot_cols(grad_scores, keys)

    grad_query = over_keys(meta_ref, block, query_at, step, jnp.zeros((2 * block, 128), F32))
    shape = dq_ref.shape[1:2] + dq_ref.shape[4:]
    dq_ref[0, :, 0, 0] = (one_row(grad_query) * HEAD_DIM**-0.5).astype(BF).reshape(shape)

    @pl.when(at_block == blocks - 1)
    def _():
        dkv_ref[..., :128] = dk_acc[...].astype(BF)
        dkv_ref[..., 128:] = dv_acc[...].astype(BF)


def attend_back(table, q, kv, full, lse, grad, share):
    block = 4 * share
    blocks = 2 * Z_LEN
    rows, keys = q.shape[0], kv.shape[0]
    shape = (2, 2, 2, Z_LEN // 2, 2 * share, 128)
    kv_shape = (keys // (4 * Z_LEN * share), 2, 2, Z_LEN // 2, 2 * share, 256)
    kv_spec = pl.BlockSpec(kv_shape, lambda i, *_: (0, 0, 0, 0, 0, 0))
    dq, dkv = pl.pallas_call(
        functools.partial(attend_back_kernel, blocks, block),
        grid_spec=pltpu.PrefetchScalarGridSpec(
            num_scalar_prefetch=3,
            grid=(blocks,),
            in_specs=[
                placed(share, 128),
                kv_spec,
                placed(share, 128),
                pl.BlockSpec((1, 8, 2 * block), lambda i, *_: (i, 0, 0)),
                placed(share, 128),
            ],
            out_specs=[placed(share, 128), kv_spec],
            scratch_shapes=[pltpu.VMEM(kv_shape[:-1] + (128,), F32), pltpu.VMEM(kv_shape[:-1] + (128,), F32)],
        ),
        out_shape=[jax.ShapeDtypeStruct(shape, BF), jax.ShapeDtypeStruct(kv_shape, BF)],
        compiler_params=pltpu.CompilerParams(vmem_limit_bytes=VMEM_LIMIT),
        cost_estimate=pl.CostEstimate(
            flops=40 * rows * keys * 128, bytes_accessed=rows * 128 * 24, transcendentals=rows * keys
        ),
    )(*table, q.reshape(shape), kv.reshape(kv_shape), full, lse, grad.reshape(shape))
    return dq.reshape(rows, 128), dkv.reshape(keys, 256)


def store_parts(parts, total_ref):
    for at in range(8):
        half, core, ky = at // 4, at // 2 % 2, at % 2

        @pl.when(pl.program_id(0) == at)
        def _(ref=parts[4 * (1 - core) + 2 * (1 - ky) + half]):
            ref[...] = total_ref[...]


def part_shapes(rows, width):
    return [jax.ShapeDtypeStruct((rows, width), BF)] * 8


def out_kernel(plane_ref, attn_ref, units_ref, dense_ref, own_ref, other_ref, *refs):
    parts, total_ref = refs[:-1], refs[-1]
    attn, units = attn_ref[...], units_ref[...]
    for part, weight_ref in zip(halves(plane_ref[0], total_ref.shape[1]), (own_ref, other_ref)):
        total_ref[:, part] = (dot(attn, dense_ref[:, part]) + dot_rows(units, weight_ref[...])).astype(BF)
    store_parts(parts, total_ref)


def out_partial(plane, attn, units, dense, own, other, block):
    rows, width = attn.shape[0], dense.shape[1]
    wide = units.shape[1]
    shapes = part_shapes(block, width)
    return pl.pallas_call(
        out_kernel,
        grid_spec=pltpu.PrefetchScalarGridSpec(
            num_scalar_prefetch=1,
            grid=(rows // block,),
            in_specs=[by_row(block, 128), by_row(block, wide)] + fixed(dense, own, other),
            out_specs=fixed(*shapes),
            scratch_shapes=[pltpu.VMEM((block, width), BF)],
        ),
        out_shape=shapes,
        compiler_params=pltpu.CompilerParams(vmem_limit_bytes=VMEM_LIMIT),
        cost_estimate=pl.CostEstimate(
            flops=2 * rows * width * (128 + wide), bytes_accessed=2 * rows * width, transcendentals=0
        ),
    )(plane[None], attn, units, dense, own, other)


def branch_kernel(steps, plane_ref, *refs):
    count = len(flatten(steps))
    pieces, refs = like(steps, refs[:count]), refs[count:]
    dense_ref, own_ref, other_ref, pre_ref, attn_ref, grad_ref, g_ref = refs
    take_rows(g_ref, pieces, 0)
    attn_ref[...] = dot_rows(g_ref[...], dense_ref[...]).astype(BF)
    grad = dot_halves(g_ref, plane_ref[0], own_ref, other_ref)
    u = pre_ref[...]
    square = u * u
    bend = jnp.tanh(0.7978845608 * u * (1.0 + 0.044715 * square))
    slope = 0.5 * (1.0 + bend) + 0.5 * u * (1.0 - bend * bend) * (0.7978845608 * (1.0 + 3 * 0.044715 * square))
    grad_ref[...] = (grad * slope).astype(BF)


def branch_grads(plane, pieces, dense, own, other, pre, block):
    width = dense.shape[1]
    rows, wide = pre.shape
    flat_pieces = flatten(pieces)
    return pl.pallas_call(
        functools.partial(branch_kernel, pieces),
        grid_spec=pltpu.PrefetchScalarGridSpec(
            num_scalar_prefetch=1,
            grid=(rows // block,),
            in_specs=fixed(*flat_pieces, dense, own, other) + [by_row(block, wide)],
            out_specs=[by_row(block, 128), by_row(block, wide), by_row(block, width)],
        ),
        out_shape=[
            jax.ShapeDtypeStruct((rows, 128), BF),
            jax.ShapeDtypeStruct((rows, wide), BF),
            jax.ShapeDtypeStruct((rows, width), BF),
        ],
        compiler_params=pltpu.CompilerParams(vmem_limit_bytes=VMEM_LIMIT),
        cost_estimate=pl.CostEstimate(
            flops=2 * rows * width * (128 + wide), bytes_accessed=rows * width * 4, transcendentals=rows * wide
        ),
    )(plane[None], *flat_pieces, dense, own, other, pre)


def turn_back(value, cosine, sine, lane):
    return turn(value.astype(F32), cosine, -sine, lane).astype(BF)


def back_kernel(steps, plane_ref, *refs):
    count = len(flatten(steps))
    pieces, refs = like(steps, refs[:count]), refs[count:]
    linear_ref, units_ref, own_ref, other_ref, mean_ref, scale_ref = refs[:6]
    parts, (gain_ref, shift_ref, small_ref, x_ref, total_ref) = refs[6:14], refs[14:]
    take_rows(x_ref, pieces, 0)
    linear, units = linear_ref[...], units_ref[...]

    @pl.when(pl.program_id(0) == 0)
    def _():
        gain_ref[...] = jnp.zeros_like(gain_ref)
        shift_ref[...] = jnp.zeros_like(shift_ref)
        small_ref[...] = jnp.zeros_like(small_ref)

    small_ref[:, :384] += jnp.sum(linear.astype(F32), 0, keepdims=True)
    small_ref[:, 384:] += jnp.sum(units.astype(F32), 0, keepdims=True)
    mean, scale = mean_ref[...], scale_ref[...]
    for part, weight_ref in zip(halves(plane_ref[0], total_ref.shape[1]), (own_ref, other_ref)):
        total = dot_rows(linear, weight_ref[:, :384]) + dot_rows(units, weight_ref[:, 384:])
        total_ref[:, part] = total.astype(BF)
        gain_ref[:, part] += jnp.sum(total * ((x_ref[:, part].astype(F32) - mean) * scale), 0, keepdims=True)
        shift_ref[:, part] += jnp.sum(total, 0, keepdims=True)
    store_parts(parts, total_ref)


def back_partial(plane, pieces, linear, units, own, other, mean, scale):
    rows = linear.shape[0]
    block = sum(piece.shape[0] for piece in pieces[0])
    width, cols = 2 * own.shape[0], own.shape[1]
    flat_pieces = flatten(pieces)
    shapes = part_shapes(block, width)
    sums = [jax.ShapeDtypeStruct((1, n), F32) for n in (width, width, cols)]
    *parts, gain, shift, small = pl.pallas_call(
        functools.partial(back_kernel, pieces),
        grid_spec=pltpu.PrefetchScalarGridSpec(
            num_scalar_prefetch=1,
            grid=(rows // block,),
            in_specs=fixed(*flat_pieces)
            + [by_row(block, 384), by_row(block, cols - 384)]
            + fixed(own, other)
            + [by_row(block, 1), by_row(block, 1)],
            out_specs=fixed(*shapes) + fixed(*sums),
            scratch_shapes=[pltpu.VMEM((block, width), BF), pltpu.VMEM((block, width), BF)],
        ),
        out_shape=shapes + sums,
        compiler_params=pltpu.CompilerParams(vmem_limit_bytes=VMEM_LIMIT),
        cost_estimate=pl.CostEstimate(
            flops=2 * rows * width * cols, bytes_accessed=4 * rows * width, transcendentals=0
        ),
    )(plane[None], *flat_pieces, linear, units, own, other, mean, scale)
    return parts, (gain, shift, small)


def weight_kernel(plane_ref, *refs):
    *pairs, away_ref, mine_ref = refs
    for out_ref, this in ((away_ref, pl.program_id(0) < 2), (mine_ref, pl.program_id(0) >= 2)):

        @pl.when(this)
        def _(out_ref=out_ref):
            begin = 0
            for left, right in zip(pairs[::2], pairs[1::2]):
                end = begin + right.shape[1]
                value = dot_cols(left[...], right[...]).astype(BF)
                out_ref[:, 0, :, begin:end] = value.reshape(out_ref.shape[0], out_ref.shape[2], end - begin)
                begin = end


def weight_rows(rows, quarter):
    return pl.BlockSpec((rows, quarter), lambda i, p: (0, ((p[0] + 1 - i // 2) % 2) * 2 + i % 2))


def weight_shape(quarter, cols):
    return jax.ShapeDtypeStruct((Z_LEN, 2, quarter // Z_LEN, cols), BF)


def weight_outs(quarter, cols):
    shape = (Z_LEN, 1, quarter // Z_LEN, cols)
    return [
        pl.BlockSpec(shape, lambda i, p: (0, jnp.minimum(i, 1), 0, 0)),
        pl.BlockSpec(shape, lambda i, p: (0, jnp.maximum(i - 2, 0), 0, 0)),
    ]


def weight_grads(plane, *pairs):
    rows, width = pairs[0][0].shape
    cols = sum(right.shape[1] for _, right in pairs)
    quarter = width // 4
    out = weight_shape(quarter, cols)
    specs = [spec for _, right in pairs for spec in (weight_rows(rows, quarter), *fixed(right))]
    return pl.pallas_call(
        weight_kernel,
        grid_spec=pltpu.PrefetchScalarGridSpec(
            num_scalar_prefetch=1,
            grid=(4,),
            in_specs=specs,
            out_specs=weight_outs(quarter, cols),
        ),
        out_shape=[out, out],
        compiler_params=pltpu.CompilerParams(vmem_limit_bytes=VMEM_LIMIT),
        cost_estimate=pl.CostEstimate(
            flops=2 * rows * width * cols, bytes_accessed=2 * rows * width, transcendentals=0
        ),
    )(plane[None], *[value for pair in pairs for value in pair])


def triple_grads_kernel(plane_ref, h_ref, dq_ref, dkv_ref, cos_ref, sin_ref, away_ref, mine_ref, linear_ref):
    @pl.when(pl.program_id(0) == 0)
    def _():
        rows = 256

        def step(at, carry):
            here = pl.ds(pl.multiple_of(at * rows, rows), rows)
            lane = lax.broadcasted_iota(jnp.int32, (rows, 128), 1)
            cosine, sine = cos_ref[here, :], sin_ref[here, :]
            linear_ref[here, :128] = turn_back(dq_ref[here, :], cosine, sine, lane)
            linear_ref[here, 128:256] = turn_back(dkv_ref[here, :128], cosine, sine, lane)
            linear_ref[here, 256:] = dkv_ref[here, 128:]
            return carry

        lax.fori_loop(0, dq_ref.shape[0] // rows, step, 0)

    weight_kernel(plane_ref, h_ref, linear_ref, away_ref, mine_ref)


def triple_grads(plane, h, dq, dkv, cosine, sine):
    rows, width = h.shape
    quarter = width // 4
    out = weight_shape(quarter, 384)
    linear = jax.ShapeDtypeStruct((rows, 384), BF)
    return pl.pallas_call(
        triple_grads_kernel,
        grid_spec=pltpu.PrefetchScalarGridSpec(
            num_scalar_prefetch=1,
            grid=(4,),
            in_specs=[weight_rows(rows, quarter)] + fixed(dq, dkv, cosine, sine),
            out_specs=weight_outs(quarter, 384) + fixed(linear),
        ),
        out_shape=[out, out, linear],
        compiler_params=pltpu.CompilerParams(vmem_limit_bytes=VMEM_LIMIT),
        cost_estimate=pl.CostEstimate(
            flops=2 * rows * width * 384, bytes_accessed=2 * rows * width, transcendentals=0
        ),
    )(plane[None], h, dq, dkv, cosine, sine)


def pack_kernel(triple_ref, expand_ref, shrink_ref, in_ref, out_ref):
    ranks, wide = in_ref.shape[0], out_ref.shape[2]
    for rank in range(ranks):
        for s in range(3):
            pair = [triple_ref[:, pl.ds((s * HEADS + x * ranks + rank) * HEAD_DIM, HEAD_DIM)] for x in range(2)]
            in_ref[rank, :, s * 128 : (s + 1) * 128] = jnp.concatenate(pair, 1)
        in_ref[rank, :, 384:] = expand_ref[:, rank * wide : (rank + 1) * wide]
        out_ref[rank] = shrink_ref[:, rank * wide : (rank + 1) * wide]


def pack(triple, expand, shrink, ranks):
    held = triple.shape[0]
    wide = expand.shape[1] // ranks
    return pl.pallas_call(
        pack_kernel,
        out_shape=[
            jax.ShapeDtypeStruct((ranks, held, 384 + wide), BF),
            jax.ShapeDtypeStruct((ranks, held, wide), BF),
        ],
        compiler_params=pltpu.CompilerParams(vmem_limit_bytes=VMEM_LIMIT),
    )(triple, expand, shrink)


def unpack_units_kernel(place_ref, *refs):
    units, (shrink_ref, expand_ref) = refs[:4], refs[4:]
    core, by = place_ref[0], place_ref[1]
    wide = units[0].shape[2] // 2
    for away in range(2):
        for bz in range(Z_LEN):
            first = jnp.bitwise_xor(core, away) * 2 * Z_LEN + bz * 2
            for across_y in range(2):
                value = units[2 * away + across_y][bz].astype(F32)
                at = pl.ds(pl.multiple_of((first + jnp.bitwise_xor(by, across_y)) * wide, wide), wide)
                shrink_ref[:, at] = value[:, :wide]
                expand_ref[:, at] = value[:, wide:]


def unpack_triple_kernel(place_ref, *refs):
    triples, triple_ref = refs[:4], refs[4]
    core, by = place_ref[0], place_ref[1]
    for away in range(2):
        for bz in range(Z_LEN):
            first = jnp.bitwise_xor(core, away) * 2 * Z_LEN + bz * 2
            own, other = triples[2 * away][bz].astype(F32), triples[2 * away + 1][bz].astype(F32)
            low, high = jnp.where(by == 0, own, other), jnp.where(by == 0, other, own)
            for s in range(3):
                for x in range(2):
                    lanes = slice(s * 128 + x * HEAD_DIM, s * 128 + (x + 1) * HEAD_DIM)
                    at = pl.multiple_of((s * HEADS + x * 4 * Z_LEN + first) * HEAD_DIM, 128)
                    triple_ref[:, pl.ds(at, 128)] = jnp.concatenate([low[:, lanes], high[:, lanes]], 1)


def unpack(kernel, widths, core, by, pieces):
    shapes = [jax.ShapeDtypeStruct((pieces[0].shape[1], width), F32) for width in widths]
    return pl.pallas_call(
        kernel,
        grid_spec=pltpu.PrefetchScalarGridSpec(
            num_scalar_prefetch=1,
            grid=(1,),
            in_specs=fixed(*pieces),
            out_specs=fixed(*shapes),
        ),
        out_shape=shapes,
        compiler_params=pltpu.CompilerParams(vmem_limit_bytes=VMEM_LIMIT),
    )(jnp.where(jnp.arange(2) == 0, core, by).astype(jnp.int32), *pieces)


def turn_tables(positions):
    half = ROT // 2
    inverse = 10000.0 ** (-(jnp.arange(half, dtype=F32) * 2.0) / ROT)
    angles = positions.astype(F32)[:, None] * inverse[None, :]
    cosine, sine = jnp.cos(angles), jnp.sin(angles)
    rest = (positions.shape[0], HEAD_DIM - ROT)
    cosine = jnp.concatenate([cosine, cosine, jnp.ones(rest, F32)], 1)
    sine = jnp.concatenate([-sine, sine, jnp.zeros(rest, F32)], 1)
    return jnp.tile(cosine, (1, 2)), jnp.tile(sine, (1, 2))


def core_pair(own, other, core):
    return jnp.where(core == 0, jnp.stack([own, other], 1), jnp.stack([other, own], 1))


def body(
    inputs,
    norm_gain,
    norm_bias,
    triple_weight,
    triple_bias,
    dense_weight,
    dense_bias,
    expand_weight,
    expand_bias,
    shrink_weight,
    shrink_bias,
    lengths,
    block_order,
    cotangent,
):
    share, width = inputs.shape[2], inputs.shape[3]
    hx, core, bs, bz, by = (lax.axis_index(name) for name in ALL)
    spread = lax.axis_size("bs")
    ranks = 2 * Z_LEN * 2
    devices = 2 * ranks * spread
    block = 4 * share
    rows = ranks * 2 * share
    near_blocks = Z_LEN * 2
    blocks = block_order.shape[0]
    held = width // devices
    ff = expand_weight.shape[1]
    ff_here = ff // ranks
    length = lengths[hx]

    def block_at(index):
        return jnp.sum(jnp.where(jnp.arange(blocks, dtype=jnp.int32) == index, block_order, 0))

    token_pos = (
        block_at(bs * near_blocks + bz * 2 + by) * block
        + (hx * 2 + core) * share
        + jnp.arange(share, dtype=jnp.int32)
    )
    valid = (token_pos[None, :] < lengths[:, None]).astype(F32)[:, :, None]

    spots = jnp.arange(blocks, dtype=jnp.int32)
    within = spots % near_blocks
    index = spots - within + ((bz + Z_LEN - within // 2) % Z_LEN) * 2 + (by + within) % 2
    key_at = jnp.sum(jnp.where(index[:, None] == spots[None, :], block_order[None, :], 0), 1)
    query_at = lax.dynamic_slice_in_dim(key_at, bs * near_blocks, near_blocks)
    turned = hx * 2 * share + core * share
    inside = place_in(jnp.arange(block, dtype=jnp.int32), share) ^ turned
    block_pos = query_at.reshape(2, Z_LEN // 2, 2).transpose(0, 2, 1)[:, None, :, :, None]
    row_pos = (block_pos * block + inside.reshape(1, 2, 1, 1, 2 * share)).reshape(rows)
    order = jnp.sum(jnp.where(key_at[None, :] == spots[:, None], spots[None, :], 0), 1)
    table = jnp.where(jnp.arange(2) == 0, turned, length).astype(jnp.int32), query_at, order
    cosine, sine = turn_tables(row_pos)

    def to_cols(sent):
        cols = sent.shape[2]
        got = lax.all_to_all(sent, RANK, split_axis=0, concat_axis=0, tiled=True)
        if spread > 1:
            got = lax.all_gather(got.reshape(2, 1, near_blocks, held, cols), "bs", axis=1, tiled=True)
        return got.reshape(width // 2, cols)

    def to_rows_z(mine):
        cols = mine.shape[-1]
        got = lax.all_to_all(mine, "bz", split_axis=0, concat_axis=0, tiled=True)
        return got.reshape(Z_LEN, 2, 2, held, cols)

    def over_bs(mine):
        if spread == 1:
            return mine
        cols = mine.shape[-1]
        mine = mine.transpose(1, 0, 2, 3).reshape(2, spread, Z_LEN, 2 * held, cols)
        mine = lax.psum_scatter(mine, "bs", scatter_dimension=1, tiled=True)
        return mine.reshape(2, Z_LEN, 2 * held, cols).transpose(1, 0, 2, 3)

    def split(value, index, axis):
        return (
            lax.dynamic_index_in_dim(value, index, axis, keepdims=False),
            lax.dynamic_index_in_dim(value, 1 - index, axis, keepdims=False),
        )

    def both(low, high):
        return jnp.concatenate([low, high], 0)

    x_a = lax.dynamic_index_in_dim(inputs[:, 0], hx, 0, keepdims=False)
    x_b = lax.dynamic_index_in_dim(inputs[:, 0], 1 - hx, 0, keepdims=False)
    vectors = (norm_gain, norm_bias, triple_bias, expand_bias, dense_bias, shrink_bias)
    sent_in, sent_out = pack(triple_weight, expand_weight, shrink_weight, ranks)

    sent_in, sent_out, vectors, cotangent, x_b = fence((sent_in, sent_out, vectors, cotangent, x_b))
    in_own = to_cols(sent_in)
    x_b = swap(x_b, "hx")
    small = jnp.concatenate(vectors)[None]
    x_0 = both(x_a, x_b)
    grad_y = (cotangent[:, 0].astype(F32) * valid).astype(BF)
    g_a = lax.dynamic_index_in_dim(grad_y, hx, 0, keepdims=False)
    g_b = swap(lax.dynamic_index_in_dim(grad_y, 1 - hx, 0, keepdims=False), "hx")
    small = joined(by, small, swap(small, "by"))
    small = joined(core, small, swap(small, "core"))
    more = swap(small, "hx")

    x_0, in_own, g_b, small, more, row_pos = fence((x_0, in_own, g_b, small, more, row_pos), table)
    in_other = swap(in_own, "hx")
    small = joined(hx, small, more)

    x_0, small, row_pos = fence((x_0, small, row_pos))
    y_0 = swap(x_0, "by")
    x_1 = ring(x_0)
    g_0 = both(g_a, g_b)
    more = across(small, 1)
    cosine, sine = turn_tables(row_pos)

    y_0, x_1, g_0, small, more, cosine, sine = fence((y_0, x_1, g_0, small, more, cosine, sine))
    y_1 = swap(x_1, "by")
    x_2 = ring(x_1)
    small = joined(bz % 2, small, more)
    more = across(small, 2)

    y_1, x_2, small, more = fence((y_1, x_2, small, more))
    y_2 = swap(x_2, "by")
    x_3 = ring(x_2)
    own_one, y_one = both(x_0, x_1), both(y_0, y_1)
    c_one = swap(own_one, "core"), swap(y_one, "core")
    small = in_all(joined(bz // 2, small, more), spread)

    cuts = [0]
    for leaf in (norm_gain, norm_bias, triple_bias, expand_bias, dense_bias, shrink_bias):
        cuts.append(cuts[-1] + leaf.shape[0])
    gain, shift, triple_b, expand_b, dense_b, shrink_b = (
        small[:, low:high].reshape(-1).astype(F32) for low, high in zip(cuts[:-1], cuts[1:])
    )
    rank = core * near_blocks + bz * 2 + by
    bias_triple = lax.dynamic_index_in_dim(
        triple_b.reshape(3, 2, ranks, HEAD_DIM).transpose(2, 0, 1, 3).reshape(ranks, 384), rank, 0
    )
    bias_expand = lax.dynamic_index_in_dim(expand_b.reshape(ranks, ff_here), rank, 0)
    bias_in = jnp.concatenate([bias_triple, bias_expand], 1)

    y_2, x_3, c_one, in_other, bias_in = fence((y_2, x_3, c_one, in_other, bias_in))
    y_3 = swap(x_3, "by")
    g_1 = ring(g_0)
    own_two = both(x_2, x_3)
    c_two = (swap(own_two, "core"),)
    x_one = ((own_one,), (y_one,), (c_one[0],), (c_one[1],))
    into = (gain[None], shift[None], in_own, in_other, bias_in, cosine, sine)
    held_one = front(hx, x_one, (), *into)

    held_one, y_3, g_1, c_two, sent_out = fence((held_one, y_3, g_1, c_two, sent_out))
    y_two = both(y_2, y_3)
    out_own = to_cols(sent_out)
    c_two = c_two[0], swap(y_two, "core")

    held_one, c_two = fence((held_one, c_two))
    x_two = ((own_two,), (y_two,), (c_two[0],), (c_two[1],))
    h, q, kv, pre, expand_out, mean, scale = front(hx, x_two, held_one, *into)

    q, g_0, g_1, out_own = fence((q, g_0, g_1, out_own))
    out_other = swap(out_own, "hx")
    own_one = both(g_0, g_1)
    y_one = swap(own_one, "by")
    g_2 = ring(g_1)
    g_3 = lax.ppermute(g_0, "bz", around(3))
    kv_all = kv if spread == 1 else lax.all_gather(kv, "bs", axis=0, tiled=True)
    attn_full, attn_low, lse = attend(table, q, kv_all, share)
    if spread == 1:
        dense_away = swap(dense_weight, "hx")
        dense_pair = jnp.where(hx == 0, both(dense_weight, dense_away), both(dense_away, dense_weight))
    else:
        dense_all = lax.all_gather(dense_weight, ALL, axis=0, tiled=True).reshape(2, ranks, HEAD_DIM, width)
        dense_pair = lax.dynamic_index_in_dim(dense_all, rank, 1, keepdims=False).reshape(128, width)

    attn_low, y_one, g_2, g_3, own_one, out_other, dense_pair = fence(
        (attn_low, y_one, g_2, g_3, own_one, out_other, dense_pair)
    )
    own_two = both(g_2, g_3)
    y_two = swap(own_two, "by")
    c_one = swap(own_one, "core"), swap(y_one, "core")
    c_two = (swap(own_two, "core"),)
    onto = (dense_pair, out_own, out_other)
    out_parts = out_partial(hx, attn_low, expand_out, *onto, block)

    y_two, c_one, c_two, out_parts = fence((y_two, c_one, c_two, out_parts))
    g_one = own_one, y_one
    c_two = c_two[0], swap(y_two, "core")
    g_pieces = tuple((piece,) for piece in g_one + c_one + (own_two, y_two) + c_two)

    out_parts, g_pieces = fence((out_parts, g_pieces))
    got = [swap(part, "core") for part in out_parts[:4]]
    grad_attention, grad_pre, g_all = branch_grads(hx, g_pieces, *onto, pre, block)

    grad_attention, grad_pre, g_all, got = fence((grad_attention, grad_pre, g_all, got))
    far = add_low(both(*out_parts[4:6]), both(*got[:2]))

    grad_attention, grad_pre, g_all, far = fence((grad_attention, grad_pre, g_all, far))
    out_y = swap(far, "by")
    units_away, units_mine = weight_grads(hx, (g_all, expand_out), (h, grad_pre))

    grad_attention, units_away = fence((grad_attention, units_away))
    units_away = swap(units_away, "hx")
    dq, dkv = attend_back(table, q, kv_all, attn_full, lse, grad_attention, share)
    if spread > 1:
        dkv = lax.psum_scatter(dkv, "bs", scatter_dimension=0, tiled=True)

    def three(k, near_part, got_part, y_part):
        rows = slice(k * 2 * share, (k + 1) * 2 * share)
        return near_part[rows].astype(F32) + got_part[rows].astype(F32) + y_part[rows].astype(F32)

    def out_three(kz):
        half = kz // 2
        return three(kz % 2, out_parts[6 + half], got[2 + half], out_y[half * block : (half + 1) * block])

    dq, out_y, out_parts, got = fence((dq, out_y, out_parts, got))
    out_sum = out_three(3)

    dq, out_sum = fence((dq, out_sum))
    ringed = ring_back(out_sum)
    triple_away, triple_mine, grad_linear = triple_grads(hx, h, dq, dkv, cosine, sine)

    units_away, triple_away, grad_linear, ringed = fence((units_away, triple_away, grad_linear, ringed))
    mine = add_low(units_mine, units_away)

    mine, triple_away, grad_linear = fence((mine, triple_away, grad_linear))
    units_rows = to_rows_z(over_bs(mine))
    triple_away = swap(triple_away, "hx")
    h_parts, sums = back_partial(hx, x_one + x_two, grad_linear, grad_pre, in_own, in_other, mean, scale)

    h_parts, sums, triple_away, ringed, g_all = fence((h_parts, sums, triple_away, ringed, g_all))
    h_got = [swap(part, "core") for part in h_parts[:4]]
    mine = add_low(triple_mine, triple_away)
    grad_dense_here = dot_cols(g_all, attn_low)
    out_sum = out_three(2) + ringed

    sum_gain, sum_shift, sum_in = sums
    here = jnp.arange(ranks, dtype=jnp.int32)[:, None] == rank
    sum_triple = (
        jnp.where(here, sum_in[:, :384], 0.0)
        .reshape(ranks, 3, 2, HEAD_DIM)
        .transpose(1, 2, 0, 3)
        .reshape(3 * width)
    )
    sum_expand = jnp.where(here, sum_in[:, 384:], 0.0).reshape(ff)
    sum_y = jnp.sum(grad_y.astype(F32), (0, 1))
    pieces = [leaf.reshape(devices, -1) for leaf in (sum_gain, sum_shift, sum_triple, sum_expand, sum_y)]
    small = jnp.concatenate(pieces, 1).reshape(2, 2, spread, Z_LEN, 2, -1)


    h_got, units_rows, out_sum, small, mine = fence((h_got, units_rows, out_sum, small, mine), grad_dense_here)
    far_one, far_two = add_low(h_parts[4], h_got[0]), add_low(h_parts[5], h_got[1])

    far_one, far_two, out_sum, small, mine = fence((far_one, far_two, out_sum, small, mine))
    h_y_two = swap(far_two, "by")
    triple_rows = to_rows_z(over_bs(mine))
    ringed = ring_back(out_sum)
    small, away = halved(small, "core", 1)

    h_y_two, far_one, small, away, ringed, triple_rows = fence((h_y_two, far_one, small, away, ringed, triple_rows))
    h_sum = three(1, h_parts[7], h_got[3], h_y_two)
    out_sum = out_three(1) + ringed

    h_sum, far_one, small, away, out_sum = fence((h_sum, far_one, small, away, out_sum))
    h_y_one = swap(far_one, "by")
    ringed, out_ringed = ring_back(h_sum), ring_back(out_sum)
    away = swap(away, "core")
    units_parts, triple_parts = split(units_rows, by, 2), split(triple_rows, by, 2)

    h_y_one, ringed, out_ringed, small, away, units_parts, triple_parts = fence(
        (h_y_one, ringed, out_ringed, small, away, units_parts, triple_parts)
    )
    h_sum = three(0, h_parts[7], h_got[3], h_y_two) + ringed
    out_sum = (out_three(0) + out_ringed).reshape(2, share, width)
    out_away = out_sum[1].astype(BF)
    small, away = halved(small + away, "hx", 0)

    h_sum, out_sum, out_away, small, away, units_parts = fence((h_sum, out_sum, out_away, small, away, units_parts))
    ringed = ring_back(h_sum)
    units_got = swap(units_parts[1], "by")
    out_away = swap(out_away, "hx")
    away = swap(away, "hx")
    h_last = [three(at, h_parts[6], h_got[2], h_y_one) for at in (0, 1)]

    ringed, out_away, small, away, h_last, units_got = fence((ringed, out_away, small, away, h_last, units_got))
    h_sum = h_last[1] + ringed
    small, away = halved(small + away, "by", 2)

    h_sum, small, away, triple_parts, units_got = fence((h_sum, small, away, triple_parts, units_got))
    ringed = ring_back(h_sum)
    triple_got = swap(triple_parts[1], "by")
    units_own, units_away = split(jnp.stack([units_parts[0], units_got]), core, 2)
    units_away = swap(units_away, "core")
    grad_shrink, grad_expand = unpack(unpack_units_kernel, (ff, ff), core, by, (*units_own, *units_away))
    small = small + swap(away, "by")
    terms = [lax.dynamic_index_in_dim(small, (bz + kz) % Z_LEN, 1, keepdims=False) for kz in range(Z_LEN)]
    terms = terms[:1] + [lax.ppermute(terms[kz], "bz", around(kz)) for kz in range(1, Z_LEN)]

    source = inputs[:, 0].astype(F32)
    out_away = out_away.astype(F32)
    mixed = jnp.where(hx == 0, jnp.stack([out_sum[0], out_away]), jnp.stack([out_away, out_sum[0]]))
    output = (valid * (source + mixed + dense_b + shrink_b)).astype(BF).reshape(inputs.shape)

    ringed, terms, output, triple_got = fence((ringed, terms, output, triple_got), grad_shrink, grad_expand)
    triple_own, triple_away = split(jnp.stack([triple_parts[0], triple_got]), core, 2)
    triple_away = swap(triple_away, "core")
    (grad_triple,) = unpack(unpack_triple_kernel, (3 * width,), core, by, (*triple_own, *triple_away))
    h_sum = (h_last[0] + ringed).reshape(2, share, width)

    dense_grads = grad_dense_here.T.reshape(2, HEAD_DIM, width)
    if spread == 1:
        dense_mine = lax.dynamic_index_in_dim(dense_grads, hx, 0, keepdims=False)
        dense_away = lax.dynamic_index_in_dim(dense_grads, 1 - hx, 0, keepdims=False)
        grad_dense = dense_mine + swap(dense_away.astype(BF), "hx").astype(F32)
    else:
        spot = jnp.arange(ranks, dtype=jnp.int32)[None, :, None, None] == rank
        dense_whole = jnp.where(spot, dense_grads[:, None], 0.0).reshape(width, width)
        grad_dense = lax.psum_scatter(dense_whole, ALL, scatter_dimension=0, tiled=True)

    small = sum(terms)
    if spread > 1:
        small = lax.psum_scatter(small, "bs", scatter_dimension=0, tiled=True)
    small = small.reshape(-1)
    small_grads = []
    begin = 0
    for piece in pieces:
        small_grads.append(small[begin : begin + piece.shape[1]])
        begin += piece.shape[1]
    small_gain, small_shift, small_triple, small_expand, small_out = small_grads

    h_away = swap(h_sum[1].astype(BF), "hx").astype(F32)
    grad_h = jnp.where(hx == 0, jnp.stack([h_sum[0], h_away]), jnp.stack([h_away, h_sum[0]]))
    centred = source - jnp.mean(source, -1, keepdims=True)
    scale = lax.rsqrt(jnp.mean(centred * centred, -1, keepdims=True) + EPS)
    normed = centred * scale
    g = grad_h * gain
    grad_source = scale * (
        g - jnp.mean(g, -1, keepdims=True) - normed * jnp.mean(g * normed, -1, keepdims=True)
    )
    grad_inputs = (grad_y.astype(F32) + grad_source).astype(BF).reshape(inputs.shape)
    return (
        output,
        grad_inputs,
        small_gain,
        small_shift,
        grad_triple,
        small_triple,
        grad_dense,
        small_out,
        grad_expand,
        small_expand,
        grad_shrink,
        small_out,
    )


def solution(mesh):
    head, blk = mesh.devices.shape
    split = Mesh(mesh.devices.reshape(head // 2, 2, blk // (2 * Z_LEN), Z_LEN, 2), ALL)
    tokens = P(None, ("bs", "bz", "by"), ("hx", "core"), None)
    vector = P(ALL)
    matrix = P(ALL, None)
    return jax.shard_map(
        body,
        mesh=split,
        in_specs=(
            tokens,
            vector,
            vector,
            matrix,
            vector,
            matrix,
            vector,
            matrix,
            vector,
            matrix,
            vector,
            P(),
            P(),
            tokens,
        ),
        out_specs=(
            tokens,
            tokens,
            vector,
            vector,
            matrix,
            vector,
            matrix,
            vector,
            matrix,
            vector,
            matrix,
            vector,
        ),
        check_vma=False,
    )
```
